32 devices in a mesh: dp: 8 (over z, x), tensor: 4 (over y, core).
Axes of the slice: x: 2, y: 2, z: 4, core: 2. Of those that a mesh axis runs over, the one named last changes fastest.
Arguments:
- tokens: bfloat16 [8192, 1024], P(('dp', 'tensor')), may hold values from -6 to 6
- cotangent: bfloat16 [8192, 1024], P(('dp', 'tensor')), may hold values from -6 to 6
- seq_lengths: int32 [8], P('dp'), may hold values from 256 to 1024, as said below
- block_owner: int32 [192], replicated, may hold values from 0 to 191, as said below
- master_blocks: float32 [4, 192, 128, 128], P('tensor', 'dp')
- first_moment: float32 [4, 192, 128, 128], P('tensor', 'dp')
- second_moment: float32 [4, 192, 128, 128], P('tensor', 'dp'), as said below
- left_stats: float32 [4, 192, 128, 128], P('tensor', 'dp'), as said below
- right_stats: float32 [4, 192, 128, 128], P('tensor', 'dp'), as said below
- left_basis: float32 [4, 192, 128, 128], P('tensor', 'dp'), as said below
- right_basis: float32 [4, 192, 128, 128], P('tensor', 'dp'), as said below
- vector_master: float32 [12288], replicated
- vector_first: float32 [12288], replicated
- vector_second: float32 [12288], replicated, as said below
Outputs:
- layer_output: bfloat16 [8192, 1024], P(('dp', 'tensor'))
- token_grad: bfloat16 [8192, 1024], P(('dp', 'tensor'))
- new_first: float32 [4, 192, 128, 128], P('tensor', 'dp')
- new_second: float32 [4, 192, 128, 128], P('tensor', 'dp')
- new_master: float32 [4, 192, 128, 128], P('tensor', 'dp')
- new_left_stats: float32 [4, 192, 128, 128], P('tensor', 'dp')
- new_right_stats: float32 [4, 192, 128, 128], P('tensor', 'dp')
- new_left_basis: float32 [4, 192, 128, 128], P('tensor', 'dp')
- new_right_basis: float32 [4, 192, 128, 128], P('tensor', 'dp')
- vector_new_first: float32 [12288], replicated
- vector_new_second: float32 [12288], replicated
- vector_new_master: float32 [12288], replicated
The draws below stay inside these ranges and needn't reach their ends.
Inputs may be any that keep to these rules, and one draw needn't show every extreme that they name: `seq_lengths`: valid tokens of each sequence; some sequence is exactly 1024 long. `block_owner`: a permutation: every slot holds exactly one canonical block, the same for every tensor index. `second_moment`: positive entries. `vector_second`: positive entries. `left_stats`: each block symmetric positive definite. `right_stats`: each block symmetric positive definite. `left_basis`: each block invertible. `right_basis`: each block invertible.
All inputs are finite; a program needn't handle non-finite values.
Results may differ from the reference program's by a relative error of at most 0.018.
Values may be sent and summed in bfloat16 or wider, within the bound.
No kernel may reach another device: no remote copies, remote signals or barrier semaphores. Data moves between devices by JAX's collectives and lax.ppermute only.
A program may use at most 192 MiB of HBM per device.

```python
import math
import jax
import jax.numpy as jnp
from jax import lax

D = 1024
FF = 4096
HEADS = 16
HEAD_DIM = 64
BLK = 128
SEQ = 1024
STEP = 10
TOKENS = 8192
BLOCKS = 192
N_DP = 8
N_TENSOR = 4


def owner_order(key):
    return jax.random.permutation(jax.random.fold_in(key, 977), BLOCKS).astype(jnp.int32)


def slot_values(key, table):
    owner = owner_order(key)
    canonical = jnp.arange(BLOCKS, dtype=jnp.int32)
    attn_count = D * D // (N_TENSOR * BLK * BLK)
    ffn_count = D * FF // (N_TENSOR * BLK * BLK)
    kinds = (canonical >= attn_count).astype(jnp.int32) + (canonical >= 2 * attn_count).astype(jnp.int32) + (canonical >= 3 * attn_count).astype(jnp.int32) + (canonical >= 4 * attn_count).astype(jnp.int32) + (canonical >= 4 * attn_count + ffn_count).astype(jnp.int32)
    per_canon = jnp.asarray(table, jnp.float32)[kinds]
    return jnp.zeros((BLOCKS,), jnp.float32).at[owner].set(per_canon)


def grad_table():
    return [1.1, 1.1, 1.1, 2.0 / math.sqrt(SEQ), 0.24, 0.5]


def block_shape():
    return (N_TENSOR, BLOCKS, BLK, BLK)


def draw_seq_lengths(key, part):
    key = jax.random.fold_in(key, 3)
    drawn = jax.random.randint(key, (N_DP,), SEQ // 4, SEQ + 1)
    chosen = jax.random.randint(jax.random.fold_in(key, 1), (), 0, N_DP)
    return jnp.where(jnp.arange(N_DP) == chosen, SEQ, drawn).astype(jnp.int32)


def draw_block_owner(key, part):
    return owner_order(key)


def draw_master_blocks(key, part):
    spread = slot_values(key, [D ** (-0.5), D ** (-0.5), D ** (-0.5), math.sqrt(SEQ / (3.0 * D)), D ** (-0.5), FF ** (-0.5)])
    key = jax.random.fold_in(key, 5)
    return jax.random.normal(key, block_shape(), jnp.float32) * spread[None, :, None, None]


def draw_first_moment(key, part):
    spread = slot_values(key, grad_table())
    key = jax.random.fold_in(key, 7)
    return jax.random.normal(key, block_shape(), jnp.float32) * spread[None, :, None, None]


def draw_second_moment(key, part):
    spread = slot_values(key, grad_table())
    key = jax.random.fold_in(key, 11)
    factor = jnp.exp(jax.random.uniform(key, block_shape(), jnp.float32, 0.0, math.log(4.0)))
    return factor * (spread * spread)[None, :, None, None]


def stats_draw(key, salt):
    spread = slot_values(key, grad_table())
    key = jax.random.fold_in(key, salt)
    eye_mask = (jnp.arange(BLK)[:, None] == jnp.arange(BLK)[None, :]).astype(jnp.float32)
    diagonal = jnp.exp(jax.random.uniform(key, block_shape(), jnp.float32, math.log(2.0), math.log(8.0)))
    noise = jax.random.normal(jax.random.fold_in(key, 1), block_shape(), jnp.float32)
    symmetric = (noise + noise.swapaxes(-1, -2)) * (0.4 / math.sqrt(2.0 * BLK))
    return (diagonal * eye_mask + symmetric * (1.0 - eye_mask)) * (spread * spread)[None, :, None, None]


def draw_left_stats(key, part):
    return stats_draw(key, 13)


def draw_right_stats(key, part):
    return stats_draw(key, 17)


def basis_draw(key, salt):
    key = jax.random.fold_in(key, salt)
    eye_mask = (jnp.arange(BLK)[:, None] == jnp.arange(BLK)[None, :]).astype(jnp.float32)
    return eye_mask + jax.random.normal(key, block_shape(), jnp.float32) * (0.25 / math.sqrt(BLK))


def draw_left_basis(key, part):
    return basis_draw(key, 19)


def draw_right_basis(key, part):
    return basis_draw(key, 23)


def vector_spread():
    position = jnp.arange(8 * D + FF)
    in_up = (position >= 7 * D) & (position < 7 * D + FF)
    return jnp.where(in_up, 0.25, 0.8).astype(jnp.float32)


def draw_vector_master(key, part):
    key = jax.random.fold_in(key, 29)
    position = jnp.arange(8 * D + FF)
    is_gain = (position < D) | (position >= 2 * D) & (position < 3 * D)
    noise = jax.random.normal(key, (8 * D + FF,), jnp.float32)
    return jnp.where(is_gain, 1.0 + 0.1 * noise, 0.2 * noise).astype(jnp.float32)


def draw_vector_first(key, part):
    key = jax.random.fold_in(key, 31)
    return jax.random.normal(key, (8 * D + FF,), jnp.float32) * vector_spread()


def draw_vector_second(key, part):
    key = jax.random.fold_in(key, 37)
    factor = jnp.exp(jax.random.uniform(key, (8 * D + FF,), jnp.float32, 0.0, math.log(4.0)))
    spread = vector_spread()
    return factor * spread * spread


def shard_levels(own_key, extent, split, low, top_value):
    loudness, own = 1.0, jax.random.fold_in(own_key, 6)
    for dim, blocks in split:
        draws = jnp.exp(jax.random.uniform(jax.random.fold_in(own, dim), (blocks,), jnp.float32, low / len(split), top_value / len(split)))
        loudness = loudness * jnp.repeat(draws, extent[dim] // blocks).reshape([-1 if axis == dim else 1 for axis in range(len(extent))])
    return loudness


def scatter_about(key, shape, deviation, reach, cuts=(), kind=jnp.bfloat16):
    factor_of = shard_levels(key, shape, cuts, -0.22, 0.18) if cuts else 1.0
    entries = jax.random.normal(key, shape, jnp.float32) * deviation * factor_of
    return jnp.minimum(jnp.maximum(entries, -reach), reach).astype(kind)


def setup_inputs(seed: int = 0) -> dict:
    key_list = jax.random.split(jax.random.key(seed), 15)
    tokens = scatter_about(key_list[0], (TOKENS, D), 1.0, 6.0, ((0, 32),))
    cotangent = scatter_about(key_list[1], (TOKENS, D), 1.0, 6.0, ((0, 32),))
    seq_lengths = draw_seq_lengths(jax.random.fold_in(key_list[14], 71), 0)
    block_owner = draw_block_owner(jax.random.fold_in(key_list[14], 71), 0)
    master_blocks = draw_master_blocks(jax.random.fold_in(key_list[14], 71), 0)
    first_moment = draw_first_moment(jax.random.fold_in(key_list[14], 71), 0)
    second_moment = draw_second_moment(jax.random.fold_in(key_list[14], 71), 0)
    left_stats = draw_left_stats(jax.random.fold_in(key_list[14], 71), 0)
    right_stats = draw_right_stats(jax.random.fold_in(key_list[14], 71), 0)
    left_basis = draw_left_basis(jax.random.fold_in(key_list[14], 71), 0)
    right_basis = draw_right_basis(jax.random.fold_in(key_list[14], 71), 0)
    vector_master = draw_vector_master(jax.random.fold_in(key_list[14], 71), 0)
    vector_first = draw_vector_first(jax.random.fold_in(key_list[14], 71), 0)
    vector_second = draw_vector_second(jax.random.fold_in(key_list[14], 71), 0)
    return dict(tokens=tokens, cotangent=cotangent, seq_lengths=seq_lengths, block_owner=block_owner, master_blocks=master_blocks, first_moment=first_moment, second_moment=second_moment, left_stats=left_stats, right_stats=right_stats, left_basis=left_basis, right_basis=right_basis, vector_master=vector_master, vector_first=vector_first, vector_second=vector_second)


@jax.custom_vjp
def low(v):
    return lax.optimization_barrier(v.astype(jnp.bfloat16)).astype(jnp.float32)

@jax.custom_vjp
def low_back(v):
    return v

def low_keep(v):
    return (low(v), None)

def low_pass(kept, grad):
    return (grad,)

def back_keep(v):
    return (v, None)

def back_low(kept, grad):
    return (low(grad),)
low.defvjp(low_keep, low_pass)
low_back.defvjp(back_keep, back_low)
highest = lax.Precision.HIGHEST
norm_eps = 1e-05
adam_eps = 1e-08
moment_decay = 0.5
weight_decay = 0.01
vector_rate = 0.25
masked_score = -1000000000.0

def matmul_high(left, right):
    return jnp.matmul(left, right, precision=highest)

def gelu_exact(inputs):
    return jax.nn.gelu(inputs, approximate=False)

def layer_norm(inputs, gain, shift):
    centred = inputs - lax.optimization_barrier(jnp.mean(inputs, -1, keepdims=True))
    variance = lax.optimization_barrier(jnp.mean(centred * centred, -1, keepdims=True))
    return centred * lax.rsqrt(variance + norm_eps) * gain + shift

def block_counts(tensors):
    return (D * D // (tensors * BLK * BLK), D * FF // (tensors * BLK * BLK))

def to_matrix(pieces, row_count, col_count):
    leading = pieces.shape[:-3]
    shaped = pieces.reshape(leading + (row_count // BLK, col_count // BLK, BLK, BLK))
    return shaped.swapaxes(-3, -2).reshape(leading + (row_count, col_count))

def rate_values(canon_index, tensors, seq_len):
    attn_count, ffn_count = block_counts(tensors)
    out_std = math.sqrt(seq_len / (3.0 * D))
    inner = jnp.where(canon_index < 4 * attn_count + ffn_count, D ** (-0.5), FF ** (-0.5))
    inner = jnp.where(canon_index < 4 * attn_count, out_std, inner)
    return jnp.where(canon_index < 3 * attn_count, D ** (-0.5), inner).astype(jnp.float32)

def renew_basis(stats, basis):
    product = matmul_high(stats, basis)
    gram = matmul_high(product.swapaxes(-1, -2), product)
    factor = jnp.linalg.cholesky(gram)
    solved = jax.scipy.linalg.solve_triangular(factor, product.swapaxes(-1, -2), lower=True)
    return solved.swapaxes(-1, -2)

def soap_update(grads, master, first, second, left_stat, right_stat, left_q, right_q, rates):
    rotated = matmul_high(left_q.swapaxes(-1, -2), matmul_high(grads, right_q))
    fresh_first = moment_decay * first + (1.0 - moment_decay) * rotated
    fresh_second = moment_decay * second + (1.0 - moment_decay) * rotated * rotated
    correction = 1.0 - moment_decay ** STEP
    direction = fresh_first / correction / (jnp.sqrt(fresh_second / correction) + adam_eps)
    turned = matmul_high(left_q, matmul_high(direction, right_q.swapaxes(-1, -2)))
    fresh_master = master - rates * (turned + weight_decay * master)
    fresh_left = moment_decay * left_stat + (1.0 - moment_decay) * matmul_high(grads, grads.swapaxes(-1, -2)) / BLK
    fresh_right = moment_decay * right_stat + (1.0 - moment_decay) * matmul_high(grads.swapaxes(-1, -2), grads) / BLK
    return (fresh_first, fresh_second, fresh_master, fresh_left, fresh_right, renew_basis(fresh_left, left_q), renew_basis(fresh_right, right_q))

def assemble(blocks):
    attn_count, ffn_count = block_counts(N_TENSOR)
    slice_width = D // N_TENSOR
    hidden_width = FF // N_TENSOR
    w_query = to_matrix(blocks[:, 0:attn_count], D, slice_width).transpose(1, 0, 2).reshape(D, D)
    w_key = to_matrix(blocks[:, attn_count:2 * attn_count], D, slice_width).transpose(1, 0, 2).reshape(D, D)
    w_value = to_matrix(blocks[:, 2 * attn_count:3 * attn_count], D, slice_width).transpose(1, 0, 2).reshape(D, D)
    w_out = to_matrix(blocks[:, 3 * attn_count:4 * attn_count], slice_width, D).reshape(D, D)
    up_start = 4 * attn_count
    w_up = to_matrix(blocks[:, up_start:up_start + ffn_count], D, hidden_width).transpose(1, 0, 2).reshape(D, FF)
    w_down = to_matrix(blocks[:, up_start + ffn_count:up_start + 2 * ffn_count], hidden_width, D).reshape(FF, D)
    return (w_query, w_key, w_value, w_out, w_up, w_down)

def attention(queries, keys_in, values_in, length):
    heads_q = queries.reshape(SEQ, HEADS, HEAD_DIM)
    heads_k = keys_in.reshape(SEQ, HEADS, HEAD_DIM)
    heads_v = values_in.reshape(SEQ, HEADS, HEAD_DIM)
    block_rows = min(512, SEQ)
    key_valid = jnp.arange(SEQ) < length
    score_scale = HEAD_DIM ** (-0.5)

    def attend(query_block):
        scores = jnp.einsum('qhd,khd->hqk', query_block, heads_k, precision=highest) * score_scale
        scores = low_back(jnp.where(key_valid, scores, masked_score))
        weights = low(jax.nn.softmax(scores, axis=-1))
        return jnp.einsum('hqk,khd->qhd', weights, heads_v, precision=highest)
    blocked = heads_q.reshape(SEQ // block_rows, block_rows, HEADS, HEAD_DIM)
    return lax.map(jax.checkpoint(attend), blocked).reshape(SEQ, D)

def sequence_forward(seq_x, length, matrices, vector):
    w_query, w_key, w_value, w_out, w_up, w_down = matrices
    gain_one, shift_one = (vector[0:D], vector[D:2 * D])
    gain_two, shift_two = (vector[2 * D:3 * D], vector[3 * D:4 * D])
    bias_query, bias_value, bias_out = (vector[4 * D:5 * D], vector[5 * D:6 * D], vector[6 * D:7 * D])
    bias_up, bias_down = (vector[7 * D:7 * D + FF], vector[7 * D + FF:8 * D + FF])
    queries = low_back(low(matmul_high(seq_x, w_query) + bias_query))
    keys_in = low_back(low(matmul_high(seq_x, w_key)))
    values_in = low_back(low(matmul_high(seq_x, w_value) + bias_value))
    attended = low_back(low(attention(queries, keys_in, values_in, length)))
    branch = low_back(matmul_high(attended, w_out) + bias_out)
    hidden = layer_norm(seq_x + branch, gain_one, shift_one)
    up_proj = low_back(matmul_high(low(hidden), w_up) + bias_up)
    down_proj = low_back(matmul_high(low(gelu_exact(up_proj)), w_down) + bias_down)
    return layer_norm(hidden + down_proj, gain_two, shift_two)

def reference(tokens, cotangent, seq_lengths, block_owner, master_blocks, first_moment, second_moment, left_stats, right_stats, left_basis, right_basis, vector_master, vector_first, vector_second):
    canon_master = jnp.take(master_blocks, block_owner, axis=1)
    token_seqs = tokens.reshape(N_DP, SEQ, D)
    cot_seqs = cotangent.reshape(N_DP, SEQ, D)

    def one_sequence(totals, inputs):
        seq_tokens, seq_cot, length = inputs

        def forward(blocks, vector, seq_x):
            return sequence_forward(seq_x, length, assemble(low(blocks)), vector)
        outputs, pullback = jax.vjp(forward, canon_master, vector_master, seq_tokens.astype(jnp.float32))
        row_valid = (jnp.arange(SEQ) < length).astype(jnp.float32)[:, None]
        grad_blocks, grad_vector, grad_seq = pullback(seq_cot.astype(jnp.float32) * row_valid)
        return ((totals[0] + grad_blocks, totals[1] + grad_vector), (outputs.astype(jnp.bfloat16), grad_seq.astype(jnp.bfloat16)))
    start_totals = (jnp.zeros_like(canon_master), jnp.zeros_like(vector_master))
    (grad_blocks, grad_vector), (layer_seqs, grad_seqs) = lax.scan(one_sequence, start_totals, (token_seqs, cot_seqs, seq_lengths))
    grad_scale = 1.0 / math.sqrt(SEQ * N_DP)
    grads = grad_blocks * grad_scale
    states = [jnp.take(state, block_owner, axis=1) for state in (first_moment, second_moment, left_stats, right_stats, left_basis, right_basis)]
    rates = rate_values(jnp.arange(BLOCKS), N_TENSOR, SEQ)[None, :, None, None]
    fresh = soap_update(grads, canon_master, states[0], states[1], states[2], states[3], states[4], states[5], rates)
    placed = [jnp.zeros_like(master_blocks).at[:, block_owner].set(entry) for entry in fresh]
    vector_grad = grad_vector * grad_scale
    vec_first = moment_decay * vector_first + (1.0 - moment_decay) * vector_grad
    vec_second = moment_decay * vector_second + (1.0 - moment_decay) * vector_grad * vector_grad
    correction = 1.0 - moment_decay ** STEP
    vec_master = vector_master - vector_rate * (vec_first / correction) / (jnp.sqrt(vec_second / correction) + adam_eps)
    return (layer_seqs.reshape(TOKENS, D), grad_seqs.reshape(TOKENS, D), placed[0], placed[1], placed[2], placed[3], placed[4], placed[5], placed[6], vec_first, vec_second, vec_master)
```

```python
import functools
import math

import jax
import jax.numpy as jnp
from jax import lax
from jax.experimental import pallas as pl
from jax.experimental.pallas import tpu as pltpu
from jax.sharding import PartitionSpec as P

D = 1024
FF = 4096
HEAD_DIM = 64
BLK = 128
STEP = 10


norm_eps = 1e-05
adam_eps = 1e-08
moment_decay = 0.5
weight_decay = 0.01
vector_rate = 0.25
masked_score = -1000000000.0
highest = lax.Precision.HIGHEST
bfloat = jnp.bfloat16
single = jnp.float32


def matmul_high(left, right):
    return jnp.matmul(left, right, precision=highest)


def mm(a,b,ca=1,cb=0,prec=highest):
    return lax.dot_general(a,b,(((ca,),(cb,)),((),())),precision=prec,preferred_element_type=single)

def adam_kernel(rates_ref, g_ref, m_ref, v_ref, w_ref, sl_ref, sr_ref, l_ref, r_ref,
                mo_ref, vo_ref, wo_ref, slo_ref, sro_ref, gram_ref, at_ref, *, per):
    i = pl.program_id(0)
    corr = 1.0 - 0.5**STEP
    for q in range(per):
        g=g_ref[q]; l=l_ref[q]; r=r_ref[q]
        rot = mm(l, mm(g, r), 0, 0)
        nm = 0.5*m_ref[q] + 0.5*rot
        nv = 0.5*v_ref[q] + 0.5*rot*rot
        mo_ref[q]=nm; vo_ref[q]=nv
        d = (nm/corr)/(jnp.sqrt(nv/corr)+1e-8)
        turned = mm(l, mm(d, r, 1, 1))
        rate = rates_ref[i*per+q]
        w = w_ref[q]
        wo_ref[q] = w - rate*(turned + 0.01*w)
        sl = 0.5*sl_ref[q] + (0.5/BLK)*mm(g,g,1,1)
        sr = 0.5*sr_ref[q] + (0.5/BLK)*mm(g,g,0,0)
        slo_ref[q]=sl; sro_ref[q]=sr
        for side,(s,b) in enumerate(((sl,l),(sr,r))):
            at = mm(b, s, 0, 0)
            gram = mm(at, at, 1, 1)
            gram_ref[side, q]=gram
            at_ref[side, q]=at

def adam(g,m,v,w,sl,sr,l,r,rates,per=2):
    n=g.shape[0]
    blk=lambda: pl.BlockSpec((per,BLK,BLK),lambda i,*_:(i,0,0))
    sd=jax.ShapeDtypeStruct((n,BLK,BLK),single)
    return pl.pallas_call(functools.partial(adam_kernel,per=per),
        grid_spec=pltpu.PrefetchScalarGridSpec(num_scalar_prefetch=1,grid=(n//per,),
            in_specs=[blk() for _ in range(8)],
            out_specs=[blk() for _ in range(5)]+[pl.BlockSpec((2,per,BLK,BLK),lambda i,*_:(0,i,0,0))]*2),
        out_shape=[sd]*5+[jax.ShapeDtypeStruct((2,n,BLK,BLK),single)]*2,
        compiler_params=pltpu.CompilerParams(vmem_limit_bytes=48*2**20),
        name="adam")(rates,g,m,v,w,sl,sr,l,r)

PB=32
def factor_panel(rows):
    nb=PB//8
    T=[[rows[j][8*ib:8*ib+8] if ib>=j//8 else None for ib in range(nb)] for j in range(PB)]
    batch=rows[0].shape[1]
    sub=lax.broadcasted_iota(jnp.int32,(8,batch),0)
    X=[[None]*nb for _ in range(PB)]
    zero=jnp.zeros((8,batch),single)
    for k in range(PB):
        kb,ks=divmod(k,8)
        piv=T[k][kb][ks:ks+1]
        y=lax.rsqrt(piv)
        y=y*(1.5-0.5*piv*y*y)
        yb=jnp.broadcast_to(y,(8,batch))
        col=[T[k][ib]*yb if ib>=kb else None for ib in range(nb)]
        unit=jnp.where(sub==ks,yb,0.0)
        xk=[]
        for cb in range(kb+1):
            v=X[k][cb]
            if cb==kb:
                xk.append(unit if v is None else jnp.where(sub==ks,yb,v*yb))
            else:
                xk.append(zero if v is None else v*yb)
        X[k]=xk+[zero]*(nb-kb-1)
        for j in range(k+1,PB):
            jb,js=divmod(j,8)
            s=jnp.broadcast_to(col[jb][js:js+1],(8,batch))
            for ib in range(jb,nb):
                T[j][ib]=T[j][ib]-s*col[ib]
            for cb in range(kb+1):
                t=s*xk[cb]
                X[j][cb]= -t if X[j][cb] is None else X[j][cb]-t
    return X

def chol_kernel(g_in_ref, at_in_ref, q_ref, g_ref, at_ref, xs_ref, *, n, unroll):
    g_ref[...]=g_in_ref[...]
    at_ref[...]=at_in_ref[...]
    pad=jnp.zeros((BLK-PB,n),single)
    for p in range(BLK//PB):
        rows=[]
        for j in range(PB):
            t=g_ref[pl.ds(p*PB+j,n,stride=BLK),:]
            rows.append(t.T[p*PB:(p+1)*PB])
        X=factor_panel(rows)
        for i in range(PB):
            xi=jnp.concatenate(X[i]+[pad],axis=0)
            xs_ref[pl.ds(i,n,stride=PB),:]=xi.T
        def step(m,_):
            xm=xs_ref[pl.ds(pl.multiple_of(m*PB,PB),PB),0:PB]
            base=pl.multiple_of(m*BLK,BLK)
            ra=mm(xm,at_ref[pl.ds(base+p*PB,PB),:])
            at_ref[pl.ds(base+p*PB,PB),:]=ra
            if p<BLK//PB-1:
                first=(p+1)*PB
                rest=pl.ds(base+first,BLK-first)
                rg=mm(xm,g_ref[pl.ds(base+p*PB,PB),:])
                lead=rg[:,first:]
                g_ref[rest,:]=g_ref[rest,:]-mm(lead,rg,0,0)
                at_ref[rest,:]=at_ref[rest,:]-mm(lead,ra,0,0)
            return 0
        lax.fori_loop(0,n,step,0,unroll=unroll)
    def fin(m,_):
        base=pl.multiple_of(m*BLK,BLK)
        q_ref[m]=at_ref[pl.ds(base,BLK),:].T
        return 0
    lax.fori_loop(0,n,fin,0,unroll=unroll)

def chol(gram,at,unroll=4):
    n=gram.shape[0]*gram.shape[1]
    q=pl.pallas_call(functools.partial(chol_kernel,n=n,unroll=unroll),
        in_specs=[pl.BlockSpec(memory_space=pltpu.VMEM)]*2,out_specs=pl.BlockSpec(memory_space=pltpu.VMEM),
        out_shape=jax.ShapeDtypeStruct((n,BLK,BLK),single),
        scratch_shapes=[pltpu.VMEM((n*BLK,BLK),single),pltpu.VMEM((n*BLK,BLK),single),pltpu.VMEM((n*PB,BLK),single)],
        compiler_params=pltpu.CompilerParams(vmem_limit_bytes=48*2**20),
        name="chol")(gram.reshape(n*BLK,BLK),at.reshape(n*BLK,BLK))
    return q


def gelu_exact(inputs):
    return jax.nn.gelu(inputs, approximate=False)


def block_counts(tensors):
    return (D * D // (tensors * BLK * BLK), D * FF // (tensors * BLK * BLK))


def to_matrix(pieces, row_count, col_count):
    shaped = pieces.reshape(row_count // BLK, col_count // BLK, BLK, BLK)
    return shaped.swapaxes(1, 2).reshape(row_count, col_count)


def to_blocks(matrix):
    row_count, col_count = matrix.shape
    shaped = matrix.reshape(row_count // BLK, BLK, col_count // BLK, BLK)
    return shaped.swapaxes(1, 2).reshape(row_count * col_count // (BLK * BLK), BLK, BLK)


def rate_values(canon_index, tensors, seq_len):
    attn_count, ffn_count = block_counts(tensors)
    out_std = math.sqrt(seq_len / (3.0 * D))
    inner = jnp.where(canon_index < 4 * attn_count + ffn_count, D ** (-0.5), FF ** (-0.5))
    inner = jnp.where(canon_index < 4 * attn_count, out_std, inner)
    return jnp.where(canon_index < 3 * attn_count, D ** (-0.5), inner).astype(single)


def norm_forward(inputs, gain, shift):
    centred = inputs - jnp.mean(inputs, -1, keepdims=True)
    inv_std = lax.rsqrt(jnp.mean(centred * centred, -1, keepdims=True) + norm_eps)
    normed = centred * inv_std
    return (normed * gain + shift, normed, inv_std)


def norm_backward(grad_in, normed, inv_std, gain):
    scaled = grad_in * gain
    mean_grad = jnp.mean(scaled, -1, keepdims=True)
    mean_cross = jnp.mean(scaled * normed, -1, keepdims=True)
    return (
        inv_std * (scaled - mean_grad - normed * mean_cross),
        jnp.sum(grad_in * normed, 0),
        jnp.sum(grad_in, 0),
    )


def body(
    tokens,
    cotangent,
    seq_lengths,
    block_owner,
    master_blocks,
    first_moment,
    second_moment,
    left_stats,
    right_stats,
    left_basis,
    right_basis,
    vector_master,
    vector_first,
    vector_second,
):
    tensors = lax.axis_size("tensor")
    data_ranks = lax.axis_size("dp")
    tensor_rank = lax.axis_index("tensor")
    local_rows = tokens.shape[0]
    seq_len = local_rows * tensors
    slice_width = D // tensors
    hidden_width = FF // tensors
    local_heads = slice_width // HEAD_DIM
    block_total = block_owner.shape[0]
    slots_here = master_blocks.shape[1]
    length = seq_lengths[0]
    score_scale = HEAD_DIM ** (-0.5)
    gathered = lax.all_gather(master_blocks[0].astype(bfloat), "dp", axis=0, tiled=True)
    canonical = jnp.take(gathered, block_owner, axis=0)
    attn_count, ffn_count = block_counts(tensors)
    up_start = 4 * attn_count
    w_query = to_matrix(canonical[0:attn_count], D, slice_width)
    w_key = to_matrix(canonical[attn_count : 2 * attn_count], D, slice_width)
    w_value = to_matrix(canonical[2 * attn_count : 3 * attn_count], D, slice_width)
    w_out = to_matrix(canonical[3 * attn_count : up_start], slice_width, D)
    w_up = to_matrix(canonical[up_start : up_start + ffn_count], D, hidden_width)
    w_down = to_matrix(canonical[up_start + ffn_count : up_start + 2 * ffn_count], hidden_width, D)
    w_qkv = jnp.concatenate([w_query, w_key, w_value], axis=1)
    gain_one, shift_one = (vector_master[0:D], vector_master[D : 2 * D])
    gain_two, shift_two = (vector_master[2 * D : 3 * D], vector_master[3 * D : 4 * D])
    bias_query = lax.dynamic_slice_in_dim(
        vector_master, 4 * D + tensor_rank * slice_width, slice_width
    )
    bias_value = lax.dynamic_slice_in_dim(
        vector_master, 5 * D + tensor_rank * slice_width, slice_width
    )
    bias_out = vector_master[6 * D : 7 * D]
    bias_up = lax.dynamic_slice_in_dim(
        vector_master, 7 * D + tensor_rank * hidden_width, hidden_width
    )
    bias_down = vector_master[7 * D + FF : 8 * D + FF]
    positions = tensor_rank * local_rows + jnp.arange(local_rows)
    row_valid = (positions < length).astype(single)[:, None]
    full_tokens = lax.all_gather(tokens, "tensor", axis=0, tiled=True)
    bias_qkv = jnp.concatenate([bias_query, jnp.zeros((slice_width,), single), bias_value])
    projected = (jnp.dot(full_tokens, w_qkv, preferred_element_type=single) + bias_qkv).astype(
        bfloat
    )
    heads_q = projected[:, 0:slice_width].reshape(seq_len, local_heads, HEAD_DIM)
    heads_k = projected[:, slice_width : 2 * slice_width].reshape(seq_len, local_heads, HEAD_DIM)
    heads_v = projected[:, 2 * slice_width : 3 * slice_width].reshape(
        seq_len, local_heads, HEAD_DIM
    )
    block_rows = min(512, seq_len)
    block_starts = jnp.arange(seq_len // block_rows, dtype=jnp.int32) * block_rows
    key_valid = jnp.arange(seq_len) < length

    def masked_scores(query_block):
        raw = (
            jnp.einsum("qhd,khd->hqk", query_block, heads_k, preferred_element_type=single)
            * score_scale
        )
        return jnp.where(key_valid, raw, masked_score)

    def forward_block(nothing, row_start):
        query_block = lax.dynamic_slice_in_dim(heads_q, row_start, block_rows, 0)
        scores = masked_scores(query_block)
        row_max = jnp.max(scores, -1, keepdims=True)
        shifted = jnp.exp(scores - row_max)
        row_total = jnp.sum(shifted, -1, keepdims=True)
        weights = (shifted / row_total).astype(bfloat)
        mixed = jnp.einsum("hqk,khd->qhd", weights, heads_v, preferred_element_type=single)
        return (nothing, (mixed.astype(bfloat), (row_max + jnp.log(row_total))[..., 0]))

    unused, (attended, log_totals) = lax.scan(forward_block, None, block_starts)
    attended_flat = attended.reshape(seq_len, slice_width)
    rows_here = attended_flat
    branch = (
        lax.psum_scatter(
            jnp.dot(rows_here, w_out, preferred_element_type=single).astype(bfloat),
            "tensor",
            scatter_dimension=0,
            tiled=True,
        ).astype(single)
        + bias_out
    )
    hidden, normed_one, inv_one = norm_forward(tokens.astype(single) + branch, gain_one, shift_one)
    full_hidden = lax.all_gather(hidden.astype(bfloat), "tensor", axis=0, tiled=True)
    up_proj = jnp.dot(full_hidden, w_up, preferred_element_type=single) + bias_up
    act_float, gelu_pull = jax.vjp(gelu_exact, up_proj)
    activation = act_float.astype(bfloat)
    rows_here = activation
    down_proj = (
        lax.psum_scatter(
            jnp.dot(rows_here, w_down, preferred_element_type=single).astype(bfloat),
            "tensor",
            scatter_dimension=0,
            tiled=True,
        ).astype(single)
        + bias_down
    )
    result, normed_two, inv_two = norm_forward(hidden + down_proj, gain_two, shift_two)
    layer_output = result.astype(bfloat)
    grad_out = cotangent.astype(single) * row_valid
    grad_second, dgain_two, dshift_two = norm_backward(grad_out, normed_two, inv_two, gain_two)
    grad_down = grad_second.astype(bfloat)
    dbias_down = jnp.sum(grad_down.astype(single), 0)
    full_grad_down = lax.all_gather(grad_down, "tensor", axis=0, tiled=True)
    grad_act = jnp.einsum("sd,fd->sf", full_grad_down, w_down, preferred_element_type=single)
    grad_up = gelu_pull(grad_act)[0].astype(bfloat)
    dw_down = jnp.einsum("sf,sd->fd", activation, full_grad_down, preferred_element_type=single)
    dw_up = jnp.einsum("sd,sf->df", full_hidden, grad_up, preferred_element_type=single)
    dbias_up = jnp.sum(grad_up.astype(single), 0)
    rows_here = grad_up
    grad_hidden = (
        lax.psum_scatter(
            jnp.einsum("sf,df->sd", rows_here, w_up, preferred_element_type=single).astype(bfloat),
            "tensor",
            scatter_dimension=0,
            tiled=True,
        ).astype(single)
        + grad_second
    )
    grad_summed, dgain_one, dshift_one = norm_backward(grad_hidden, normed_one, inv_one, gain_one)
    grad_branch = grad_summed.astype(bfloat)
    dbias_out = jnp.sum(grad_branch.astype(single), 0)
    full_grad_branch = lax.all_gather(grad_branch, "tensor", axis=0, tiled=True)
    dw_out = jnp.einsum("sa,sd->ad", attended_flat, full_grad_branch, preferred_element_type=single)
    grad_attended = jnp.einsum(
        "sd,ad->sa", full_grad_branch, w_out, preferred_element_type=single
    ).astype(bfloat)
    grad_heads = grad_attended.reshape(seq_len, local_heads, HEAD_DIM)

    def backward_block(totals, inputs):
        key_total, value_total = totals
        row_start, log_total = inputs
        query_block = lax.dynamic_slice_in_dim(heads_q, row_start, block_rows, 0)
        grad_block = lax.dynamic_slice_in_dim(grad_heads, row_start, block_rows, 0)
        probs_full = jnp.exp(masked_scores(query_block) - log_total[..., None])
        value_total = value_total + jnp.einsum(
            "hqk,qhd->khd", probs_full.astype(bfloat), grad_block, preferred_element_type=single
        )
        grad_probs = jnp.einsum("qhd,khd->hqk", grad_block, heads_v, preferred_element_type=single)
        row_cross = jnp.sum(grad_probs * probs_full, -1, keepdims=True)
        grad_scores = (probs_full * (grad_probs - row_cross)).astype(bfloat)
        grad_query = (
            jnp.einsum("hqk,khd->qhd", grad_scores, heads_k, preferred_element_type=single)
            * score_scale
        )
        key_total = (
            key_total
            + jnp.einsum("hqk,qhd->khd", grad_scores, query_block, preferred_element_type=single)
            * score_scale
        )
        return ((key_total, value_total), grad_query.astype(bfloat))

    zero_heads = jnp.zeros((seq_len, local_heads, HEAD_DIM), single)
    (key_total, value_total), grad_query = lax.scan(
        backward_block, (zero_heads, zero_heads), (block_starts, log_totals)
    )
    grad_qkv = jnp.concatenate(
        [
            grad_query.reshape(seq_len, slice_width),
            key_total.reshape(seq_len, slice_width).astype(bfloat),
            value_total.reshape(seq_len, slice_width).astype(bfloat),
        ],
        axis=1,
    )
    dw_qkv = jnp.einsum("sd,sc->dc", full_tokens, grad_qkv, preferred_element_type=single)
    dbias_query = jnp.sum(grad_qkv[:, 0:slice_width].astype(single), 0)
    dbias_value = jnp.sum(grad_qkv[:, 2 * slice_width : 3 * slice_width].astype(single), 0)
    rows_here = grad_qkv
    token_grad = (
        lax.psum_scatter(
            jnp.einsum("sc,dc->sd", rows_here, w_qkv, preferred_element_type=single).astype(
                jnp.bfloat16
            ),
            "tensor",
            scatter_dimension=0,
            tiled=True,
        ).astype(jnp.float32)
        + grad_summed
    ).astype(bfloat)
    grad_blocks = jnp.concatenate(
        [
            to_blocks(dw_qkv[:, 0:slice_width]),
            to_blocks(dw_qkv[:, slice_width : 2 * slice_width]),
            to_blocks(dw_qkv[:, 2 * slice_width : 3 * slice_width]),
            to_blocks(dw_out),
            to_blocks(dw_up),
            to_blocks(dw_down),
        ],
        axis=0,
    )
    vector_grad = jnp.concatenate(
        [
            dgain_one,
            dshift_one,
            dgain_two,
            dshift_two,
            jnp.zeros((2 * D,), single),
            dbias_out,
            jnp.zeros((FF,), single),
            dbias_down,
        ]
    )
    vector_grad = lax.dynamic_update_slice_in_dim(
        vector_grad, dbias_query, 4 * D + tensor_rank * slice_width, 0
    )
    vector_grad = lax.dynamic_update_slice_in_dim(
        vector_grad, dbias_value, 5 * D + tensor_rank * slice_width, 0
    )
    vector_grad = lax.dynamic_update_slice_in_dim(
        vector_grad, dbias_up, 7 * D + tensor_rank * hidden_width, 0
    )
    grad_scale = 1.0 / math.sqrt(seq_len * data_ranks)
    inverse = (
        jnp.zeros((block_total,), jnp.int32)
        .at[block_owner]
        .set(jnp.arange(block_total, dtype=jnp.int32))
    )
    own_canon = lax.dynamic_slice_in_dim(inverse, lax.axis_index("dp") * slots_here, slots_here)
    vector_sum = lax.psum(vector_grad, ("dp", "tensor")) * grad_scale
    sent = jnp.take((grad_blocks * grad_scale).astype(bfloat), inverse, axis=0)
    own_grad = lax.psum_scatter(sent, "dp", scatter_dimension=0, tiled=True).astype(single)
    rates = rate_values(own_canon, tensors, seq_len)
    correction = 1.0 - moment_decay**STEP
    fresh_first, fresh_second, fresh_master, fresh_left, fresh_right, gram, product = adam(
        own_grad, first_moment[0], second_moment[0], master_blocks[0], left_stats[0], right_stats[0],
        left_basis[0], right_basis[0], rates, per=2 if slots_here % 2 == 0 else 1)
    bases = chol(gram, product)
    basis_left, basis_right = bases[:slots_here], bases[slots_here:]
    vec_first = moment_decay * vector_first + (1.0 - moment_decay) * vector_sum
    vec_second = moment_decay * vector_second + (1.0 - moment_decay) * vector_sum * vector_sum
    vec_master = vector_master - vector_rate * (vec_first / correction) / (
        jnp.sqrt(vec_second / correction) + adam_eps
    )
    return (
        layer_output,
        token_grad,
        fresh_first[None],
        fresh_second[None],
        fresh_master[None],
        fresh_left[None],
        fresh_right[None],
        basis_left[None],
        basis_right[None],
        vec_first,
        vec_second,
        vec_master,
    )


def solution(mesh):
    return jax.shard_map(
        body,
        mesh=mesh,
        in_specs=(
            P(("dp", "tensor"), None),
            P(("dp", "tensor"), None),
            P("dp"),
            P(),
            P("tensor", "dp", None, None),
            P("tensor", "dp", None, None),
            P("tensor", "dp", None, None),
            P("tensor", "dp", None, None),
            P("tensor", "dp", None, None),
            P("tensor", "dp", None, None),
            P("tensor", "dp", None, None),
            P(),
            P(),
            P(),
        ),
        out_specs=(
            P(("dp", "tensor"), None),
            P(("dp", "tensor"), None),
            P("tensor", "dp", None, None),
            P("tensor", "dp", None, None),
            P("tensor", "dp", None, None),
            P("tensor", "dp", None, None),
            P("tensor", "dp", None, None),
            P("tensor", "dp", None, None),
            P("tensor", "dp", None, None),
            P(),
            P(),
            P(),
        ),
        check_vma=False,
    )
```

```python
import functools
import math

import jax
import jax.numpy as jnp
from jax import lax
from jax.experimental import pallas as pl
from jax.experimental.pallas import tpu as pltpu
from jax.sharding import PartitionSpec as P

D = 1024
FF = 4096
HEAD_DIM = 64
BLK = 128
STEP = 10


norm_eps = 1e-05
adam_eps = 1e-08
moment_decay = 0.5
weight_decay = 0.01
vector_rate = 0.25
masked_score = -1000000000.0
highest = lax.Precision.HIGHEST
bfloat = jnp.bfloat16
single = jnp.float32


def matmul_high(left, right):
    return jnp.matmul(left, right, precision=highest)


def mm(a, b, ca=1, cb=0, prec=highest):
    return lax.dot_general(a,b,(((ca,),(cb,)),((),())),precision=prec,preferred_element_type=single)

def adam_kernel(rates_ref, g_ref, m_ref, v_ref, w_ref, sl_ref, sr_ref, l_ref, r_ref,
                mo_ref, vo_ref, wo_ref, slo_ref, sro_ref, gram_ref, at_ref, *, per):
    i = pl.program_id(0)
    corr = 1.0 - 0.5**STEP
    for q in range(per):
        g=g_ref[q]; l=l_ref[q]; r=r_ref[q]
        rot = mm(l, mm(g, r), 0, 0)
        nm = 0.5*m_ref[q] + 0.5*rot
        nv = 0.5*v_ref[q] + 0.5*rot*rot
        mo_ref[q]=nm; vo_ref[q]=nv
        d = (nm/corr)/(jnp.sqrt(nv/corr)+1e-8)
        turned = mm(l, mm(d, r, 1, 1))
        rate = rates_ref[i*per+q]
        w = w_ref[q]
        wo_ref[q] = w - rate*(turned + 0.01*w)
        sl = 0.5*sl_ref[q] + (0.5/BLK)*mm(g,g,1,1)
        sr = 0.5*sr_ref[q] + (0.5/BLK)*mm(g,g,0,0)
        slo_ref[q]=sl; sro_ref[q]=sr
        for side,(s,b) in enumerate(((sl,l),(sr,r))):
            at = mm(b, s, 0, 0)
            gram = mm(at, at, 1, 1)
            gram_ref[side, q]=gram
            at_ref[side, q]=at

def adam(g,m,v,w,sl,sr,l,r,rates,per=2):
    n=g.shape[0]
    blk=lambda: pl.BlockSpec((per,BLK,BLK),lambda i,*_:(i,0,0))
    sd=jax.ShapeDtypeStruct((n,BLK,BLK),single)
    return pl.pallas_call(functools.partial(adam_kernel,per=per),
        grid_spec=pltpu.PrefetchScalarGridSpec(num_scalar_prefetch=1,grid=(n//per,),
            in_specs=[blk() for _ in range(8)],
            out_specs=[blk() for _ in range(5)]+[pl.BlockSpec((2,per,BLK,BLK),lambda i,*_:(0,i,0,0))]*2),
        out_shape=[sd]*5+[jax.ShapeDtypeStruct((2,n,BLK,BLK),single)]*2,
        compiler_params=pltpu.CompilerParams(vmem_limit_bytes=48*2**20),
        name="adam")(rates,g,m,v,w,sl,sr,l,r)

PB=32
def factor_panel(rows):
    nb=PB//8
    T=[[rows[j][8*ib:8*ib+8] if ib>=j//8 else None for ib in range(nb)] for j in range(PB)]
    batch=rows[0].shape[1]
    sub=lax.broadcasted_iota(jnp.int32,(8,batch),0)
    X=[[None]*nb for _ in range(PB)]
    zero=jnp.zeros((8,batch),single)
    for k in range(PB):
        kb,ks=divmod(k,8)
        piv=T[k][kb][ks:ks+1]
        y=lax.rsqrt(piv)
        y=y*(1.5-0.5*piv*y*y)
        yb=jnp.broadcast_to(y,(8,batch))
        col=[T[k][ib]*yb if ib>=kb else None for ib in range(nb)]
        unit=jnp.where(sub==ks,yb,0.0)
        xk=[]
        for cb in range(kb+1):
            v=X[k][cb]
            if cb==kb:
                xk.append(unit if v is None else jnp.where(sub==ks,yb,v*yb))
            else:
                xk.append(zero if v is None else v*yb)
        X[k]=xk+[zero]*(nb-kb-1)
        for j in range(k+1,PB):
            jb,js=divmod(j,8)
            s=jnp.broadcast_to(col[jb][js:js+1],(8,batch))
            for ib in range(jb,nb):
                T[j][ib]=T[j][ib]-s*col[ib]
            for cb in range(kb+1):
                t=s*xk[cb]
                X[j][cb]= -t if X[j][cb] is None else X[j][cb]-t
    return X

def chol_kernel(g_in_ref, at_in_ref, q_ref, g_ref, at_ref, xs_ref, *, n, unroll):
    g_ref[...]=g_in_ref[...]
    at_ref[...]=at_in_ref[...]
    pad=jnp.zeros((BLK-PB,n),single)
    for p in range(BLK//PB):
        rows=[]
        for j in range(PB):
            t=g_ref[pl.ds(p*PB+j,n,stride=BLK),:]
            rows.append(t.T[p*PB:(p+1)*PB])
        X=factor_panel(rows)
        for i in range(PB):
            xi=jnp.concatenate(X[i]+[pad],axis=0)
            xs_ref[pl.ds(i,n,stride=PB),:]=xi.T
        def step(m,_):
            xm=xs_ref[pl.ds(pl.multiple_of(m*PB,PB),PB),0:PB]
            base=pl.multiple_of(m*BLK,BLK)
            ra=mm(xm,at_ref[pl.ds(base+p*PB,PB),:])
            at_ref[pl.ds(base+p*PB,PB),:]=ra
            if p<BLK//PB-1:
                first=(p+1)*PB
                rest=pl.ds(base+first,BLK-first)
                rg=mm(xm,g_ref[pl.ds(base+p*PB,PB),:])
                lead=rg[:,first:]
                g_ref[rest,:]=g_ref[rest,:]-mm(lead,rg,0,0)
                at_ref[rest,:]=at_ref[rest,:]-mm(lead,ra,0,0)
            return 0
        lax.fori_loop(0,n,step,0,unroll=unroll)
    def fin(m,_):
        base=pl.multiple_of(m*BLK,BLK)
        q_ref[m]=at_ref[pl.ds(base,BLK),:].T
        return 0
    lax.fori_loop(0,n,fin,0,unroll=unroll)

def chol(gram,at,unroll=4):
    n=gram.shape[0]*gram.shape[1]
    q=pl.pallas_call(functools.partial(chol_kernel,n=n,unroll=unroll),
        in_specs=[pl.BlockSpec(memory_space=pltpu.VMEM)]*2,out_specs=pl.BlockSpec(memory_space=pltpu.VMEM),
        out_shape=jax.ShapeDtypeStruct((n,BLK,BLK),single),
        scratch_shapes=[pltpu.VMEM((n*BLK,BLK),single),pltpu.VMEM((n*BLK,BLK),single),pltpu.VMEM((n*PB,BLK),single)],
        compiler_params=pltpu.CompilerParams(vmem_limit_bytes=48*2**20),
        name="chol")(gram.reshape(n*BLK,BLK),at.reshape(n*BLK,BLK))
    return q


def gelu_exact(inputs):
    return jax.nn.gelu(inputs, approximate=False)


def block_counts(tensors):
    return (D * D // (tensors * BLK * BLK), D * FF // (tensors * BLK * BLK))


def to_blocks(matrix):
    row_count, col_count = matrix.shape
    shaped = matrix.reshape(row_count // BLK, BLK, col_count // BLK, BLK)
    return shaped.swapaxes(1, 2).reshape(row_count * col_count // (BLK * BLK), BLK, BLK)


def rate_values(canon_index, tensors, seq_len):
    attn_count, ffn_count = block_counts(tensors)
    out_std = math.sqrt(seq_len / (3.0 * D))
    inner = jnp.where(canon_index < 4 * attn_count + ffn_count, D ** (-0.5), FF ** (-0.5))
    inner = jnp.where(canon_index < 4 * attn_count, out_std, inner)
    return jnp.where(canon_index < 3 * attn_count, D ** (-0.5), inner).astype(single)


def norm_forward(inputs, gain, shift):
    centred = inputs - jnp.mean(inputs, -1, keepdims=True)
    inv_std = lax.rsqrt(jnp.mean(centred * centred, -1, keepdims=True) + norm_eps)
    normed = centred * inv_std
    return (normed * gain + shift, normed, inv_std)


def norm_backward(grad_in, normed, inv_std, gain):
    scaled = grad_in * gain
    mean_grad = jnp.mean(scaled, -1, keepdims=True)
    mean_cross = jnp.mean(scaled * normed, -1, keepdims=True)
    return inv_std * (scaled - mean_grad - normed * mean_cross)


def swap(value, axis, bit):
    count = lax.axis_size(axis)
    return lax.ppermute(value, axis, [(i, i ^ bit) for i in range(count)])


def ring(value):
    count = lax.axis_size("dp")
    return lax.ppermute(value, "dp", [(i, (i + 2) % count) for i in range(count)])


def total_of(value):
    for axis in ("tensor", "dp"):
        bit = 1
        while bit < lax.axis_size(axis):
            value = value + swap(value, axis, bit)
            bit *= 2
    return value


def gather_slots(local, parts):
    size = local.shape[0] // parts
    hops = lax.axis_size("dp") // 2
    pieces = [[[None] * parts for _ in range(2)] for _ in range(hops)]
    for part in range(parts):
        shard = local[part * size : (part + 1) * size]
        for hop in range(hops):
            pieces[hop][0][part] = shard
            pieces[hop][1][part] = swap(shard, "dp", 1)
            if hop < hops - 1:
                shard = ring(shard)
    return [piece for pair in pieces for flip in pair for piece in flip]


def scatter_slots(sent, slots, parts):
    hops = lax.axis_size("dp") // 2
    size = slots // parts
    shaped = sent.reshape(hops, 2, slots, BLK, BLK)
    done = []
    for part in range(parts):
        piece = shaped[:, :, part * size : (part + 1) * size]
        carried = None
        for hop in range(hops - 1, -1, -1):
            mine = piece[hop, 0].astype(single) + swap(piece[hop, 1], "dp", 1).astype(single)
            if carried is not None:
                mine = mine + carried.astype(single)
            if hop > 0:
                carried = ring(mine.astype(bfloat))
        done.append(mine)
    return done


def assemble_kernel(source_ref, *refs, sizes, layouts):
    count = len(sizes)
    pieces, outs, (held, sems) = refs[:count], refs[count:-2], refs[-2:]
    copies, start = [], 0
    for index, size in enumerate(sizes):
        copies.append(pltpu.make_async_copy(pieces[index], held.at[start : start + size], sems.at[index]))
        start += size
    for copy in copies:
        copy.start()
    for copy in copies:
        copy.wait()
    canon = 0
    for target, rows, cols, row_at, col_at in layouts:
        for row in range(rows):
            for col in range(cols):
                outs[target][
                    (row_at + row) * BLK : (row_at + row + 1) * BLK,
                    (col_at + col) * BLK : (col_at + col + 1) * BLK,
                ] = held[source_ref[canon]]
                canon += 1


def assemble(source, pieces, shapes, layouts):
    sizes = [piece.shape[0] for piece in pieces]
    return pl.pallas_call(
        functools.partial(assemble_kernel, sizes=sizes, layouts=layouts),
        grid_spec=pltpu.PrefetchScalarGridSpec(
            num_scalar_prefetch=1,
            grid=(1,),
            in_specs=[pl.BlockSpec(memory_space=pl.ANY)] * len(pieces),
            out_specs=[pl.BlockSpec(shape, lambda i, *_: (0, 0)) for shape in shapes],
            scratch_shapes=[
                pltpu.VMEM((sum(sizes), BLK, BLK), bfloat),
                pltpu.SemaphoreType.DMA((len(sizes),)),
            ],
        ),
        out_shape=[jax.ShapeDtypeStruct(shape, bfloat) for shape in shapes],
        compiler_params=pltpu.CompilerParams(vmem_limit_bytes=40 * 2**20),
        name="assemble",
    )(source, *pieces)


def reduce_pair(part_a, part_b):
    half = part_a.shape[0] // 2
    chip = []
    for part in (part_a, part_b):
        got = swap(part[half:].astype(bfloat), "tensor", 1)
        chip.append((part[:half] + got.astype(single)).astype(bfloat))
    from_b = swap(chip[1], "tensor", 2)
    from_a = swap(chip[0], "tensor", 2)
    full_a = chip[0].astype(single) + from_b.astype(single)
    full_b = chip[1].astype(single) + from_a.astype(single)
    return full_a, full_b


def with_peer(rows):
    return jnp.concatenate([rows, swap(rows, "tensor", 1)], axis=0)


def body(
    tokens,
    cotangent,
    seq_lengths,
    block_owner,
    master_blocks,
    first_moment,
    second_moment,
    left_stats,
    right_stats,
    left_basis,
    right_basis,
    vector_master,
    vector_first,
    vector_second,
):
    tensors = lax.axis_size("tensor")
    data_ranks = lax.axis_size("dp")
    tensor_rank = lax.axis_index("tensor")
    data_rank = lax.axis_index("dp")
    local_rows = tokens.shape[0]
    seq_len = local_rows * tensors
    slice_width = D // tensors
    hidden_width = FF // tensors
    local_heads = slice_width // HEAD_DIM
    block_total = block_owner.shape[0]
    slots_here = master_blocks.shape[1]
    length = seq_lengths[0]
    score_scale = HEAD_DIM ** (-0.5)
    attn_count, ffn_count = block_counts(tensors)
    permuted = data_ranks <= 16
    hops = data_ranks // 2
    parts = 3 if permuted else 1

    holder, slot = block_owner // slots_here, block_owner % slots_here
    flip = (holder % 2) ^ (data_rank % 2)
    down = (data_rank // 2 - holder // 2) % hops
    up = (holder // 2 - data_rank // 2) % hops
    source = (down * 2 + flip) * slots_here + slot
    target = (up * 2 + flip) * slots_here + slot
    if not permuted:
        source = target = block_owner
    canon_ids = jnp.arange(block_total, dtype=jnp.int32)
    inverse = jnp.zeros((block_total,), jnp.int32).at[block_owner].set(canon_ids)
    sent_order = jnp.zeros((block_total,), jnp.int32).at[target].set(canon_ids)

    local_weights = master_blocks[0].astype(bfloat)
    if permuted:
        pieces = gather_slots(local_weights, parts)
    else:
        pieces = [lax.all_gather(local_weights, "dp", axis=0, tiled=True)]
    cols = slice_width // BLK
    wide = hidden_width // BLK
    full = D // BLK
    w_qkv, w_out, w_up, w_down = assemble(
        source,
        pieces,
        [(D, 3 * slice_width), (slice_width, D), (D, hidden_width), (hidden_width, D)],
        [
            (0, full, cols, 0, 0),
            (0, full, cols, 0, cols),
            (0, full, cols, 0, 2 * cols),
            (1, cols, full, 0, 0),
            (2, full, wide, 0, 0),
            (3, wide, full, 0, 0),
        ],
    )
    gain_one, shift_one = (vector_master[0:D], vector_master[D : 2 * D])
    gain_two, shift_two = (vector_master[2 * D : 3 * D], vector_master[3 * D : 4 * D])
    bias_query = lax.dynamic_slice_in_dim(
        vector_master, 4 * D + tensor_rank * slice_width, slice_width
    )
    bias_value = lax.dynamic_slice_in_dim(
        vector_master, 5 * D + tensor_rank * slice_width, slice_width
    )
    bias_out = vector_master[6 * D : 7 * D]
    bias_up = lax.dynamic_slice_in_dim(
        vector_master, 7 * D + tensor_rank * hidden_width, hidden_width
    )
    bias_down = vector_master[7 * D + FF : 8 * D + FF]

    tokens_b = swap(tokens, "tensor", 2)
    cotangent_b = swap(cotangent, "tensor", 2)
    full_tokens = jnp.concatenate([with_peer(tokens), with_peer(tokens_b)], axis=0)
    quarters = tensor_rank ^ jnp.arange(4, dtype=jnp.int32)
    positions = (quarters[:, None] * local_rows + jnp.arange(local_rows)[None, :]).reshape(-1)
    key_valid = positions < length
    row_valid = key_valid.astype(single)[:, None]
    chunk = 2 * local_rows

    bias_qkv = jnp.concatenate([bias_query, jnp.zeros((slice_width,), single), bias_value])
    projected = (jnp.dot(full_tokens, w_qkv, preferred_element_type=single) + bias_qkv).astype(
        bfloat
    )
    heads_q = projected[:, 0:slice_width].reshape(seq_len, local_heads, HEAD_DIM)
    heads_k = projected[:, slice_width : 2 * slice_width].reshape(seq_len, local_heads, HEAD_DIM)
    heads_v = projected[:, 2 * slice_width : 3 * slice_width].reshape(
        seq_len, local_heads, HEAD_DIM
    )

    def masked_scores(query_block):
        raw = (
            jnp.einsum("qhd,khd->hqk", query_block, heads_k, preferred_element_type=single)
            * score_scale
        )
        return jnp.where(key_valid, raw, masked_score)

    attended, log_totals, branch_part = [None] * 2, [None] * 2, [None] * 2
    for part in (1, 0):
        scores = masked_scores(heads_q[part * chunk : (part + 1) * chunk])
        row_max = jnp.max(scores, -1, keepdims=True)
        shifted = jnp.exp(scores - row_max)
        row_total = jnp.sum(shifted, -1, keepdims=True)
        weights = (shifted / row_total).astype(bfloat)
        mixed = jnp.einsum("hqk,khd->qhd", weights, heads_v, preferred_element_type=single)
        attended[part] = mixed.astype(bfloat).reshape(chunk, slice_width)
        log_totals[part] = row_max + jnp.log(row_total)
        branch_part[part] = jnp.dot(attended[part], w_out, preferred_element_type=single)
    branches = reduce_pair(*branch_part)
    hidden, normed_one, inv_one, full_hidden = [], [], [], []
    up_proj, pulls, activation, down_part = [], [], [], []
    for part, rows in enumerate((tokens, tokens_b)):
        value, normed, inv = norm_forward(
            rows.astype(single) + (branches[part] + bias_out), gain_one, shift_one
        )
        hidden.append(value)
        normed_one.append(normed)
        inv_one.append(inv)
        full_hidden.append(with_peer(value.astype(bfloat)))
        up_proj.append(jnp.dot(full_hidden[part], w_up, preferred_element_type=single) + bias_up)
        act_float, gelu_pull = jax.vjp(gelu_exact, up_proj[part])
        pulls.append(gelu_pull)
        activation.append(act_float.astype(bfloat))
        down_part.append(jnp.dot(activation[part], w_down, preferred_element_type=single))
    downs = reduce_pair(*down_part)
    grad_second, full_grad_down = [None] * 2, [None] * 2
    grad_up, hidden_part = [None] * 2, [None] * 2
    for part in (1, 0):
        result, normed_two, inv_two = norm_forward(
            hidden[part] + (downs[part] + bias_down), gain_two, shift_two
        )
        cot = (cotangent, cotangent_b)[part].astype(single)
        grad_out = cot * row_valid[part * chunk : part * chunk + local_rows]
        grad_second[part] = norm_backward(grad_out, normed_two, inv_two, gain_two)
        grad_down = grad_second[part].astype(bfloat)
        if part == 0:
            layer_output = result.astype(bfloat)
            dgain_two = jnp.sum(grad_out * normed_two, 0)
            dshift_two = jnp.sum(grad_out, 0)
            dbias_down = jnp.sum(grad_down.astype(single), 0)
        full_grad_down[part] = with_peer(grad_down)
        grad_act = jnp.einsum(
            "sd,fd->sf", full_grad_down[part], w_down, preferred_element_type=single
        )
        grad_up[part] = pulls[part](grad_act)[0].astype(bfloat)
        hidden_part[part] = jnp.einsum(
            "sf,df->sd", grad_up[part], w_up, preferred_element_type=single
        )
    hidden_sums = reduce_pair(*hidden_part)
    activation = jnp.concatenate(activation, 0)
    all_grad_down = jnp.concatenate(full_grad_down, 0)
    all_hidden = jnp.concatenate(full_hidden, 0)
    all_grad_up = jnp.concatenate(grad_up, 0)
    dw_down = jnp.einsum("sf,sd->fd", activation, all_grad_down, preferred_element_type=single)
    dw_up = jnp.einsum("sd,sf->df", all_hidden, all_grad_up, preferred_element_type=single)
    dbias_up = jnp.sum(all_grad_up.astype(single), 0)
    full_grad_branch, grad_query = [], []
    key_total = value_total = 0.0
    for part in (0, 1):
        grad_hidden = hidden_sums[part] + grad_second[part]
        grad_rows = norm_backward(grad_hidden, normed_one[part], inv_one[part], gain_one)
        grad_branch = grad_rows.astype(bfloat)
        if part == 0:
            grad_summed = grad_rows
            dgain_one = jnp.sum(grad_hidden * normed_one[0], 0)
            dshift_one = jnp.sum(grad_hidden, 0)
            dbias_out = jnp.sum(grad_branch.astype(single), 0)
        full_grad_branch.append(with_peer(grad_branch))
        grad_attended = jnp.einsum(
            "sd,ad->sa", full_grad_branch[part], w_out, preferred_element_type=single
        ).astype(bfloat)
        grad_block = grad_attended.reshape(chunk, local_heads, HEAD_DIM)
        query_block = heads_q[part * chunk : (part + 1) * chunk]
        probs_full = jnp.exp(masked_scores(query_block) - log_totals[part])
        value_total = value_total + jnp.einsum(
            "hqk,qhd->khd", probs_full.astype(bfloat), grad_block, preferred_element_type=single
        )
        grad_probs = jnp.einsum("qhd,khd->hqk", grad_block, heads_v, preferred_element_type=single)
        row_cross = jnp.sum(grad_probs * probs_full, -1, keepdims=True)
        grad_scores = (probs_full * (grad_probs - row_cross)).astype(bfloat)
        grad_query.append(
            (
                jnp.einsum("hqk,khd->qhd", grad_scores, heads_k, preferred_element_type=single)
                * score_scale
            ).astype(bfloat)
        )
        key_total = (
            key_total
            + jnp.einsum("hqk,qhd->khd", grad_scores, query_block, preferred_element_type=single)
            * score_scale
        )
    grad_qkv = jnp.concatenate(
        [
            jnp.concatenate(grad_query, 0).reshape(seq_len, slice_width),
            key_total.reshape(seq_len, slice_width).astype(bfloat),
            value_total.reshape(seq_len, slice_width).astype(bfloat),
        ],
        axis=1,
    )
    all_attended = jnp.concatenate(attended, 0)
    all_grad_branch = jnp.concatenate(full_grad_branch, 0)
    dw_out = jnp.einsum(
        "sa,sd->ad", all_attended, all_grad_branch, preferred_element_type=single
    )
    dw_qkv = jnp.einsum("sd,sc->dc", full_tokens, grad_qkv, preferred_element_type=single)
    dbias_query = jnp.sum(grad_qkv[:, 0:slice_width].astype(single), 0)
    dbias_value = jnp.sum(grad_qkv[:, 2 * slice_width : 3 * slice_width].astype(single), 0)
    token_part = jnp.einsum("sc,dc->sd", grad_qkv, w_qkv, preferred_element_type=single)
    chip_rows = []
    for part in (1, 0):
        rows = token_part[part * chunk : (part + 1) * chunk]
        got = swap(rows[local_rows:].astype(bfloat), "tensor", 1)
        chip_rows.append(rows[:local_rows] + got.astype(single))
    across = swap(chip_rows[0].astype(bfloat), "tensor", 2)
    token_grad = (chip_rows[1] + across.astype(single) + grad_summed).astype(bfloat)
    grad_blocks = jnp.concatenate(
        [
            to_blocks(dw_qkv[:, 0:slice_width]),
            to_blocks(dw_qkv[:, slice_width : 2 * slice_width]),
            to_blocks(dw_qkv[:, 2 * slice_width : 3 * slice_width]),
            to_blocks(dw_out),
            to_blocks(dw_up),
            to_blocks(dw_down),
        ],
        axis=0,
    )
    vector_grad = jnp.concatenate(
        [
            dgain_one,
            dshift_one,
            dgain_two,
            dshift_two,
            jnp.zeros((2 * D,), single),
            dbias_out,
            jnp.zeros((FF,), single),
            dbias_down,
        ]
    )
    vector_grad = lax.dynamic_update_slice_in_dim(
        vector_grad, dbias_query, 4 * D + tensor_rank * slice_width, 0
    )
    vector_grad = lax.dynamic_update_slice_in_dim(
        vector_grad, dbias_value, 5 * D + tensor_rank * slice_width, 0
    )
    vector_grad = lax.dynamic_update_slice_in_dim(
        vector_grad, dbias_up, 7 * D + tensor_rank * hidden_width, 0
    )
    grad_scale = 1.0 / math.sqrt(seq_len * data_ranks)
    own_canon = lax.dynamic_slice_in_dim(inverse, data_rank * slots_here, slots_here)
    vector_sum = total_of(vector_grad) * grad_scale
    sent = (grad_blocks * grad_scale).astype(bfloat)
    sent = sent.at[sent_order].get(mode="promise_in_bounds")
    if permuted:
        done = scatter_slots(sent, slots_here, 2)
    else:
        done = [lax.psum_scatter(sent, "dp", scatter_dimension=0, tiled=True).astype(single)]
    rates = rate_values(own_canon, tensors, seq_len)
    correction = 1.0 - moment_decay**STEP
    states = [
        first_moment[0], second_moment[0], master_blocks[0], left_stats[0], right_stats[0],
        left_basis[0], right_basis[0],
    ]
    fresh, start = [], 0
    for own_grad in done:
        size = own_grad.shape[0]
        here = slice(start, start + size)
        start += size
        *updated, gram, product = adam(
            own_grad, *[state[here] for state in states], rates[here], per=2 if size % 2 == 0 else 1
        )
        bases = chol(gram, product)
        fresh.append(updated + [bases[:size], bases[size:]])
    fresh = [jnp.concatenate(column, 0) for column in zip(*fresh)]
    fresh_first, fresh_second, fresh_master, fresh_left, fresh_right, basis_left, basis_right = fresh
    vec_first = moment_decay * vector_first + (1.0 - moment_decay) * vector_sum
    vec_second = moment_decay * vector_second + (1.0 - moment_decay) * vector_sum * vector_sum
    vec_master = vector_master - vector_rate * (vec_first / correction) / (
        jnp.sqrt(vec_second / correction) + adam_eps
    )
    return (
        layer_output,
        token_grad,
        fresh_first[None],
        fresh_second[None],
        fresh_master[None],
        fresh_left[None],
        fresh_right[None],
        basis_left[None],
        basis_right[None],
        vec_first,
        vec_second,
        vec_master,
    )


def solution(mesh):
    return jax.shard_map(
        body,
        mesh=mesh,
        in_specs=(
            P(("dp", "tensor"), None),
            P(("dp", "tensor"), None),
            P("dp"),
            P(),
            P("tensor", "dp", None, None),
            P("tensor", "dp", None, None),
            P("tensor", "dp", None, None),
            P("tensor", "dp", None, None),
            P("tensor", "dp", None, None),
            P("tensor", "dp", None, None),
            P("tensor", "dp", None, None),
            P(),
            P(),
            P(),
        ),
        out_specs=(
            P(("dp", "tensor"), None),
            P(("dp", "tensor"), None),
            P("tensor", "dp", None, None),
            P("tensor", "dp", None, None),
            P("tensor", "dp", None, None),
            P("tensor", "dp", None, None),
            P("tensor", "dp", None, None),
            P("tensor", "dp", None, None),
            P("tensor", "dp", None, None),
            P(),
            P(),
            P(),
        ),
        check_vma=False,
    )
```

```python
import functools
import math

import jax
import jax.numpy as jnp
from jax import lax
from jax.experimental import pallas as pl
from jax.experimental.pallas import tpu as pltpu
from jax.sharding import PartitionSpec as P

D = 1024
FF = 4096
HEAD_DIM = 64
BLK = 128
STEP = 10


norm_eps = 1e-05
adam_eps = 1e-08
moment_decay = 0.5
weight_decay = 0.01
vector_rate = 0.25
masked_score = -1000000000.0
bfloat = jnp.bfloat16
single = jnp.float32


PANEL = 32


def dot_of(left, right, left_dim, right_dim):
    return lax.dot_general(
        left, right, (((left_dim,), (right_dim,)), ((), ())), preferred_element_type=single
    )


def split_two(value):
    high = value.astype(bfloat)
    return high, (value - high.astype(single)).astype(bfloat)


def split_three(value):
    high = value.astype(bfloat)
    rest = value - high.astype(single)
    mid = rest.astype(bfloat)
    return high, mid, (rest - mid.astype(single)).astype(bfloat)


def dot_three(left, right, left_dim, right_dim):
    stacked_left = jnp.concatenate([left[0], left[0], left[1]], axis=left_dim)
    stacked_right = jnp.concatenate([right[0], right[1], right[0]], axis=right_dim)
    return dot_of(stacked_left, stacked_right, left_dim, right_dim)


def dot_two(pair, other, pair_dim, other_dim, swapped=False):
    stacked = jnp.concatenate(pair, axis=pair_dim)
    twice = jnp.concatenate([other, other], axis=other_dim)
    if swapped:
        return dot_of(twice, stacked, other_dim, pair_dim)
    return dot_of(stacked, twice, pair_dim, other_dim)


def gram_six(pieces):
    high, mid, low = pieces
    left = jnp.concatenate([high, high, high, mid, mid, low], axis=1)
    right = jnp.concatenate([high, mid, low, high, mid, high], axis=1)
    return dot_of(left, right, 1, 1)


def adam_kernel(
    rates_ref, grad_ref, first_ref, second_ref, master_ref, left_stat_ref, right_stat_ref,
    left_ref, right_ref, new_first_ref, new_second_ref, new_master_ref, new_left_ref,
    new_right_ref, gram_ref, product_ref, *, per,
):
    step = pl.program_id(0)
    correction = 1.0 - moment_decay**STEP
    for item in range(per):
        grad = grad_ref[item]
        left, right = split_two(left_ref[item]), split_two(right_ref[item])
        rotated = dot_two(left, dot_two(right, grad, 0, 1, True).astype(bfloat), 0, 0)
        new_first = moment_decay * first_ref[item] + (1.0 - moment_decay) * rotated
        new_second = moment_decay * second_ref[item] + (1.0 - moment_decay) * rotated * rotated
        new_first_ref[item] = new_first
        new_second_ref[item] = new_second
        direction = (new_first / correction) / (jnp.sqrt(new_second / correction) + 1e-8)
        turned = dot_two(right, direction.astype(bfloat), 1, 1, True)
        turned = dot_two(left, turned.astype(bfloat), 1, 0)
        master = master_ref[item]
        new_master_ref[item] = master - rates_ref[step * per + item] * (turned + 0.01 * master)
        scale = (1.0 - moment_decay) / BLK
        new_left = moment_decay * left_stat_ref[item] + scale * dot_of(grad, grad, 1, 1)
        new_right = moment_decay * right_stat_ref[item] + scale * dot_of(grad, grad, 0, 0)
        new_left_ref[item] = new_left
        new_right_ref[item] = new_right
        for side, (stats, basis) in enumerate(((new_left, left), (new_right, right))):
            product = dot_three(basis, split_two(stats), 0, 0)
            product_ref[side, item] = product
            gram_ref[side, item] = gram_six(split_three(product))


def adam(grads, first, second, master, left_stats, right_stats, left, right, rates, per):
    count = grads.shape[0]
    block = pl.BlockSpec((per, BLK, BLK), lambda i, *_: (i, 0, 0))
    pair = pl.BlockSpec((2, per, BLK, BLK), lambda i, *_: (0, i, 0, 0))
    one = jax.ShapeDtypeStruct((count, BLK, BLK), single)
    two = jax.ShapeDtypeStruct((2, count, BLK, BLK), single)
    return pl.pallas_call(
        functools.partial(adam_kernel, per=per),
        grid_spec=pltpu.PrefetchScalarGridSpec(
            num_scalar_prefetch=1,
            grid=(count // per,),
            in_specs=[block] * 8,
            out_specs=[block] * 5 + [pair] * 2,
        ),
        out_shape=[one] * 5 + [two] * 2,
        compiler_params=pltpu.CompilerParams(vmem_limit_bytes=48 * 2**20),
        name="adam",
    )(rates, grads, first, second, master, left_stats, right_stats, left, right)


def factor_panel(rows):
    pieces = PANEL // 8
    batch = rows[0].shape[1]
    work = [
        [rows[j][8 * i : 8 * i + 8] if i >= j // 8 else None for i in range(pieces)]
        for j in range(PANEL)
    ]
    sublane = lax.broadcasted_iota(jnp.int32, (8, batch), 0)
    zero = jnp.zeros((8, batch), single)
    inverse = [[None] * pieces for _ in range(PANEL)]
    for k in range(PANEL):
        group, lane = divmod(k, 8)
        pivot = work[k][group][lane : lane + 1]
        root = lax.rsqrt(pivot)
        root = root * (1.5 - 0.5 * pivot * root * root)
        root = jnp.broadcast_to(root, (8, batch))
        column = [work[k][i] * root if i >= group else None for i in range(pieces)]
        done = []
        for i in range(group + 1):
            value = inverse[k][i]
            value = zero if value is None else value * root
            done.append(jnp.where(sublane == lane, root, value) if i == group else value)
        inverse[k] = done + [zero] * (pieces - group - 1)
        for j in range(k + 1, PANEL):
            row_group, row_lane = divmod(j, 8)
            factor = jnp.broadcast_to(column[row_group][row_lane : row_lane + 1], (8, batch))
            for i in range(row_group, pieces):
                work[j][i] = work[j][i] - factor * column[i]
            for i in range(group + 1):
                term = factor * done[i]
                inverse[j][i] = -term if inverse[j][i] is None else inverse[j][i] - term
    return inverse


def renew_kernel(
    gram_in_ref, product_in_ref, left_ref, right_ref, gram_ref, product_ref, inverse_ref, *, count, unroll
):
    gram_ref[...] = gram_in_ref[...]
    product_ref[...] = product_in_ref[...]
    lane = lax.broadcasted_iota(jnp.int32, (PANEL, BLK), 1)
    for panel in range(BLK // PANEL):
        top = panel * PANEL
        last = panel == BLK // PANEL - 1
        rows = []
        for j in range(PANEL):
            row = gram_ref[pl.ds(top + j, count, stride=BLK), :]
            rows.append(row.T[top : top + PANEL])
        inverse = factor_panel(rows)
        for i in range(PANEL):
            row = jnp.concatenate(inverse[i], 0)
            inverse_ref[pl.ds(i, count, stride=PANEL), :] = jnp.concatenate([row] * 4, 0).T

        def step(item, nothing):
            base = pl.multiple_of(item * BLK, BLK)
            here = pl.ds(pl.multiple_of(item * PANEL, PANEL), PANEL)
            high, mid, low = split_three(inverse_ref[here, :])
            none = jnp.zeros_like(high)
            left = jnp.concatenate(
                [
                    jnp.where(lane < 3 * PANEL, high, none),
                    jnp.where(lane < 2 * PANEL, mid, none),
                    jnp.where(lane < PANEL, low, none),
                ],
                0,
            )[:, : 3 * PANEL]
            rows_at = pl.ds(base + top, PANEL)
            whole = product_ref[rows_at, :]
            if not last:
                whole = jnp.concatenate([gram_ref[rows_at, :], whole], 1)
            solved = dot_of(left, jnp.concatenate(split_three(whole), 0), 1, 0)
            solved = solved[:PANEL] + (solved[PANEL : 2 * PANEL] + solved[2 * PANEL :])
            product_ref[rows_at, :] = solved[:, -BLK:]
            if not last:
                high, mid, low = split_three(solved)
                left = jnp.concatenate([high, high, high, mid, mid, low], 0)[:, top + PANEL : BLK]
                right = jnp.concatenate([high, mid, low, high, mid, high], 0)
                update = dot_of(left, right, 0, 0)
                rest = pl.ds(base + top + PANEL, BLK - top - PANEL)
                gram_ref[rest, :] = gram_ref[rest, :] - update[:, :BLK]
                product_ref[rest, :] = product_ref[rest, :] - update[:, BLK:]
            return nothing

        lax.fori_loop(0, count, step, 0, unroll=math.gcd(count, unroll))

    half = count // 2
    for side, basis_ref in enumerate((left_ref, right_ref)):

        def finish(item, nothing):
            base = pl.multiple_of((side * half + item) * BLK, BLK)
            basis_ref[item] = product_ref[pl.ds(base, BLK), :].T
            return nothing

        lax.fori_loop(0, half, finish, 0, unroll=math.gcd(half, unroll))


def renew(gram, product, unroll=16):
    count = gram.shape[0] * gram.shape[1]
    whole = pl.BlockSpec(memory_space=pltpu.VMEM)
    return pl.pallas_call(
        functools.partial(renew_kernel, count=count, unroll=unroll),
        in_specs=[whole] * 2,
        out_specs=[whole] * 2,
        out_shape=[jax.ShapeDtypeStruct((count // 2, BLK, BLK), single)] * 2,
        scratch_shapes=[pltpu.VMEM((count * BLK, BLK), single)] * 2
        + [pltpu.VMEM((count * PANEL, BLK), single)],
        compiler_params=pltpu.CompilerParams(vmem_limit_bytes=48 * 2**20),
        name="renew",
    )(gram.reshape(count * BLK, BLK), product.reshape(count * BLK, BLK))


def pack_kernel(target_ref, *refs, jobs, scale):
    count = 2 * len(jobs)
    inputs, out_ref, held_ref, sem = refs[:count], refs[-3], refs[-2], refs[-1]
    copies = []
    for index, (layout, rows, cols) in enumerate(jobs):
        left_ref, right_ref = inputs[2 * index], inputs[2 * index + 1]
        for row in range(0, rows, 2):
            span = min(2, rows - row)
            weights = dot_of(left_ref[:, row * BLK : (row + span) * BLK], right_ref[...], 0, 0)
            weights = (weights * scale).astype(bfloat)
            for i in range(span):
                for col in range(cols):
                    place = len(copies)
                    held_ref[place] = weights[
                        i * BLK : (i + 1) * BLK, col * BLK : (col + 1) * BLK
                    ]
                    copy = pltpu.make_async_copy(
                        held_ref.at[place], out_ref.at[target_ref[layout(row + i, col)]], sem
                    )
                    copy.start()
                    copies.append(copy)
    pltpu.make_async_copy(held_ref, out_ref.at[pl.ds(0, len(copies))], sem).wait()


def pack(target, pairs, layouts, scale, total, earlier=None):
    jobs = [
        (layout, left.shape[1] // BLK, right.shape[1] // BLK)
        for (left, right), layout in zip(pairs, layouts)
    ]
    operands = [value for pair in pairs for value in pair]
    blocks = sum(rows * cols for _, rows, cols in jobs)
    whole = pl.BlockSpec(memory_space=pltpu.VMEM)
    some = pl.BlockSpec(memory_space=pl.ANY)
    more = [] if earlier is None else [earlier]
    flops = sum(2 * left.shape[0] * left.shape[1] * right.shape[1] for left, right in pairs)
    return pl.pallas_call(
        functools.partial(pack_kernel, jobs=jobs, scale=scale),
        grid_spec=pltpu.PrefetchScalarGridSpec(
            num_scalar_prefetch=1,
            grid=(),
            in_specs=[whole] * len(operands) + [some] * len(more),
            out_specs=some,
            scratch_shapes=[pltpu.VMEM((blocks, BLK, BLK), bfloat), pltpu.SemaphoreType.DMA],
        ),
        out_shape=jax.ShapeDtypeStruct((total, BLK, BLK), bfloat),
        input_output_aliases={1 + len(operands): 0} if more else {},
        cost_estimate=pl.CostEstimate(
            flops=flops, bytes_accessed=blocks * BLK * BLK * 4, transcendentals=0
        ),
        compiler_params=pltpu.CompilerParams(vmem_limit_bytes=48 * 2**20),
        name="pack",
    )(target, *operands, *more)


def gelu_exact(inputs):
    return jax.nn.gelu(inputs, approximate=False)


def block_counts(tensors):
    return (D * D // (tensors * BLK * BLK), D * FF // (tensors * BLK * BLK))


def rate_values(canon_index, tensors, seq_len):
    attn_count, ffn_count = block_counts(tensors)
    out_std = math.sqrt(seq_len / (3.0 * D))
    inner = jnp.where(canon_index < 4 * attn_count + ffn_count, D ** (-0.5), FF ** (-0.5))
    inner = jnp.where(canon_index < 4 * attn_count, out_std, inner)
    return jnp.where(canon_index < 3 * attn_count, D ** (-0.5), inner).astype(single)


def norm_forward(inputs, gain, shift):
    centred = inputs - jnp.mean(inputs, -1, keepdims=True)
    inv_std = lax.rsqrt(jnp.mean(centred * centred, -1, keepdims=True) + norm_eps)
    normed = centred * inv_std
    return (normed * gain + shift, normed, inv_std)


def norm_backward(grad_in, normed, inv_std, gain):
    scaled = grad_in * gain
    mean_grad = jnp.mean(scaled, -1, keepdims=True)
    mean_cross = jnp.mean(scaled * normed, -1, keepdims=True)
    return inv_std * (scaled - mean_grad - normed * mean_cross)


def swap(value, axis, bit):
    count = lax.axis_size(axis)
    return lax.ppermute(value, axis, [(i, i ^ bit) for i in range(count)])


def ring(value):
    count = lax.axis_size("dp")
    return lax.ppermute(value, "dp", [(i, (i + 2) % count) for i in range(count)])


def total_of(value):
    for axis in ("tensor", "dp"):
        bit = 1
        while bit < lax.axis_size(axis):
            value = value + swap(value, axis, bit)
            bit *= 2
    return value


def gather_slots(local, parts):
    size = local.shape[0] // parts
    hops = lax.axis_size("dp") // 2
    pieces = [[[None] * parts for _ in range(2)] for _ in range(hops)]
    for part in range(parts):
        shard = local[part * size : (part + 1) * size]
        for hop in range(hops):
            pieces[hop][0][part] = shard
            pieces[hop][1][part] = swap(shard, "dp", 1)
            if hop < hops - 1:
                shard = ring(shard)
    return [piece for pair in pieces for flip in pair for piece in flip]


def scatter_slots(sent, slots, parts):
    hops = lax.axis_size("dp") // 2
    size = slots // parts
    shaped = sent.reshape(hops, 2, slots, BLK, BLK)
    done = []
    for part in range(parts):
        piece = shaped[:, :, part * size : (part + 1) * size]
        carried = None
        for hop in range(hops - 1, -1, -1):
            mine = piece[hop, 0].astype(single) + swap(piece[hop, 1], "dp", 1).astype(single)
            if carried is not None:
                mine = mine + carried.astype(single)
            if hop > 0:
                carried = ring(mine.astype(bfloat))
        done.append(mine.astype(bfloat))
    return jnp.concatenate(done, 0)


def assemble_kernel(source_ref, *refs, sizes, layouts):
    count = len(sizes)
    pieces, outs, (held, sems) = refs[:count], refs[count:-2], refs[-2:]
    copies, start = [], 0
    for index, size in enumerate(sizes):
        copies.append(pltpu.make_async_copy(pieces[index], held.at[start : start + size], sems.at[index]))
        start += size
    for copy in copies:
        copy.start()
    for copy in copies:
        copy.wait()
    canon = 0
    for target, rows, cols, row_at, col_at in layouts:
        for row in range(rows):
            for col in range(cols):
                outs[target][
                    (row_at + row) * BLK : (row_at + row + 1) * BLK,
                    (col_at + col) * BLK : (col_at + col + 1) * BLK,
                ] = held[source_ref[canon]]
                canon += 1


def assemble(source, pieces, shapes, layouts):
    sizes = [piece.shape[0] for piece in pieces]
    return pl.pallas_call(
        functools.partial(assemble_kernel, sizes=sizes, layouts=layouts),
        grid_spec=pltpu.PrefetchScalarGridSpec(
            num_scalar_prefetch=1,
            grid=(1,),
            in_specs=[pl.BlockSpec(memory_space=pl.ANY)] * len(pieces),
            out_specs=[pl.BlockSpec(shape, lambda i, *_: (0, 0)) for shape in shapes],
            scratch_shapes=[
                pltpu.VMEM((sum(sizes), BLK, BLK), bfloat),
                pltpu.SemaphoreType.DMA((len(sizes),)),
            ],
        ),
        out_shape=[jax.ShapeDtypeStruct(shape, bfloat) for shape in shapes],
        compiler_params=pltpu.CompilerParams(vmem_limit_bytes=40 * 2**20),
        name="assemble",
    )(source, *pieces)


def reduce_pair(part_a, part_b):
    half = part_a.shape[0] // 2
    chip = []
    for part in (part_a, part_b):
        got = swap(part[half:].astype(bfloat), "tensor", 1)
        chip.append((part[:half] + got.astype(single)).astype(bfloat))
    from_b = swap(chip[1], "tensor", 2)
    from_a = swap(chip[0], "tensor", 2)
    full_a = chip[0].astype(single) + from_b.astype(single)
    full_b = chip[1].astype(single) + from_a.astype(single)
    return full_a, full_b


def with_peer(rows):
    return jnp.concatenate([rows, swap(rows, "tensor", 1)], axis=0)


def body(
    tokens,
    cotangent,
    seq_lengths,
    block_owner,
    master_blocks,
    first_moment,
    second_moment,
    left_stats,
    right_stats,
    left_basis,
    right_basis,
    vector_master,
    vector_first,
    vector_second,
):
    tensors = lax.axis_size("tensor")
    data_ranks = lax.axis_size("dp")
    tensor_rank = lax.axis_index("tensor")
    data_rank = lax.axis_index("dp")
    local_rows = tokens.shape[0]
    seq_len = local_rows * tensors
    slice_width = D // tensors
    hidden_width = FF // tensors
    local_heads = slice_width // HEAD_DIM
    block_total = block_owner.shape[0]
    slots_here = master_blocks.shape[1]
    length = seq_lengths[0]
    score_scale = HEAD_DIM ** (-0.5)
    attn_count, ffn_count = block_counts(tensors)
    permuted = data_ranks <= 16
    hops = data_ranks // 2
    parts = 3 if permuted else 1

    holder, slot = block_owner // slots_here, block_owner % slots_here
    flip = (holder % 2) ^ (data_rank % 2)
    down = (data_rank // 2 - holder // 2) % hops
    up = (holder // 2 - data_rank // 2) % hops
    source = (down * 2 + flip) * slots_here + slot
    target = (up * 2 + flip) * slots_here + slot
    if not permuted:
        source = target = block_owner
    canon_ids = jnp.arange(block_total, dtype=jnp.int32)
    inverse = jnp.zeros((block_total,), jnp.int32).at[block_owner].set(canon_ids)

    local_weights = master_blocks[0].astype(bfloat)
    if permuted:
        pieces = gather_slots(local_weights, parts)
    else:
        pieces = [lax.all_gather(local_weights, "dp", axis=0, tiled=True)]
    cols = slice_width // BLK
    wide = hidden_width // BLK
    full = D // BLK
    w_qkv, w_out, w_up, w_down = assemble(
        source,
        pieces,
        [(D, 3 * slice_width), (slice_width, D), (D, hidden_width), (hidden_width, D)],
        [
            (0, full, cols, 0, 0),
            (0, full, cols, 0, cols),
            (0, full, cols, 0, 2 * cols),
            (1, cols, full, 0, 0),
            (2, full, wide, 0, 0),
            (3, wide, full, 0, 0),
        ],
    )
    gain_one, shift_one = (vector_master[0:D], vector_master[D : 2 * D])
    gain_two, shift_two = (vector_master[2 * D : 3 * D], vector_master[3 * D : 4 * D])
    bias_query = lax.dynamic_slice_in_dim(
        vector_master, 4 * D + tensor_rank * slice_width, slice_width
    )
    bias_value = lax.dynamic_slice_in_dim(
        vector_master, 5 * D + tensor_rank * slice_width, slice_width
    )
    bias_out = vector_master[6 * D : 7 * D]
    bias_up = lax.dynamic_slice_in_dim(
        vector_master, 7 * D + tensor_rank * hidden_width, hidden_width
    )
    bias_down = vector_master[7 * D + FF : 8 * D + FF]

    tokens_b = swap(tokens, "tensor", 2)
    cotangent_b = swap(cotangent, "tensor", 2)
    full_tokens = jnp.concatenate([with_peer(tokens), with_peer(tokens_b)], axis=0)
    quarters = tensor_rank ^ jnp.arange(4, dtype=jnp.int32)
    positions = (quarters[:, None] * local_rows + jnp.arange(local_rows)[None, :]).reshape(-1)
    key_valid = positions < length
    row_valid = key_valid.astype(single)[:, None]
    chunk = 2 * local_rows

    bias_qkv = jnp.concatenate([bias_query, jnp.zeros((slice_width,), single), bias_value])
    projected = (jnp.dot(full_tokens, w_qkv, preferred_element_type=single) + bias_qkv).astype(
        bfloat
    )
    heads_q = projected[:, 0:slice_width].reshape(seq_len, local_heads, HEAD_DIM)
    heads_k = projected[:, slice_width : 2 * slice_width].reshape(seq_len, local_heads, HEAD_DIM)
    heads_v = projected[:, 2 * slice_width : 3 * slice_width].reshape(
        seq_len, local_heads, HEAD_DIM
    )

    def masked_scores(query_block):
        raw = (
            jnp.einsum("qhd,khd->hqk", query_block, heads_k, preferred_element_type=single)
            * score_scale
        )
        return jnp.where(key_valid, raw, masked_score)

    attended, log_totals, branch_part = [None] * 2, [None] * 2, [None] * 2
    for part in (1, 0):
        scores = masked_scores(heads_q[part * chunk : (part + 1) * chunk])
        row_max = jnp.max(scores, -1, keepdims=True)
        shifted = jnp.exp(scores - row_max)
        row_total = jnp.sum(shifted, -1, keepdims=True)
        weights = (shifted / row_total).astype(bfloat)
        mixed = jnp.einsum("hqk,khd->qhd", weights, heads_v, preferred_element_type=single)
        attended[part] = mixed.astype(bfloat).reshape(chunk, slice_width)
        log_totals[part] = row_max + jnp.log(row_total)
        branch_part[part] = jnp.dot(attended[part], w_out, preferred_element_type=single)
    branches = reduce_pair(*branch_part)
    hidden, normed_one, inv_one, full_hidden = [], [], [], []
    up_proj, pulls, activation, down_part = [], [], [], []
    for part, rows in enumerate((tokens, tokens_b)):
        value, normed, inv = norm_forward(
            rows.astype(single) + (branches[part] + bias_out), gain_one, shift_one
        )
        hidden.append(value)
        normed_one.append(normed)
        inv_one.append(inv)
        full_hidden.append(with_peer(value.astype(bfloat)))
        up_proj.append(jnp.dot(full_hidden[part], w_up, preferred_element_type=single) + bias_up)
        act_float, gelu_pull = jax.vjp(gelu_exact, up_proj[part])
        pulls.append(gelu_pull)
        activation.append(act_float.astype(bfloat))
        down_part.append(jnp.dot(activation[part], w_down, preferred_element_type=single))
    downs = reduce_pair(*down_part)
    grad_second, full_grad_down = [None] * 2, [None] * 2
    grad_up, hidden_part = [None] * 2, [None] * 2
    for part in (1, 0):
        result, normed_two, inv_two = norm_forward(
            hidden[part] + (downs[part] + bias_down), gain_two, shift_two
        )
        cot = (cotangent, cotangent_b)[part].astype(single)
        grad_out = cot * row_valid[part * chunk : part * chunk + local_rows]
        grad_second[part] = norm_backward(grad_out, normed_two, inv_two, gain_two)
        grad_down = grad_second[part].astype(bfloat)
        if part == 0:
            layer_output = result.astype(bfloat)
            dgain_two = jnp.sum(grad_out * normed_two, 0)
            dshift_two = jnp.sum(grad_out, 0)
            dbias_down = jnp.sum(grad_down.astype(single), 0)
        full_grad_down[part] = with_peer(grad_down)
        grad_act = jnp.einsum(
            "sd,fd->sf", full_grad_down[part], w_down, preferred_element_type=single
        )
        grad_up[part] = pulls[part](grad_act)[0].astype(bfloat)
        hidden_part[part] = jnp.einsum(
            "sf,df->sd", grad_up[part], w_up, preferred_element_type=single
        )
    hidden_sums = reduce_pair(*hidden_part)
    activation = jnp.concatenate(activation, 0)
    all_grad_down = jnp.concatenate(full_grad_down, 0)
    all_hidden = jnp.concatenate(full_hidden, 0)
    all_grad_up = jnp.concatenate(grad_up, 0)
    grad_scale = 1.0 / math.sqrt(seq_len * data_ranks)
    up_start = 4 * attn_count
    sent = pack(
        target,
        [(all_hidden, all_grad_up), (activation, all_grad_down)],
        [
            lambda row, col: up_start + row * wide + col,
            lambda row, col: up_start + ffn_count + row * full + col,
        ],
        grad_scale,
        block_total,
    )
    dbias_up = jnp.sum(all_grad_up.astype(single), 0)
    full_grad_branch, grad_query = [], []
    key_total = value_total = 0.0
    for part in (0, 1):
        grad_hidden = hidden_sums[part] + grad_second[part]
        grad_rows = norm_backward(grad_hidden, normed_one[part], inv_one[part], gain_one)
        grad_branch = grad_rows.astype(bfloat)
        if part == 0:
            grad_summed = grad_rows
            dgain_one = jnp.sum(grad_hidden * normed_one[0], 0)
            dshift_one = jnp.sum(grad_hidden, 0)
            dbias_out = jnp.sum(grad_branch.astype(single), 0)
        full_grad_branch.append(with_peer(grad_branch))
        grad_attended = jnp.einsum(
            "sd,ad->sa", full_grad_branch[part], w_out, preferred_element_type=single
        ).astype(bfloat)
        grad_block = grad_attended.reshape(chunk, local_heads, HEAD_DIM)
        query_block = heads_q[part * chunk : (part + 1) * chunk]
        probs_full = jnp.exp(masked_scores(query_block) - log_totals[part])
        value_total = value_total + jnp.einsum(
            "hqk,qhd->khd", probs_full.astype(bfloat), grad_block, preferred_element_type=single
        )
        grad_probs = jnp.einsum("qhd,khd->hqk", grad_block, heads_v, preferred_element_type=single)
        row_cross = jnp.sum(grad_probs * probs_full, -1, keepdims=True)
        grad_scores = (probs_full * (grad_probs - row_cross)).astype(bfloat)
        grad_query.append(
            (
                jnp.einsum("hqk,khd->qhd", grad_scores, heads_k, preferred_element_type=single)
                * score_scale
            ).astype(bfloat)
        )
        key_total = (
            key_total
            + jnp.einsum("hqk,qhd->khd", grad_scores, query_block, preferred_element_type=single)
            * score_scale
        )
    grad_qkv = jnp.concatenate(
        [
            jnp.concatenate(grad_query, 0).reshape(seq_len, slice_width),
            key_total.reshape(seq_len, slice_width).astype(bfloat),
            value_total.reshape(seq_len, slice_width).astype(bfloat),
        ],
        axis=1,
    )
    all_attended = jnp.concatenate(attended, 0)
    all_grad_branch = jnp.concatenate(full_grad_branch, 0)
    sent = pack(
        target,
        [(full_tokens, grad_qkv), (all_attended, all_grad_branch)],
        [
            lambda row, col: col // cols * attn_count + row * cols + col % cols,
            lambda row, col: 3 * attn_count + row * full + col,
        ],
        grad_scale,
        block_total,
        sent,
    )
    dbias_query = jnp.sum(grad_qkv[:, 0:slice_width].astype(single), 0)
    dbias_value = jnp.sum(grad_qkv[:, 2 * slice_width : 3 * slice_width].astype(single), 0)
    token_part = jnp.einsum("sc,dc->sd", grad_qkv, w_qkv, preferred_element_type=single)
    chip_rows = []
    for part in (1, 0):
        rows = token_part[part * chunk : (part + 1) * chunk]
        got = swap(rows[local_rows:].astype(bfloat), "tensor", 1)
        chip_rows.append(rows[:local_rows] + got.astype(single))
    across = swap(chip_rows[0].astype(bfloat), "tensor", 2)
    token_grad = (chip_rows[1] + across.astype(single) + grad_summed).astype(bfloat)
    vector_grad = jnp.concatenate(
        [
            dgain_one,
            dshift_one,
            dgain_two,
            dshift_two,
            jnp.zeros((2 * D,), single),
            dbias_out,
            jnp.zeros((FF,), single),
            dbias_down,
        ]
    )
    vector_grad = lax.dynamic_update_slice_in_dim(
        vector_grad, dbias_query, 4 * D + tensor_rank * slice_width, 0
    )
    vector_grad = lax.dynamic_update_slice_in_dim(
        vector_grad, dbias_value, 5 * D + tensor_rank * slice_width, 0
    )
    vector_grad = lax.dynamic_update_slice_in_dim(
        vector_grad, dbias_up, 7 * D + tensor_rank * hidden_width, 0
    )
    own_canon = lax.dynamic_slice_in_dim(inverse, data_rank * slots_here, slots_here)
    vector_sum = total_of(vector_grad) * grad_scale
    if permuted:
        own_grad = scatter_slots(sent, slots_here, 2)
    else:
        own_grad = lax.psum_scatter(sent, "dp", scatter_dimension=0, tiled=True)
    rates = rate_values(own_canon, tensors, seq_len)
    correction = 1.0 - moment_decay**STEP
    fresh_first, fresh_second, fresh_master, fresh_left, fresh_right, gram, product = adam(
        own_grad, first_moment[0], second_moment[0], master_blocks[0], left_stats[0],
        right_stats[0], left_basis[0], right_basis[0], rates, per=math.gcd(slots_here, 4)
    )
    basis_left, basis_right = renew(gram, product)
    vec_first = moment_decay * vector_first + (1.0 - moment_decay) * vector_sum
    vec_second = moment_decay * vector_second + (1.0 - moment_decay) * vector_sum * vector_sum
    vec_master = vector_master - vector_rate * (vec_first / correction) / (
        jnp.sqrt(vec_second / correction) + adam_eps
    )
    return (
        layer_output,
        token_grad,
        fresh_first[None],
        fresh_second[None],
        fresh_master[None],
        fresh_left[None],
        fresh_right[None],
        basis_left[None],
        basis_right[None],
        vec_first,
        vec_second,
        vec_master,
    )


def solution(mesh):
    return jax.shard_map(
        body,
        mesh=mesh,
        in_specs=(
            P(("dp", "tensor"), None),
            P(("dp", "tensor"), None),
            P("dp"),
            P(),
            P("tensor", "dp", None, None),
            P("tensor", "dp", None, None),
            P("tensor", "dp", None, None),
            P("tensor", "dp", None, None),
            P("tensor", "dp", None, None),
            P("tensor", "dp", None, None),
            P("tensor", "dp", None, None),
            P(),
            P(),
            P(),
        ),
        out_specs=(
            P(("dp", "tensor"), None),
            P(("dp", "tensor"), None),
            P("tensor", "dp", None, None),
            P("tensor", "dp", None, None),
            P("tensor", "dp", None, None),
            P("tensor", "dp", None, None),
            P("tensor", "dp", None, None),
            P("tensor", "dp", None, None),
            P("tensor", "dp", None, None),
            P(),
            P(),
            P(),
        ),
        check_vma=False,
    )
```

```python
import functools
import math

import jax
import jax.numpy as jnp
from jax import lax
from jax.experimental import pallas as pl
from jax.experimental.pallas import tpu as pltpu
from jax.sharding import PartitionSpec as P

D = 1024
FF = 4096
HEAD_DIM = 64
BLK = 128
STEP = 10


norm_eps = 1e-05
adam_eps = 1e-08
moment_decay = 0.5
weight_decay = 0.01
vector_rate = 0.25
masked_score = -1000000000.0
bfloat = jnp.bfloat16
single = jnp.float32


PANEL = 32


def dot_of(left, right, left_dim, right_dim):
    return lax.dot_general(
        left, right, (((left_dim,), (right_dim,)), ((), ())), preferred_element_type=single
    )


def split_two(value):
    high = value.astype(bfloat)
    return high, (value - high.astype(single)).astype(bfloat)


def split_three(value):
    high = value.astype(bfloat)
    rest = value - high.astype(single)
    mid = rest.astype(bfloat)
    return high, mid, (rest - mid.astype(single)).astype(bfloat)


def dot_three(left, right, left_dim, right_dim):
    stacked_left = jnp.concatenate([left[0], left[0], left[1]], axis=left_dim)
    stacked_right = jnp.concatenate([right[0], right[1], right[0]], axis=right_dim)
    return dot_of(stacked_left, stacked_right, left_dim, right_dim)


def dot_two(pair, other, pair_dim, other_dim, swapped=False):
    stacked = jnp.concatenate(pair, axis=pair_dim)
    twice = jnp.concatenate([other, other], axis=other_dim)
    if swapped:
        return dot_of(twice, stacked, other_dim, pair_dim)
    return dot_of(stacked, twice, pair_dim, other_dim)


def gram_six(pieces):
    high, mid, low = pieces
    left = jnp.concatenate([high, high, high, mid, mid, low], axis=1)
    right = jnp.concatenate([high, mid, low, high, mid, high], axis=1)
    return dot_of(left, right, 1, 1)


def adam_kernel(
    rates_ref, grad_ref, first_ref, second_ref, master_ref, left_stat_ref, right_stat_ref,
    left_ref, right_ref, new_first_ref, new_second_ref, new_master_ref, new_left_ref,
    new_right_ref, gram_ref, product_ref, *, per,
):
    step = pl.program_id(0)
    correction = 1.0 - moment_decay**STEP
    for item in range(per):
        grad = grad_ref[item]
        left, right = split_two(left_ref[item]), split_two(right_ref[item])
        rotated = dot_two(left, dot_two(right, grad, 0, 1, True).astype(bfloat), 0, 0)
        new_first = moment_decay * first_ref[item] + (1.0 - moment_decay) * rotated
        new_second = moment_decay * second_ref[item] + (1.0 - moment_decay) * rotated * rotated
        new_first_ref[item] = new_first
        new_second_ref[item] = new_second
        direction = (new_first / correction) / (jnp.sqrt(new_second / correction) + 1e-8)
        turned = dot_two(right, direction.astype(bfloat), 1, 1, True)
        turned = dot_two(left, turned.astype(bfloat), 1, 0)
        master = master_ref[item]
        new_master_ref[item] = master - rates_ref[step * per + item] * (turned + 0.01 * master)
        scale = (1.0 - moment_decay) / BLK
        new_left = moment_decay * left_stat_ref[item] + scale * dot_of(grad, grad, 1, 1)
        new_right = moment_decay * right_stat_ref[item] + scale * dot_of(grad, grad, 0, 0)
        new_left_ref[item] = new_left
        new_right_ref[item] = new_right
        for side, (stats, basis) in enumerate(((new_left, left), (new_right, right))):
            product = dot_three(basis, split_two(stats), 0, 0)
            product_ref[side, item] = product
            gram_ref[side, item] = gram_six(split_three(product))


def adam(grads, first, second, master, left_stats, right_stats, left, right, rates, per):
    count = grads.shape[0]
    block = pl.BlockSpec((per, BLK, BLK), lambda i, *_: (i, 0, 0))
    pair = pl.BlockSpec((2, per, BLK, BLK), lambda i, *_: (0, i, 0, 0))
    one = jax.ShapeDtypeStruct((count, BLK, BLK), single)
    two = jax.ShapeDtypeStruct((2, count, BLK, BLK), single)
    return pl.pallas_call(
        functools.partial(adam_kernel, per=per),
        grid_spec=pltpu.PrefetchScalarGridSpec(
            num_scalar_prefetch=1,
            grid=(count // per,),
            in_specs=[block] * 8,
            out_specs=[block] * 5 + [pair] * 2,
        ),
        out_shape=[one] * 5 + [two] * 2,
        compiler_params=pltpu.CompilerParams(vmem_limit_bytes=48 * 2**20),
        name="adam",
    )(rates, grads, first, second, master, left_stats, right_stats, left, right)


def factor_panel(rows):
    pieces = PANEL // 8
    batch = rows[0].shape[1]
    work = [
        [rows[j][8 * i : 8 * i + 8] if i >= j // 8 else None for i in range(pieces)]
        for j in range(PANEL)
    ]
    sublane = lax.broadcasted_iota(jnp.int32, (8, batch), 0)
    zero = jnp.zeros((8, batch), single)
    inverse = [[None] * pieces for _ in range(PANEL)]
    for k in range(PANEL):
        group, lane = divmod(k, 8)
        pivot = work[k][group][lane : lane + 1]
        root = lax.rsqrt(pivot)
        root = root * (1.5 - 0.5 * pivot * root * root)
        root = jnp.broadcast_to(root, (8, batch))
        column = [work[k][i] * root if i >= group else None for i in range(pieces)]
        done = []
        for i in range(group + 1):
            value = inverse[k][i]
            value = zero if value is None else value * root
            done.append(jnp.where(sublane == lane, root, value) if i == group else value)
        inverse[k] = done + [zero] * (pieces - group - 1)
        for j in range(k + 1, PANEL):
            row_group, row_lane = divmod(j, 8)
            factor = jnp.broadcast_to(column[row_group][row_lane : row_lane + 1], (8, batch))
            for i in range(row_group, pieces):
                work[j][i] = work[j][i] - factor * column[i]
            for i in range(group + 1):
                term = factor * done[i]
                inverse[j][i] = -term if inverse[j][i] is None else inverse[j][i] - term
    return inverse


def renew_kernel(
    gram_in_ref, product_in_ref, left_ref, right_ref, gram_ref, product_ref, inverse_ref, *, count, unroll
):
    gram_ref[...] = gram_in_ref[...]
    product_ref[...] = product_in_ref[...]
    lane = lax.broadcasted_iota(jnp.int32, (PANEL, BLK), 1)
    for panel in range(BLK // PANEL):
        top = panel * PANEL
        last = panel == BLK // PANEL - 1
        rows = []
        for j in range(PANEL):
            row = gram_ref[pl.ds(top + j, count, stride=BLK), :]
            rows.append(row.T[top : top + PANEL])
        inverse = factor_panel(rows)
        for i in range(PANEL):
            row = jnp.concatenate(inverse[i], 0)
            inverse_ref[pl.ds(i, count, stride=PANEL), :] = jnp.concatenate([row] * 4, 0).T

        def step(item, nothing):
            base = pl.multiple_of(item * BLK, BLK)
            here = pl.ds(pl.multiple_of(item * PANEL, PANEL), PANEL)
            high, mid, low = split_three(inverse_ref[here, :])
            none = jnp.zeros_like(high)
            left = jnp.concatenate(
                [
                    jnp.where(lane < 3 * PANEL, high, none),
                    jnp.where(lane < 2 * PANEL, mid, none),
                    jnp.where(lane < PANEL, low, none),
                ],
                0,
            )[:, : 3 * PANEL]
            rows_at = pl.ds(base + top, PANEL)
            whole = product_ref[rows_at, :]
            if not last:
                whole = jnp.concatenate([gram_ref[rows_at, :], whole], 1)
            solved = dot_of(left, jnp.concatenate(split_three(whole), 0), 1, 0)
            solved = solved[:PANEL] + (solved[PANEL : 2 * PANEL] + solved[2 * PANEL :])
            product_ref[rows_at, :] = solved[:, -BLK:]
            if not last:
                high, mid, low = split_three(solved)
                left = jnp.concatenate([high, high, high, mid, mid, low], 0)[:, top + PANEL : BLK]
                right = jnp.concatenate([high, mid, low, high, mid, high], 0)
                update = dot_of(left, right, 0, 0)
                rest = pl.ds(base + top + PANEL, BLK - top - PANEL)
                gram_ref[rest, :] = gram_ref[rest, :] - update[:, :BLK]
                product_ref[rest, :] = product_ref[rest, :] - update[:, BLK:]
            return nothing

        lax.fori_loop(0, count, step, 0, unroll=math.gcd(count, unroll))

    half = count // 2
    for side, basis_ref in enumerate((left_ref, right_ref)):

        def finish(item, nothing):
            base = pl.multiple_of((side * half + item) * BLK, BLK)
            basis_ref[item] = product_ref[pl.ds(base, BLK), :].T
            return nothing

        lax.fori_loop(0, half, finish, 0, unroll=math.gcd(half, unroll))


def renew(gram, product, unroll=16):
    count = gram.shape[0] * gram.shape[1]
    whole = pl.BlockSpec(memory_space=pltpu.VMEM)
    return pl.pallas_call(
        functools.partial(renew_kernel, count=count, unroll=unroll),
        in_specs=[whole] * 2,
        out_specs=[whole] * 2,
        out_shape=[jax.ShapeDtypeStruct((count // 2, BLK, BLK), single)] * 2,
        scratch_shapes=[pltpu.VMEM((count * BLK, BLK), single)] * 2
        + [pltpu.VMEM((count * PANEL, BLK), single)],
        compiler_params=pltpu.CompilerParams(vmem_limit_bytes=48 * 2**20),
        name="renew",
    )(gram.reshape(count * BLK, BLK), product.reshape(count * BLK, BLK))


def whole_spec():
    return pl.BlockSpec(memory_space=pltpu.VMEM)


def fixed(shape):
    return pl.BlockSpec(shape, lambda *_: (0,) * len(shape))


def anywhere():
    return pl.BlockSpec(memory_space=pl.ANY)


def cost(flops, *arrays):
    moved = sum(math.prod(a.shape) * jnp.dtype(a.dtype).itemsize for a in arrays)
    return pl.CostEstimate(flops=flops // 16, bytes_accessed=moved // 16, transcendentals=0)


def of(shape, dtype):
    return jax.ShapeDtypeStruct(shape, dtype)


def flip_rows(value):
    return value.astype(single).T.astype(bfloat)


def attend_kernel(q_ref, k_ref, v_ref, valid_ref, w_ref, *refs, heads, own):
    attended_ref, lse_ref, branch_ref, flipped_ref, score_ref, prob_ref = refs[-6:]
    keys, width = k_ref.shape
    rows = q_ref.shape[0]
    tile = 128

    flipped_ref[...] = flip_rows(v_ref[...])
    queries = flip_rows(q_ref[...]) * (HEAD_DIM ** (-0.5))
    queries = queries.astype(bfloat)
    head_of = lax.broadcasted_iota(jnp.int32, (width, rows), 0) // HEAD_DIM
    mixed = []
    for head in range(heads):
        score_ref[...] = dot_of(
            k_ref[...], jnp.where(head_of == head, queries, jnp.zeros_like(queries)), 1, 0
        )

        def masked(index):
            here = pl.ds(pl.multiple_of(index * tile, tile), tile)
            valid = valid_ref[here, :]
            valid = jnp.concatenate([valid] * (rows // 128), 1)
            return here, jnp.where(valid > 0.0, score_ref[here, :], masked_score)

        def highest_of(index, best):
            _, value = masked(index)
            return jnp.maximum(best, jnp.max(value.reshape(tile // 8, 8, rows), 0))

        best = lax.fori_loop(
            0, keys // tile, highest_of, jnp.full((8, rows), -jnp.inf, single), unroll=True
        )
        best = jnp.max(best, 0, keepdims=True)

        def weigh(index, total):
            here, value = masked(index)
            value = jnp.exp(value - best)
            prob_ref[here, :] = value.astype(bfloat)
            return total + jnp.sum(value.reshape(tile // 8, 8, rows), 0)

        total = lax.fori_loop(
            0, keys // tile, weigh, jnp.zeros((8, rows), single), unroll=True
        )
        total = jnp.sum(total, 0, keepdims=True)
        out = dot_of(
            flipped_ref[head * HEAD_DIM : (head + 1) * HEAD_DIM, :], prob_ref[...], 1, 0
        )
        mixed.append(out * (1.0 / total))
        lse_ref[head : head + 1, :] = best + jnp.log(total)
    attended = jnp.concatenate(mixed, 0).T.astype(bfloat)
    attended_ref[...] = attended
    branch = dot_of(attended, w_ref[...], 1, 0)
    if own:
        branch = branch + refs[0][...].astype(single)
    branch_ref[...] = branch.astype(bfloat)


def attend(projected, valid, w_out, block, received=None, after=()):
    seq, width = projected.shape[0], w_out.shape[0]
    rows = seq // 4
    heads = width // HEAD_DIM
    own = received is not None
    more = [received] if own else []
    out_shape = [of((rows, width), bfloat), of((heads, rows), single), of((rows, D), bfloat)]
    return pl.pallas_call(
        functools.partial(attend_kernel, heads=heads, own=own),
        grid=(1,),
        in_specs=[
            pl.BlockSpec((rows, width), lambda i: (block, 0)),
            pl.BlockSpec((seq, width), lambda i: (0, 1)),
            pl.BlockSpec((seq, width), lambda i: (0, 2)),
            fixed(valid.shape),
            fixed(w_out.shape),
        ] + [fixed(value.shape) for value in more] + [anywhere()] * len(after),
        out_specs=[fixed(value.shape) for value in out_shape],
        out_shape=out_shape,
        scratch_shapes=[
            pltpu.VMEM((width, seq), bfloat), pltpu.VMEM((seq, rows), single),
            pltpu.VMEM((seq, rows), bfloat),
        ],
        cost_estimate=cost(2 * 2 * rows * seq * width * heads, projected, *out_shape),
        compiler_params=pltpu.CompilerParams(vmem_limit_bytes=24 * 2**20),
        name="attend",
    )(projected, projected, projected, valid, w_out, *more, *after)


def attend_back_kernel(*refs, heads, first, extra):
    inputs = 11 if first else 13
    refs = refs[:inputs] + refs[inputs + extra :]
    if first:
        (own_ref, peer_ref, w_ref, q_ref, k_ref, v_ref, att_own, att_peer, lse_own, lse_peer,
         valid_ref, dq_ref, dk_ref, dv_ref, flipped_ref, grad_ref, score_ref, cross_ref, prob_ref, back_ref,
         att_ref, log_ref, dk_sum, dv_sum) = refs
    else:
        (own_ref, peer_ref, w_ref, q_ref, k_ref, v_ref, att_own, att_peer, lse_own, lse_peer,
         valid_ref, dk_in_ref, dv_in_ref, dq_ref, dk_ref, dv_ref, flipped_ref, grad_ref, score_ref,
         cross_ref, prob_ref, back_ref, att_ref, log_ref, dk_sum, dv_sum) = refs
    step = pl.program_id(0)
    keys, width = k_ref.shape
    rows = q_ref.shape[0]
    scale = HEAD_DIM ** (-0.5)
    tile = 128

    @pl.when(step == 0)
    def _():
        flipped_ref[...] = flip_rows(k_ref[...])
        grad_ref[...] = own_ref[...]
        att_ref[...] = att_own[...]
        log_ref[...] = lse_own[...]
        if first:
            dk_sum[...] = jnp.zeros_like(dk_sum)
            dv_sum[...] = jnp.zeros_like(dv_sum)
        else:
            dk_sum[...] = dk_in_ref[...]
            dv_sum[...] = dv_in_ref[...]

    @pl.when(step == 1)
    def _():
        grad_ref[...] = peer_ref[...]
        att_ref[...] = att_peer[...]
        log_ref[...] = lse_peer[...]

    grads = dot_of(grad_ref[...], w_ref[...], 1, 1).astype(bfloat)
    flat = grads.astype(single).T
    cross = flat * att_ref[...].astype(single).T
    grads_t = flat.astype(bfloat)
    queries = q_ref[...]
    queries_t = (flip_rows(queries) * scale).astype(bfloat)
    head_of = lax.broadcasted_iota(jnp.int32, (width, rows), 0) // HEAD_DIM
    none = jnp.zeros_like(grads_t)
    dq = []
    for head in range(heads):
        score_ref[...] = dot_of(k_ref[...], jnp.where(head_of == head, queries_t, none), 1, 0)
        cross_ref[...] = dot_of(v_ref[...], jnp.where(head_of == head, grads_t, none), 1, 0)
        lse = log_ref[head : head + 1, :]
        mean = jnp.sum(cross[head * HEAD_DIM : (head + 1) * HEAD_DIM], 0, keepdims=True)
        at = slice(head * rows, (head + 1) * rows)

        def weigh(index, nothing):
            here = pl.ds(pl.multiple_of(index * tile, tile), tile)
            valid = jnp.concatenate([valid_ref[here, :]] * (rows // 128), 1)
            value = jnp.where(valid > 0.0, score_ref[here, :], masked_score)
            prob = jnp.exp(value - lse)
            prob_ref[here, at] = prob.astype(bfloat)
            back_ref[here, at] = (prob * (cross_ref[here, :] - mean)).astype(bfloat)
            return nothing

        lax.fori_loop(0, keys // tile, weigh, 0, unroll=True)
        dq.append(
            dot_of(flipped_ref[head * HEAD_DIM : (head + 1) * HEAD_DIM, :], back_ref[:, at], 1, 0)
        )
    dq_ref[...] = (jnp.concatenate(dq, 0).T * scale).astype(bfloat)
    lane_head = lax.broadcasted_iota(jnp.int32, (rows, width), 1) // HEAD_DIM
    query_rows = jnp.concatenate(
        [jnp.where(lane_head == head, queries, jnp.zeros_like(queries)) for head in range(heads)], 0
    )
    grad_rows = jnp.concatenate(
        [jnp.where(lane_head == head, grads, jnp.zeros_like(grads)) for head in range(heads)], 0
    )

    def total(index, nothing):
        here = pl.ds(pl.multiple_of(index * 256, 256), 256)
        dk_sum[here, :] = dk_sum[here, :] + dot_of(back_ref[here, :], query_rows, 1, 0) * scale
        dv_sum[here, :] = dv_sum[here, :] + dot_of(prob_ref[here, :], grad_rows, 1, 0)
        return nothing

    lax.fori_loop(0, keys // 256, total, 0, unroll=True)

    @pl.when(step == 1)
    def _():
        dk_ref[...] = dk_sum[...].astype(dk_ref.dtype)
        dv_ref[...] = dv_sum[...].astype(dv_ref.dtype)


def attend_back(own, peer, w_out, projected, attended, lse, valid, part, earlier=None, after=()):
    seq, width = projected.shape[0], w_out.shape[0]
    rows = seq // 4
    heads = width // HEAD_DIM
    first = earlier is None
    kind = single if first else bfloat
    more = [] if first else list(earlier)
    out_shape = [of((2 * rows, width), bfloat), of((seq, width), kind), of((seq, width), kind)]
    return pl.pallas_call(
        functools.partial(attend_back_kernel, heads=heads, first=first, extra=len(after)),
        grid=(2,),
        in_specs=[
            fixed(own.shape), fixed(peer.shape), fixed(w_out.shape),
            pl.BlockSpec((rows, width), lambda i: (2 * part + i, 0)),
            pl.BlockSpec((seq, width), lambda i: (0, 1)),
            pl.BlockSpec((seq, width), lambda i: (0, 2)),
            fixed((rows, width)), fixed((rows, width)), fixed((heads, rows)), fixed((heads, rows)),
            fixed(valid.shape),
        ] + [fixed((seq, width))] * len(more) + [anywhere()] * len(after),
        out_specs=[
            pl.BlockSpec((rows, width), lambda i: (i, 0)),
            fixed((seq, width)), fixed((seq, width)),
        ],
        out_shape=out_shape,
        scratch_shapes=[
            pltpu.VMEM((width, seq), bfloat), pltpu.VMEM((rows, D), bfloat),
            pltpu.VMEM((seq, rows), single), pltpu.VMEM((seq, rows), single),
            pltpu.VMEM((seq, heads * rows), bfloat), pltpu.VMEM((seq, heads * rows), bfloat),
            pltpu.VMEM((rows, width), bfloat), pltpu.VMEM((heads, rows), single),
            pltpu.VMEM((seq, width), single), pltpu.VMEM((seq, width), single),
        ],
        cost_estimate=cost(2 * 2 * rows * seq * width * 5 * heads, projected, *out_shape),
        compiler_params=pltpu.CompilerParams(vmem_limit_bytes=32 * 2**20),
        name="attend_back",
    )(own, peer, w_out, projected, projected, projected, *attended, *lse, valid, *more, *after)


def gelu_pair(value):
    size = jnp.abs(value)
    ratio = 1.0 / (1.0 + (0.3275911 * 0.5**0.5) * size)
    bell = jnp.exp(-0.5 * value * value)
    series = 0.5 * 1.061405429 * ratio + 0.5 * -1.453152027
    series = series * ratio + 0.5 * 1.421413741
    series = series * ratio + 0.5 * -0.284496736
    series = series * ratio + 0.5 * 0.254829592
    tail = series * ratio * bell
    below = jnp.where(value >= 0.0, 1.0 - tail, tail)
    return value * below, below + value * bell * (1.0 / math.sqrt(2.0 * math.pi))


def feed_kernel(rows_ref, up_ref, bias_ref, down_ref, *refs):
    act_ref, slope_ref, out_ref, pre_ref, sum_ref = refs[-5:]
    step = pl.program_id(0)
    rows = rows_ref.shape[0]
    tile = 32
    pre_ref[...] = dot_of(rows_ref[...], up_ref[...], 1, 0)

    def activate(index, nothing):
        here = pl.ds(pl.multiple_of(index * tile, tile), tile)
        value, slope = gelu_pair(pre_ref[here, :] + bias_ref[...])
        act_ref[here, :] = value.astype(bfloat)
        slope_ref[here, :] = slope.astype(bfloat)
        return nothing

    lax.fori_loop(0, rows // tile, activate, 0, unroll=4)
    add_up(step, dot_of(act_ref[...], down_ref[...], 1, 0), sum_ref, out_ref)


def add_up(step, more, sum_ref, out_ref):
    last = pl.num_programs(0) - 1

    @pl.when(step == 0)
    def _():
        sum_ref[...] = more

    @pl.when((step > 0) & (step < last))
    def _():
        sum_ref[...] = sum_ref[...] + more

    @pl.when(step == last)
    def _():
        out_ref[...] = (sum_ref[...] + more).astype(out_ref.dtype)


def feed(block, w_up, bias, w_down, kind, after=()):
    rows, hidden = block.shape[0], w_up.shape[1]
    step = 256
    out_shape = [of((rows, hidden), bfloat), of((rows, hidden), bfloat), of((rows, D), kind)]
    return pl.pallas_call(
        feed_kernel,
        grid=(hidden // step,),
        in_specs=[
            fixed(block.shape),
            pl.BlockSpec((D, step), lambda j: (0, j)),
            pl.BlockSpec((1, step), lambda j: (0, j)),
            pl.BlockSpec((step, D), lambda j: (j, 0)),
        ] + [anywhere()] * len(after),
        out_specs=[
            pl.BlockSpec((rows, step), lambda j: (0, j)),
            pl.BlockSpec((rows, step), lambda j: (0, j)),
            fixed((rows, D)),
        ],
        out_shape=out_shape,
        scratch_shapes=[pltpu.VMEM((rows, step), single), pltpu.VMEM((rows, D), single)],
        cost_estimate=cost(4 * rows * D * hidden, w_up, w_down, *out_shape),
        compiler_params=pltpu.CompilerParams(vmem_limit_bytes=20 * 2**20),
        name="feed",
    )(block, w_up, bias, w_down, *after)


def feed_back_kernel(rows_ref, down_ref, up_ref, slope_ref, *refs):
    grad_ref, bias_ref, out_ref, sum_ref = refs[-4:]
    grads = dot_of(rows_ref[...], down_ref[...], 1, 1) * slope_ref[...].astype(single)
    grads = grads.astype(bfloat)
    grad_ref[...] = grads
    bias_ref[...] = jnp.sum(grads.astype(single), 0, keepdims=True)
    add_up(pl.program_id(0), dot_of(grads, up_ref[...], 1, 1), sum_ref, out_ref)


def feed_back(block, w_down, w_up, slope, kind, after=()):
    rows, hidden = block.shape[0], w_up.shape[1]
    step = 256
    out_shape = [of((rows, hidden), bfloat), of((1, hidden), single), of((rows, D), kind)]
    return pl.pallas_call(
        feed_back_kernel,
        grid=(hidden // step,),
        in_specs=[
            fixed(block.shape),
            pl.BlockSpec((step, D), lambda j: (j, 0)),
            pl.BlockSpec((D, step), lambda j: (0, j)),
            pl.BlockSpec((rows, step), lambda j: (0, j)),
        ] + [anywhere()] * len(after),
        out_specs=[
            pl.BlockSpec((rows, step), lambda j: (0, j)),
            pl.BlockSpec((1, step), lambda j: (0, j)),
            fixed((rows, D)),
        ],
        out_shape=out_shape,
        scratch_shapes=[pltpu.VMEM((rows, D), single)],
        cost_estimate=cost(4 * rows * D * hidden, w_up, w_down, *out_shape),
        compiler_params=pltpu.CompilerParams(vmem_limit_bytes=20 * 2**20),
        name="feed_back",
    )(block, w_down, w_up, slope, *after)


def chip_kernel(keep_ref, got_ref, *refs):
    refs[-1][...] = (keep_ref[...] + got_ref[...].astype(single)).astype(bfloat)


def standardise(value):
    centred = value - jnp.mean(value, -1, keepdims=True)
    inv_std = lax.rsqrt(jnp.mean(centred * centred, -1, keepdims=True) + norm_eps)
    return centred * inv_std, inv_std


def through_norm(grads, normed, inv_std, gain):
    scaled = grads * gain
    mean_grad = jnp.mean(scaled, -1, keepdims=True)
    mean_cross = jnp.mean(scaled * normed, -1, keepdims=True)
    return inv_std * (scaled - mean_grad - normed * mean_cross)


def gain_sums(grads, normed, rounded):
    total = lambda value: jnp.sum(value, 0, keepdims=True)
    blank = jnp.zeros((5, grads.shape[1]), single)
    return jnp.concatenate(
        [total(grads * normed), total(grads), total(rounded.astype(single)), blank], 0
    )


norm_tile = 64


def norm_one_kernel(chip_ref, across_ref, rows_ref, vectors_ref, *refs):
    normed_ref, inv_ref, hidden_ref = refs[-3:]
    branch = chip_ref[...].astype(single) + across_ref[...].astype(single)
    normed, inv_std = standardise(rows_ref[...].astype(single) + (branch + vectors_ref[2:3, :]))
    normed_ref[...] = normed
    inv_ref[...] = jnp.broadcast_to(inv_std, inv_ref.shape)
    hidden_ref[...] = (normed * vectors_ref[0:1, :] + vectors_ref[1:2, :]).astype(bfloat)


def norm_two_kernel(
    chip_ref, across_ref, normed_ref, cot_ref, valid_ref, one_ref, two_ref, *refs
):
    out_ref, grad_ref, low_ref, sums_ref = refs[-4:]

    @pl.when(pl.program_id(0) == 0)
    def _():
        sums_ref[...] = jnp.zeros_like(sums_ref)

    hidden = normed_ref[...] * one_ref[0:1, :] + one_ref[1:2, :]
    down = chip_ref[...].astype(single) + across_ref[...].astype(single)
    normed, inv_std = standardise(hidden + (down + two_ref[2:3, :]))
    gain = two_ref[0:1, :]
    out_ref[...] = (normed * gain + two_ref[1:2, :]).astype(bfloat)
    grads = cot_ref[...].astype(single) * valid_ref[:, 0:1]
    back = through_norm(grads, normed, inv_std, gain)
    grad_ref[...] = back
    low = back.astype(bfloat)
    low_ref[...] = low
    sums_ref[...] += gain_sums(grads, normed, low)


def norm_back_kernel(
    chip_ref, across_ref, second_ref, normed_ref, inv_ref, one_ref, *refs
):
    grad_ref, low_ref, sums_ref = refs[-3:]

    @pl.when(pl.program_id(0) == 0)
    def _():
        sums_ref[...] = jnp.zeros_like(sums_ref)

    grads = chip_ref[...].astype(single) + across_ref[...].astype(single) + second_ref[...]
    normed = normed_ref[...]
    back = through_norm(grads, normed, inv_ref[:, 0:1], one_ref[0:1, :])
    grad_ref[...] = back
    low = back.astype(bfloat)
    low_ref[...] = low
    sums_ref[...] += gain_sums(grads, normed, low)


def norm_call(kernel, name, rowed, fixed_in, row_outs, sums, after=()):
    rows = rowed[0].shape[0]
    by_row = lambda width: pl.BlockSpec((norm_tile, width), lambda i: (i, 0))
    out_shape = [of((rows, width), kind) for width, kind in row_outs]
    out_specs = [by_row(width) for width, _ in row_outs]
    if sums:
        out_shape.append(of((8, D), single))
        out_specs.append(fixed((8, D)))
    return pl.pallas_call(
        kernel,
        grid=(rows // norm_tile,),
        in_specs=[by_row(value.shape[1]) for value in rowed]
        + [fixed(value.shape) for value in fixed_in]
        + [anywhere()] * len(after),
        out_specs=out_specs,
        out_shape=out_shape,
        cost_estimate=cost(20 * rows * D, *rowed, *out_shape),
        compiler_params=pltpu.CompilerParams(vmem_limit_bytes=16 * 2**20),
        name=name,
    )(*rowed, *fixed_in, *after)


def token_back_kernel(*refs):
    dq_refs, (dk_ref, dv_ref, w_ref), outs = refs[:2], refs[2:5], refs[5:]
    width = dk_ref.shape[1]
    rows = dk_ref.shape[0] // 4
    for block in range(4):
        here = slice(block * rows, (block + 1) * rows)
        parts = [
            dq_refs[block // 2][block % 2 * rows : (block % 2 + 1) * rows, :],
            dk_ref[here, :], dv_ref[here, :],
        ]
        value = dot_of(jnp.concatenate(parts, 1), w_ref[...], 1, 1)
        outs[block][...] = value.astype(outs[block].dtype)


def token_back(dq_a, dq_b, dk, dv, w_qkv):
    rows = dk.shape[0] // 4
    out_shape = [of((rows, D), kind) for kind in (single, bfloat, single, bfloat)]
    return pl.pallas_call(
        token_back_kernel,
        in_specs=[whole_spec()] * 5,
        out_specs=[whole_spec()] * 4,
        out_shape=out_shape,
        cost_estimate=cost(8 * rows * D * w_qkv.shape[1], w_qkv, dk, *out_shape),
        compiler_params=pltpu.CompilerParams(vmem_limit_bytes=24 * 2**20),
        name="token_back",
    )(dq_a, dq_b, dk, dv, w_qkv)


def pack_kernel(target_ref, *refs, jobs, scale):
    inputs, out_ref, held_ref, sem = refs[:-3], refs[-3], refs[-2], refs[-1]
    place = 0
    for lefts, rights, layout, rows, cols in jobs:
        for row in range(0, rows, 2):
            span = min(2, rows - row)
            weights = 0.0
            for (left, left_at, size), (right, right_at, _) in zip(lefts, rights):
                weights = weights + dot_of(
                    inputs[left][left_at : left_at + size, row * BLK : (row + span) * BLK],
                    inputs[right][right_at : right_at + size, :],
                    0,
                    0,
                )
            weights = (weights * scale).astype(bfloat)
            for i in range(span):
                for col in range(cols):
                    held_ref[place] = weights[
                        i * BLK : (i + 1) * BLK, col * BLK : (col + 1) * BLK
                    ]
                    pltpu.make_async_copy(
                        held_ref.at[place], out_ref.at[target_ref[layout(row + i, col)]], sem
                    ).start()
                    place += 1
    pltpu.make_async_copy(held_ref, out_ref.at[pl.ds(0, place)], sem).wait()


def pack(target, pairs, scale, total, earlier=None, after=()):
    operands, jobs, blocks, flops = [], [], 0, 0

    def segments(arrays, size):
        found = []
        for value in arrays:
            if not any(value is other for other in operands):
                operands.append(value)
            index = [value is other for other in operands].index(True)
            found += [(index, at, size) for at in range(0, value.shape[0], size)]
        return found

    for lefts, rights, layout in pairs:
        size = min(value.shape[0] for value in lefts + rights)
        rows, cols = lefts[0].shape[1] // BLK, rights[0].shape[1] // BLK
        jobs.append((segments(lefts, size), segments(rights, size), layout, rows, cols))
        blocks += rows * cols
        flops += 2 * rows * cols * BLK * BLK * sum(value.shape[0] for value in lefts)
    some = pl.BlockSpec(memory_space=pl.ANY)
    more = [] if earlier is None else [earlier]
    return pl.pallas_call(
        functools.partial(pack_kernel, jobs=jobs, scale=scale),
        grid_spec=pltpu.PrefetchScalarGridSpec(
            num_scalar_prefetch=1,
            grid=(),
            in_specs=[whole_spec()] * len(operands) + [some] * (len(more) + len(after)),
            out_specs=some,
            scratch_shapes=[pltpu.VMEM((blocks, BLK, BLK), bfloat), pltpu.SemaphoreType.DMA],
        ),
        out_shape=of((total, BLK, BLK), bfloat),
        input_output_aliases={1 + len(operands): 0} if more else {},
        cost_estimate=cost(flops, *operands, of((blocks, BLK, BLK), bfloat)),
        compiler_params=pltpu.CompilerParams(vmem_limit_bytes=32 * 2**20),
        name="pack",
    )(target, *operands, *more, *after)


def block_counts(tensors):
    return (D * D // (tensors * BLK * BLK), D * FF // (tensors * BLK * BLK))


def rate_values(canon_index, tensors, seq_len):
    attn_count, ffn_count = block_counts(tensors)
    out_std = math.sqrt(seq_len / (3.0 * D))
    inner = jnp.where(canon_index < 4 * attn_count + ffn_count, D ** (-0.5), FF ** (-0.5))
    inner = jnp.where(canon_index < 4 * attn_count, out_std, inner)
    return jnp.where(canon_index < 3 * attn_count, D ** (-0.5), inner).astype(single)


def swap(value, axis, bit):
    count = lax.axis_size(axis)
    return lax.ppermute(value, axis, [(i, i ^ bit) for i in range(count)])


def ring(value):
    count = lax.axis_size("dp")
    return lax.ppermute(value, "dp", [(i, (i + 2) % count) for i in range(count)])


def total_of(value):
    for axis in ("tensor", "dp"):
        bit = 1
        while bit < lax.axis_size(axis):
            value = value + swap(value, axis, bit)
            bit *= 2
    return value


def gather_slots(local, parts):
    size = local.shape[0] // parts
    hops = lax.axis_size("dp") // 2
    pieces = [[[None] * parts for _ in range(2)] for _ in range(hops)]
    for part in range(parts):
        shard = local[part * size : (part + 1) * size]
        for hop in range(hops):
            pieces[hop][0][part] = shard
            pieces[hop][1][part] = swap(shard, "dp", 1)
            if hop < hops - 1:
                shard = ring(shard)
    return [piece for pair in pieces for flip in pair for piece in flip]


def scatter_slots(sent, slots, parts):
    hops = lax.axis_size("dp") // 2
    size = slots // parts
    shaped = sent.reshape(hops, 2, slots, BLK, BLK)
    done = []
    for part in range(parts):
        piece = shaped[:, :, part * size : (part + 1) * size]
        carried = None
        for hop in range(hops - 1, -1, -1):
            mine = piece[hop, 0].astype(single) + swap(piece[hop, 1], "dp", 1).astype(single)
            if carried is not None:
                mine = mine + carried.astype(single)
            if hop > 0:
                carried = ring(mine.astype(bfloat))
        done.append(mine.astype(bfloat))
    return jnp.concatenate(done, 0)


def assemble_kernel(source_ref, *refs, sizes, layouts):
    count = len(sizes)
    pieces, outs, (held, sems) = refs[:count], refs[count:-2], refs[-2:]
    copies, start = [], 0
    for index, size in enumerate(sizes):
        copies.append(pltpu.make_async_copy(pieces[index], held.at[start : start + size], sems.at[index]))
        start += size
    for copy in copies:
        copy.start()
    for copy in copies:
        copy.wait()
    canon = 0
    for target, rows, cols, row_at, col_at in layouts:
        for row in range(rows):
            for col in range(cols):
                outs[target][
                    (row_at + row) * BLK : (row_at + row + 1) * BLK,
                    (col_at + col) * BLK : (col_at + col + 1) * BLK,
                ] = held[source_ref[canon]]
                canon += 1


def assemble(source, pieces, shapes, layouts):
    sizes = [piece.shape[0] for piece in pieces]
    return pl.pallas_call(
        functools.partial(assemble_kernel, sizes=sizes, layouts=layouts),
        grid_spec=pltpu.PrefetchScalarGridSpec(
            num_scalar_prefetch=1,
            grid=(1,),
            in_specs=[pl.BlockSpec(memory_space=pl.ANY)] * len(pieces),
            out_specs=[pl.BlockSpec(shape, lambda i, *_: (0, 0)) for shape in shapes],
            scratch_shapes=[
                pltpu.VMEM((sum(sizes), BLK, BLK), bfloat),
                pltpu.SemaphoreType.DMA((len(sizes),)),
            ],
        ),
        out_shape=[jax.ShapeDtypeStruct(shape, bfloat) for shape in shapes],
        compiler_params=pltpu.CompilerParams(vmem_limit_bytes=40 * 2**20),
        name="assemble",
    )(source, *pieces)


def chip_sum(keep, send, after=()):
    return norm_call(
        chip_kernel, "chip_sum", [keep, peer_of(send)], [], [(D, bfloat)], False, after
    )[0]


def across(value):
    return swap(value, "tensor", 2)


def peer_of(value):
    return swap(value, "tensor", 1)


def body(
    tokens,
    cotangent,
    seq_lengths,
    block_owner,
    master_blocks,
    first_moment,
    second_moment,
    left_stats,
    right_stats,
    left_basis,
    right_basis,
    vector_master,
    vector_first,
    vector_second,
):
    tensors = lax.axis_size("tensor")
    data_ranks = lax.axis_size("dp")
    tensor_rank = lax.axis_index("tensor")
    data_rank = lax.axis_index("dp")
    local_rows = tokens.shape[0]
    seq_len = local_rows * tensors
    slice_width = D // tensors
    hidden_width = FF // tensors
    block_total = block_owner.shape[0]
    slots_here = master_blocks.shape[1]
    length = seq_lengths[0]
    attn_count, ffn_count = block_counts(tensors)
    permuted = data_ranks <= 16
    hops = data_ranks // 2
    parts = 3 if permuted else 1

    holder, slot = block_owner // slots_here, block_owner % slots_here
    flip = (holder % 2) ^ (data_rank % 2)
    down = (data_rank // 2 - holder // 2) % hops
    up = (holder // 2 - data_rank // 2) % hops
    source = (down * 2 + flip) * slots_here + slot
    target = (up * 2 + flip) * slots_here + slot
    if not permuted:
        source = target = block_owner
    canon_ids = jnp.arange(block_total, dtype=jnp.int32)
    inverse = jnp.zeros((block_total,), jnp.int32).at[block_owner].set(canon_ids)

    local_weights = master_blocks[0].astype(bfloat)
    if permuted:
        pieces = gather_slots(local_weights, parts)
    else:
        pieces = [lax.all_gather(local_weights, "dp", axis=0, tiled=True)]
    cols = slice_width // BLK
    wide = hidden_width // BLK
    full = D // BLK
    w_qkv, w_out, w_up, w_down = assemble(
        source,
        pieces,
        [(D, 3 * slice_width), (slice_width, D), (D, hidden_width), (hidden_width, D)],
        [
            (0, full, cols, 0, 0),
            (0, full, cols, 0, cols),
            (0, full, cols, 0, 2 * cols),
            (1, cols, full, 0, 0),
            (2, full, wide, 0, 0),
            (3, wide, full, 0, 0),
        ],
    )
    gain_one, shift_one = (vector_master[0:D], vector_master[D : 2 * D])
    gain_two, shift_two = (vector_master[2 * D : 3 * D], vector_master[3 * D : 4 * D])
    bias_query = lax.dynamic_slice_in_dim(
        vector_master, 4 * D + tensor_rank * slice_width, slice_width
    )
    bias_value = lax.dynamic_slice_in_dim(
        vector_master, 5 * D + tensor_rank * slice_width, slice_width
    )
    bias_out = vector_master[6 * D : 7 * D]
    bias_up = lax.dynamic_slice_in_dim(
        vector_master, 7 * D + tensor_rank * hidden_width, hidden_width
    )
    bias_down = vector_master[7 * D + FF : 8 * D + FF]

    tokens_b = swap(tokens, "tensor", 2)
    cotangent_b = swap(cotangent, "tensor", 2)
    full_tokens = jnp.concatenate(
        [tokens, peer_of(tokens), tokens_b, peer_of(tokens_b)], axis=0
    )
    quarters = tensor_rank ^ jnp.arange(4, dtype=jnp.int32)
    positions = (quarters[:, None] * local_rows + jnp.arange(local_rows)[None, :]).reshape(-1)
    key_valid = positions < length
    row_valid = key_valid.astype(single)[:, None]
    chunk = 2 * local_rows

    bias_qkv = jnp.concatenate([bias_query, jnp.zeros((slice_width,), single), bias_value])
    projected = (jnp.dot(full_tokens, w_qkv, preferred_element_type=single) + bias_qkv).astype(
        bfloat
    )
    one = jnp.stack([gain_one, shift_one, bias_out])
    two = jnp.stack([gain_two, shift_two, bias_down])
    valid = jnp.broadcast_to(row_valid, (seq_len, 128))
    grad_scale = 1.0 / math.sqrt(seq_len * data_ranks)
    up_start = 4 * attn_count

    attended, lse, shares = [None] * 4, [None] * 4, [None] * 4
    attended[3], lse[3], shares[3] = attend(projected, valid, w_out, 3, after=[cotangent_b])
    attended[1], lse[1], shares[1] = attend(projected, valid, w_out, 1, after=[shares[3]])
    for block in (2, 0):
        attended[block], lse[block], shares[block] = attend(
            projected, valid, w_out, block, peer_of(shares[block + 1]),
            after=[shares[1] if block == 2 else shares[2]],
        )
    chip = [shares[0], shares[2]]
    other = [across(chip[1]), across(chip[0])]

    normed_one, inv_one = [None] * 2, [None] * 2
    hidden, activation, slope, chip_two = [None] * 4, [None] * 4, [None] * 4, [None] * 2
    bias_row = bias_up[None, :]

    def norm_up(part, after):
        normed_one[part], inv_one[part], hidden[2 * part] = norm_call(
            norm_one_kernel, "norm_one", [chip[part], other[part], (tokens, tokens_b)[part]],
            [one], [(D, single), (128, single), (D, bfloat)], False, after,
        )
        hidden[2 * part + 1] = peer_of(hidden[2 * part])

    def feed_part(part, after):
        block = 2 * part
        activation[block], slope[block], keep = feed(
            hidden[block], w_up, bias_row, w_down, single, after
        )
        block += 1
        activation[block], slope[block], send = feed(
            hidden[block], w_up, bias_row, w_down, bfloat, [keep]
        )
        return keep, send

    norm_up(0, [chip[0]])
    sums = feed_part(0, [])
    norm_up(1, [sums[1]])
    chip_two[0] = chip_sum(*sums, [hidden[2]])
    sums = feed_part(1, [chip_two[0]])
    chip_two[1] = chip_sum(*sums)
    other = [across(chip_two[1]), across(chip_two[0])]

    grad_second, grad_down, grad_up = [None] * 2, [None] * 4, [None] * 4
    bias_parts, chip_three, outs, sums_two = [None] * 4, [None] * 2, [None] * 2, [None] * 2

    def norm_down(part, after):
        rows_valid = valid[part * chunk : part * chunk + local_rows]
        outs[part], grad_second[part], grad_down[2 * part], sums_two[part] = norm_call(
            norm_two_kernel, "norm_two",
            [chip_two[part], other[part], normed_one[part], (cotangent, cotangent_b)[part],
             rows_valid],
            [one, two], [(D, bfloat), (D, single), (D, bfloat)], True, after,
        )
        grad_down[2 * part + 1] = peer_of(grad_down[2 * part])

    def feed_back_part(part, after):
        block = 2 * part
        grad_up[block], bias_parts[block], keep = feed_back(
            grad_down[block], w_down, w_up, slope[block], single, after
        )
        block += 1
        grad_up[block], bias_parts[block], send = feed_back(
            grad_down[block], w_down, w_up, slope[block], bfloat, [keep]
        )
        return keep, send

    norm_down(1, [chip_two[1]])
    sums = feed_back_part(1, [])
    norm_down(0, [sums[1]])
    chip_three[1] = chip_sum(*sums, [grad_down[0]])
    sums = feed_back_part(0, [chip_three[1]])
    chip_three[0] = chip_sum(*sums)
    other = [across(chip_three[1]), across(chip_three[0])]
    layer_output = outs[0]
    dgain_two, dshift_two, dbias_down = sums_two[0][0], sums_two[0][1], sums_two[0][2]
    dbias_up = (bias_parts[0] + bias_parts[1] + bias_parts[2] + bias_parts[3])[0]
    sent = pack(
        target,
        [
            (hidden, grad_up, lambda row, col: up_start + row * wide + col),
            (activation, grad_down, lambda row, col: up_start + ffn_count + row * full + col),
        ],
        grad_scale,
        block_total,
        after=[chip_three[0]],
    )

    grad_branch, grad_query, back, grad_rows, sums_one = [None] * 4, [None] * 2, None, [0, 0], [0, 0]
    after = [sent]
    for part in (0, 1):
        block = 2 * part
        grad_rows[part], grad_branch[block], sums_one[part] = norm_call(
            norm_back_kernel, "norm_back",
            [chip_three[part], other[part], grad_second[part], normed_one[part], inv_one[part]],
            [one], [(D, single), (D, bfloat)], True, after,
        )
        grad_branch[block + 1] = peer_of(grad_branch[block])
        grad_query[part], *back = attend_back(
            grad_branch[block], grad_branch[block + 1], w_out, projected,
            attended[block : block + 2], lse[block : block + 2], valid, part, back,
        )
        after = [back[0]]
    grad_summed, sums_one = grad_rows[0], sums_one[0]
    dgain_one, dshift_one, dbias_out = sums_one[0], sums_one[1], sums_one[2]
    grad_key, grad_value = back
    sent = pack(
        target,
        [
            (
                [full_tokens],
                grad_query,
                lambda row, col: row * cols + col,
            ),
            (
                [full_tokens],
                [grad_key],
                lambda row, col: attn_count + row * cols + col,
            ),
            (
                [full_tokens],
                [grad_value],
                lambda row, col: 2 * attn_count + row * cols + col,
            ),
            (
                attended,
                grad_branch,
                lambda row, col: 3 * attn_count + row * full + col,
            ),
        ],
        grad_scale,
        block_total,
        sent,
    )
    dbias_query = jnp.sum(grad_query[0].astype(single), 0) + jnp.sum(
        grad_query[1].astype(single), 0
    )
    dbias_value = jnp.sum(grad_value.astype(single), 0)
    keep_a, send_a, keep_b, send_b = token_back(
        grad_query[0], grad_query[1], grad_key, grad_value, w_qkv
    )
    over = across(chip_sum(keep_b, send_b))
    token_grad = (
        chip_sum(keep_a, send_a).astype(single) + over.astype(single) + grad_summed
    ).astype(bfloat)
    vector_grad = jnp.concatenate(
        [
            dgain_one,
            dshift_one,
            dgain_two,
            dshift_two,
            jnp.zeros((2 * D,), single),
            dbias_out,
            jnp.zeros((FF,), single),
            dbias_down,
        ]
    )
    vector_grad = lax.dynamic_update_slice_in_dim(
        vector_grad, dbias_query, 4 * D + tensor_rank * slice_width, 0
    )
    vector_grad = lax.dynamic_update_slice_in_dim(
        vector_grad, dbias_value, 5 * D + tensor_rank * slice_width, 0
    )
    vector_grad = lax.dynamic_update_slice_in_dim(
        vector_grad, dbias_up, 7 * D + tensor_rank * hidden_width, 0
    )
    own_canon = lax.dynamic_slice_in_dim(inverse, data_rank * slots_here, slots_here)
    vector_sum = total_of(vector_grad) * grad_scale
    if permuted:
        own_grad = scatter_slots(sent, slots_here, 2)
    else:
        own_grad = lax.psum_scatter(sent, "dp", scatter_dimension=0, tiled=True)
    rates = rate_values(own_canon, tensors, seq_len)
    correction = 1.0 - moment_decay**STEP
    fresh_first, fresh_second, fresh_master, fresh_left, fresh_right, gram, product = adam(
        own_grad, first_moment[0], second_moment[0], master_blocks[0], left_stats[0],
        right_stats[0], left_basis[0], right_basis[0], rates, per=math.gcd(slots_here, 4)
    )
    basis_left, basis_right = renew(gram, product)
    vec_first = moment_decay * vector_first + (1.0 - moment_decay) * vector_sum
    vec_second = moment_decay * vector_second + (1.0 - moment_decay) * vector_sum * vector_sum
    vec_master = vector_master - vector_rate * (vec_first / correction) / (
        jnp.sqrt(vec_second / correction) + adam_eps
    )
    return (
        layer_output,
        token_grad,
        fresh_first[None],
        fresh_second[None],
        fresh_master[None],
        fresh_left[None],
        fresh_right[None],
        basis_left[None],
        basis_right[None],
        vec_first,
        vec_second,
        vec_master,
    )


def solution(mesh):
    return jax.shard_map(
        body,
        mesh=mesh,
        in_specs=(
            P(("dp", "tensor"), None),
            P(("dp", "tensor"), None),
            P("dp"),
            P(),
            P("tensor", "dp", None, None),
            P("tensor", "dp", None, None),
            P("tensor", "dp", None, None),
            P("tensor", "dp", None, None),
            P("tensor", "dp", None, None),
            P("tensor", "dp", None, None),
            P("tensor", "dp", None, None),
            P(),
            P(),
            P(),
        ),
        out_specs=(
            P(("dp", "tensor"), None),
            P(("dp", "tensor"), None),
            P("tensor", "dp", None, None),
            P("tensor", "dp", None, None),
            P("tensor", "dp", None, None),
            P("tensor", "dp", None, None),
            P("tensor", "dp", None, None),
            P("tensor", "dp", None, None),
            P("tensor", "dp", None, None),
            P(),
            P(),
            P(),
        ),
        check_vma=False,
    )
```

```python
import functools
import math

import jax
import jax.numpy as jnp
from jax import lax
from jax.experimental import pallas as pl
from jax.experimental.pallas import tpu as pltpu
from jax.sharding import PartitionSpec as P

D = 1024
FF = 4096
HEAD_DIM = 64
BLK = 128
STEP = 10


norm_eps = 1e-05
adam_eps = 1e-08
moment_decay = 0.5
weight_decay = 0.01
vector_rate = 0.25
masked_score = -1000000000.0
bfloat = jnp.bfloat16
single = jnp.float32


PANEL = 32


def dot_of(left, right, left_dim, right_dim):
    return lax.dot_general(
        left, right, (((left_dim,), (right_dim,)), ((), ())), preferred_element_type=single
    )


def split_two(value):
    high = value.astype(bfloat)
    return high, (value - high.astype(single)).astype(bfloat)


def split_three(value):
    high = value.astype(bfloat)
    rest = value - high.astype(single)
    mid = rest.astype(bfloat)
    return high, mid, (rest - mid.astype(single)).astype(bfloat)


def dot_three(left, right, left_dim, right_dim):
    stacked_left = jnp.concatenate([left[0], left[0], left[1]], axis=left_dim)
    stacked_right = jnp.concatenate([right[0], right[1], right[0]], axis=right_dim)
    return dot_of(stacked_left, stacked_right, left_dim, right_dim)


def dot_two(pair, other, pair_dim, other_dim, swapped=False):
    stacked = jnp.concatenate(pair, axis=pair_dim)
    twice = jnp.concatenate([other, other], axis=other_dim)
    if swapped:
        return dot_of(twice, stacked, other_dim, pair_dim)
    return dot_of(stacked, twice, pair_dim, other_dim)


def gram_six(pieces):
    high, mid, low = pieces
    left = jnp.concatenate([high, high, high, mid, mid, low], axis=1)
    right = jnp.concatenate([high, mid, low, high, mid, high], axis=1)
    return dot_of(left, right, 1, 1)


def adam_group(items, grads, states, rates, gram_ref, product_ref, count):
    correction = 1.0 - moment_decay**STEP
    scale = (1.0 - moment_decay) / BLK
    first, second, master, left_stat, right_stat, left, right = zip(*states)
    left_t = [split_two(value.T) for value in left]
    right_t = [split_two(value.T) for value in right]
    left = [split_two(value) for value in left]
    right = [split_two(value) for value in right]
    half = [dot_two(r, g, 0, 1, True).astype(bfloat) for r, g in zip(right, grads)]
    new_left = [
        moment_decay * old + scale * dot_of(g, g, 1, 1) for old, g in zip(left_stat, grads)
    ]
    new_right = [
        moment_decay * old + scale * dot_of(g, g, 0, 0) for old, g in zip(right_stat, grads)
    ]
    rotated = [dot_two(t, value, 1, 0) for t, value in zip(left_t, half)]
    sides = []
    for stats, basis in ((new_left, left_t), (new_right, right_t)):
        sides.append([dot_three(b, split_two(value), 1, 0) for b, value in zip(basis, stats)])
    new_first = [moment_decay * old + (1.0 - moment_decay) * r for old, r in zip(first, rotated)]
    new_second = [
        moment_decay * old + (1.0 - moment_decay) * r * r for old, r in zip(second, rotated)
    ]
    direction = [
        ((m / correction) / (jnp.sqrt(v / correction) + adam_eps)).astype(bfloat)
        for m, v in zip(new_first, new_second)
    ]
    half = [
        dot_two(t, value, 0, 1, True).astype(bfloat) for t, value in zip(right_t, direction)
    ]
    grams = [[gram_six(split_three(value)) for value in side] for side in sides]
    turned = [dot_two(b, value, 1, 0) for b, value in zip(left, half)]
    new_master = [
        old - rate * (value + weight_decay * old)
        for old, rate, value in zip(master, rates, turned)
    ]
    for side in range(2):
        for item, product, gram in zip(items, sides[side], grams[side]):
            here = pl.ds(pl.multiple_of((side * count + item) * BLK, BLK), BLK)
            product_ref[here, :] = product
            gram_ref[here, :] = gram
    return list(zip(new_first, new_second, new_master, new_left, new_right))


def factor_panel(rows):
    pieces = PANEL // 8
    batch = rows[0].shape[1]
    work = [
        [rows[j][8 * i : 8 * i + 8] if i >= j // 8 else None for i in range(pieces)]
        for j in range(PANEL)
    ]
    sublane = lax.broadcasted_iota(jnp.int32, (8, batch), 0)
    zero = jnp.zeros((8, batch), single)
    inverse = [[None] * pieces for _ in range(PANEL)]
    for k in range(PANEL):
        group, lane = divmod(k, 8)
        pivot = work[k][group][lane : lane + 1]
        root = lax.rsqrt(pivot)
        root = root * (1.5 - 0.5 * pivot * root * root)
        root = jnp.broadcast_to(root, (8, batch))
        column = [work[k][i] * root if i >= group else None for i in range(pieces)]
        done = []
        for i in range(group + 1):
            value = inverse[k][i]
            value = zero if value is None else value * root
            done.append(jnp.where(sublane == lane, root, value) if i == group else value)
        inverse[k] = done + [zero] * (pieces - group - 1)
        for j in range(k + 1, PANEL):
            row_group, row_lane = divmod(j, 8)
            factor = jnp.broadcast_to(column[row_group][row_lane : row_lane + 1], (8, batch))
            for i in range(row_group, pieces):
                work[j][i] = work[j][i] - factor * column[i]
            for i in range(group + 1):
                term = factor * done[i]
                inverse[j][i] = -term if inverse[j][i] is None else inverse[j][i] - term
    return inverse


def renew(gram_ref, product_ref, inverse_ref, count):
    group = math.gcd(count, 16)
    lane = lax.broadcasted_iota(jnp.int32, (PANEL, BLK), 1)
    for panel in range(BLK // PANEL):
        top = panel * PANEL
        last = panel == BLK // PANEL - 1
        rows = []
        for j in range(PANEL):
            row = gram_ref[pl.ds(top + j, count, stride=BLK), :]
            rows.append(row.T[top : top + PANEL])
        inverse = factor_panel(rows)
        for i in range(PANEL):
            row = jnp.concatenate(inverse[i], 0)
            inverse_ref[pl.ds(i, count, stride=PANEL), :] = jnp.concatenate([row] * 4, 0).T

        def step(index, nothing):
            bases = [pl.multiple_of((index * group + g) * BLK, BLK) for g in range(group)]
            lefts, wholes = [], []
            for g in range(group):
                here = pl.ds(pl.multiple_of((index * group + g) * PANEL, PANEL), PANEL)
                lefts.append(inverse_ref[here, :])
                rows_at = pl.ds(bases[g] + top, PANEL)
                whole = product_ref[rows_at, :]
                if not last:
                    whole = jnp.concatenate([gram_ref[rows_at, :], whole], 1)
                wholes.append(whole)
            rest = [pl.ds(base + top + PANEL, BLK - top - PANEL) for base in bases]
            if not last:
                old = [(gram_ref[at, :], product_ref[at, :]) for at in rest]
            lefts = [six_rows(split_three(left), lane) for left in lefts]
            wholes = [jnp.concatenate(split_three(whole), 0) for whole in wholes]
            solved = [dot_of(left, whole, 1, 0) for left, whole in zip(lefts, wholes)]
            solved = [
                value[:PANEL] + (value[PANEL : 2 * PANEL] + value[2 * PANEL :])
                for value in solved
            ]
            if not last:
                pieces = [split_three(value) for value in solved]
                lefts = [
                    jnp.concatenate([high, high, high, mid, mid, low], 0)[:, top + PANEL : BLK]
                    for high, mid, low in pieces
                ]
                rights = [
                    jnp.concatenate([high, mid, low, high, mid, high], 0)
                    for high, mid, low in pieces
                ]
                update = [dot_of(left, right, 0, 0) for left, right in zip(lefts, rights)]
            for g in range(group):
                product_ref[pl.ds(bases[g] + top, PANEL), :] = solved[g][:, -BLK:]
                if not last:
                    gram_ref[rest[g], :] = old[g][0] - update[g][:, :BLK]
                    product_ref[rest[g], :] = old[g][1] - update[g][:, BLK:]
            return nothing

        lax.fori_loop(0, count // group, step, 0)


def six_rows(pieces, lane):
    high, mid, low = pieces
    none = jnp.zeros_like(high)
    return jnp.concatenate(
        [
            jnp.where(lane < 3 * PANEL, high, none),
            jnp.where(lane < 2 * PANEL, mid, none),
            jnp.where(lane < PANEL, low, none),
        ],
        0,
    )[:, : 3 * PANEL]


def optimise_kernel(slots_ref, rates_ref, *refs, count, adds):
    grads, states = refs[:adds], refs[adds : adds + 7]
    outs = refs[-16:-9]
    in_ref, out_ref, gram_ref, product_ref, inverse_ref, in_sems, out_sem, _ = refs[-8:]
    for item in range(count):
        for index, state in enumerate(states):
            pltpu.make_async_copy(
                state.at[slots_ref[item]], in_ref.at[item, index], in_sems.at[item]
            ).start()

    group = math.gcd(count, 4)

    def update(step, nothing):
        items = [step * group + index for index in range(group)]
        gradients = []
        for item in items:
            pltpu.make_async_copy(in_ref.at[item], in_ref.at[item], in_sems.at[item]).wait()
            grad = grads[0][item].astype(single)
            for other in grads[1:]:
                grad = grad + other[item].astype(single)
            gradients.append(grad.astype(bfloat))
        results = adam_group(
            items, gradients, [[in_ref[item, index] for index in range(7)] for item in items],
            [rates_ref[item] for item in items], gram_ref, product_ref, count,
        )
        for item, values in zip(items, results):
            for index, value in enumerate(values):
                out_ref[item, index] = value
        for item in items:
            for index in range(5):
                pltpu.make_async_copy(
                    out_ref.at[item, index], outs[index].at[slots_ref[item]], out_sem
                ).start()
        return nothing

    lax.fori_loop(0, count // group, update, 0)
    renew(gram_ref, product_ref, inverse_ref, 2 * count)

    def finish(item, nothing):
        for side in range(2):
            base = pl.multiple_of((side * count + item) * BLK, BLK)
            out_ref[item, 5 + side] = product_ref[pl.ds(base, BLK), :].T
            pltpu.make_async_copy(
                out_ref.at[item, 5 + side], outs[5 + side].at[slots_ref[item]], out_sem
            ).start()
        return nothing

    lax.fori_loop(0, count, finish, 0, unroll=math.gcd(count, 4))
    pltpu.make_async_copy(out_ref, out_ref, out_sem).wait()


def optimise(slots, rates, grads, states, earlier=None, after=()):
    count, total = slots.shape[0], states[0].shape[0]
    more = [] if earlier is None else list(earlier)
    skip = 2 + len(grads) + 7
    return pl.pallas_call(
        functools.partial(optimise_kernel, count=count, adds=len(grads)),
        grid_spec=pltpu.PrefetchScalarGridSpec(
            num_scalar_prefetch=2,
            grid=(),
            in_specs=[whole_spec()] * len(grads)
            + [in_hbm()] * (7 + len(more))
            + [anywhere()] * len(after),
            out_specs=[in_hbm()] * 7 + [anywhere()],
            scratch_shapes=[
                pltpu.VMEM((count, 7, BLK, BLK), single),
                pltpu.VMEM((count, 7, BLK, BLK), single),
                pltpu.VMEM((2 * count * BLK, BLK), single),
                pltpu.VMEM((2 * count * BLK, BLK), single),
                pltpu.VMEM((2 * count * PANEL, BLK), single),
                pltpu.SemaphoreType.DMA((count,)),
                pltpu.SemaphoreType.DMA,
                pltpu.SMEM((1,), jnp.int32),
            ],
        ),
        out_shape=[of((total, BLK, BLK), single)] * 7 + [token_of()],
        input_output_aliases={skip + index: index for index in range(7)} if more else {},
        cost_estimate=cost(count * 40 * BLK**3, *grads, *states),
        compiler_params=pltpu.CompilerParams(vmem_limit_bytes=56 * 2**20),
        name="optimise",
    )(slots, rates, *grads, *states, *more, *after)


def whole_spec():
    return pl.BlockSpec(memory_space=pltpu.VMEM)


def fixed(shape):
    return pl.BlockSpec(shape, lambda *_: (0,) * len(shape))


def anywhere():
    return pl.BlockSpec(memory_space=pl.ANY)


def token_of():
    return of((8, 128), single)


def in_hbm():
    return pl.BlockSpec(memory_space=pltpu.HBM)


def cost(flops, *arrays):
    moved = sum(math.prod(a.shape) * jnp.dtype(a.dtype).itemsize for a in arrays)
    return pl.CostEstimate(flops=flops // 16, bytes_accessed=moved // 16, transcendentals=0)


def of(shape, dtype):
    return jax.ShapeDtypeStruct(shape, dtype)


def flip_rows(value):
    return value.astype(single).T.astype(bfloat)


def attend_kernel(q_ref, k_ref, v_ref, valid_ref, w_ref, *refs, heads, own):
    attended_ref, lse_ref, branch_ref, _, flipped_ref, score_ref, prob_ref = refs[-7:]
    keys, width = k_ref.shape
    rows = q_ref.shape[0]
    tile = 128

    flipped_ref[...] = flip_rows(v_ref[...])
    queries = flip_rows(q_ref[...]) * (HEAD_DIM ** (-0.5))
    queries = queries.astype(bfloat)
    head_of = lax.broadcasted_iota(jnp.int32, (width, rows), 0) // HEAD_DIM
    mixed = []
    for head in range(heads):
        score_ref[...] = dot_of(
            k_ref[...], jnp.where(head_of == head, queries, jnp.zeros_like(queries)), 1, 0
        )

        def masked(index):
            here = pl.ds(pl.multiple_of(index * tile, tile), tile)
            valid = valid_ref[here, :]
            valid = jnp.concatenate([valid] * (rows // 128), 1)
            return here, jnp.where(valid > 0.0, score_ref[here, :], masked_score)

        def highest_of(index, best):
            _, value = masked(index)
            return jnp.maximum(best, jnp.max(value.reshape(tile // 8, 8, rows), 0))

        best = lax.fori_loop(
            0, keys // tile, highest_of, jnp.full((8, rows), -jnp.inf, single), unroll=True
        )
        best = jnp.max(best, 0, keepdims=True)

        def weigh(index, total):
            here, value = masked(index)
            value = jnp.exp(value - best)
            prob_ref[here, :] = value.astype(bfloat)
            return total + jnp.sum(value.reshape(tile // 8, 8, rows), 0)

        total = lax.fori_loop(
            0, keys // tile, weigh, jnp.zeros((8, rows), single), unroll=True
        )
        total = jnp.sum(total, 0, keepdims=True)
        out = dot_of(
            flipped_ref[head * HEAD_DIM : (head + 1) * HEAD_DIM, :], prob_ref[...], 1, 0
        )
        mixed.append(out * (1.0 / total))
        lse_ref[head : head + 1, :] = best + jnp.log(total)
    attended = jnp.concatenate(mixed, 0).T.astype(bfloat)
    attended_ref[...] = attended
    branch = dot_of(attended, w_ref[...], 1, 0)
    if own:
        branch = branch + refs[0][...].astype(single)
    branch_ref[...] = branch.astype(bfloat)


def attend(projected, valid, w_out, block, received=None, after=()):
    seq, width = projected.shape[0], w_out.shape[0]
    rows = seq // 4
    heads = width // HEAD_DIM
    own = received is not None
    more = [received] if own else []
    out_shape = [
        of((rows, width), bfloat), of((heads, rows), single), of((rows, D), bfloat), token_of()
    ]
    return pl.pallas_call(
        functools.partial(attend_kernel, heads=heads, own=own),
        grid=(1,),
        in_specs=[
            pl.BlockSpec((rows, width), lambda i: (block, 0)),
            pl.BlockSpec((seq, width), lambda i: (0, 1)),
            pl.BlockSpec((seq, width), lambda i: (0, 2)),
            fixed(valid.shape),
            fixed(w_out.shape),
        ] + [fixed(value.shape) for value in more] + [anywhere()] * len(after),
        out_specs=[fixed(value.shape) for value in out_shape[:-1]] + [anywhere()],
        out_shape=out_shape,
        scratch_shapes=[
            pltpu.VMEM((width, seq), bfloat), pltpu.VMEM((seq, rows), single),
            pltpu.VMEM((seq, rows), bfloat),
        ],
        cost_estimate=cost(2 * 2 * rows * seq * width * heads, projected, *out_shape),
        compiler_params=pltpu.CompilerParams(vmem_limit_bytes=24 * 2**20),
        name="attend",
    )(projected, projected, projected, valid, w_out, *more, *after)


def attend_back_kernel(*refs, heads, first, extra):
    inputs = 11 if first else 13
    refs = refs[:inputs] + refs[inputs + extra :]
    if first:
        (own_ref, peer_ref, w_ref, q_ref, k_ref, v_ref, att_own, att_peer, lse_own, lse_peer,
         valid_ref, dq_ref, dk_ref, dv_ref, _, flipped_ref, grad_ref, score_ref, cross_ref, prob_ref, back_ref,
         att_ref, log_ref, dk_sum, dv_sum) = refs
    else:
        (own_ref, peer_ref, w_ref, q_ref, k_ref, v_ref, att_own, att_peer, lse_own, lse_peer,
         valid_ref, dk_in_ref, dv_in_ref, dq_ref, dk_ref, dv_ref, _, flipped_ref, grad_ref, score_ref,
         cross_ref, prob_ref, back_ref, att_ref, log_ref, dk_sum, dv_sum) = refs
    step = pl.program_id(0)
    keys, width = k_ref.shape
    rows = q_ref.shape[0]
    scale = HEAD_DIM ** (-0.5)
    tile = 128

    @pl.when(step == 0)
    def _():
        flipped_ref[...] = flip_rows(k_ref[...])
        grad_ref[...] = own_ref[...]
        att_ref[...] = att_own[...]
        log_ref[...] = lse_own[...]
        if first:
            dk_sum[...] = jnp.zeros_like(dk_sum)
            dv_sum[...] = jnp.zeros_like(dv_sum)
        else:
            dk_sum[...] = dk_in_ref[...]
            dv_sum[...] = dv_in_ref[...]

    @pl.when(step == 1)
    def _():
        grad_ref[...] = peer_ref[...]
        att_ref[...] = att_peer[...]
        log_ref[...] = lse_peer[...]

    grads = dot_of(grad_ref[...], w_ref[...], 1, 1).astype(bfloat)
    flat = grads.astype(single).T
    cross = flat * att_ref[...].astype(single).T
    grads_t = flat.astype(bfloat)
    queries = q_ref[...]
    queries_t = (flip_rows(queries) * scale).astype(bfloat)
    head_of = lax.broadcasted_iota(jnp.int32, (width, rows), 0) // HEAD_DIM
    none = jnp.zeros_like(grads_t)
    dq = []
    for head in range(heads):
        score_ref[...] = dot_of(k_ref[...], jnp.where(head_of == head, queries_t, none), 1, 0)
        cross_ref[...] = dot_of(v_ref[...], jnp.where(head_of == head, grads_t, none), 1, 0)
        lse = log_ref[head : head + 1, :]
        mean = jnp.sum(cross[head * HEAD_DIM : (head + 1) * HEAD_DIM], 0, keepdims=True)
        at = slice(head * rows, (head + 1) * rows)

        def weigh(index, nothing):
            here = pl.ds(pl.multiple_of(index * tile, tile), tile)
            valid = jnp.concatenate([valid_ref[here, :]] * (rows // 128), 1)
            value = jnp.where(valid > 0.0, score_ref[here, :], masked_score)
            prob = jnp.exp(value - lse)
            prob_ref[here, at] = prob.astype(bfloat)
            back_ref[here, at] = (prob * (cross_ref[here, :] - mean)).astype(bfloat)
            return nothing

        lax.fori_loop(0, keys // tile, weigh, 0, unroll=True)
        dq.append(
            dot_of(flipped_ref[head * HEAD_DIM : (head + 1) * HEAD_DIM, :], back_ref[:, at], 1, 0)
        )
    dq_ref[...] = (jnp.concatenate(dq, 0).T * scale).astype(bfloat)
    lane_head = lax.broadcasted_iota(jnp.int32, (rows, width), 1) // HEAD_DIM
    query_rows = jnp.concatenate(
        [jnp.where(lane_head == head, queries, jnp.zeros_like(queries)) for head in range(heads)], 0
    )
    grad_rows = jnp.concatenate(
        [jnp.where(lane_head == head, grads, jnp.zeros_like(grads)) for head in range(heads)], 0
    )

    def total(index, nothing):
        here = pl.ds(pl.multiple_of(index * 256, 256), 256)
        dk_sum[here, :] = dk_sum[here, :] + dot_of(back_ref[here, :], query_rows, 1, 0) * scale
        dv_sum[here, :] = dv_sum[here, :] + dot_of(prob_ref[here, :], grad_rows, 1, 0)
        return nothing

    lax.fori_loop(0, keys // 256, total, 0, unroll=True)

    @pl.when(step == 1)
    def _():
        dk_ref[...] = dk_sum[...].astype(dk_ref.dtype)
        dv_ref[...] = dv_sum[...].astype(dv_ref.dtype)


def attend_back(own, peer, w_out, projected, attended, lse, valid, part, earlier=None, after=()):
    seq, width = projected.shape[0], w_out.shape[0]
    rows = seq // 4
    heads = width // HEAD_DIM
    first = earlier is None
    kind = single if first else bfloat
    more = [] if first else list(earlier)
    out_shape = [
        of((2 * rows, width), bfloat), of((seq, width), kind), of((seq, width), kind), token_of()
    ]
    return pl.pallas_call(
        functools.partial(attend_back_kernel, heads=heads, first=first, extra=len(after)),
        grid=(2,),
        in_specs=[
            fixed(own.shape), fixed(peer.shape), fixed(w_out.shape),
            pl.BlockSpec((rows, width), lambda i: (2 * part + i, 0)),
            pl.BlockSpec((seq, width), lambda i: (0, 1)),
            pl.BlockSpec((seq, width), lambda i: (0, 2)),
            fixed((rows, width)), fixed((rows, width)), fixed((heads, rows)), fixed((heads, rows)),
            fixed(valid.shape),
        ] + [fixed((seq, width))] * len(more) + [anywhere()] * len(after),
        out_specs=[
            pl.BlockSpec((rows, width), lambda i: (i, 0)),
            fixed((seq, width)), fixed((seq, width)), anywhere(),
        ],
        out_shape=out_shape,
        scratch_shapes=[
            pltpu.VMEM((width, seq), bfloat), pltpu.VMEM((rows, D), bfloat),
            pltpu.VMEM((seq, rows), single), pltpu.VMEM((seq, rows), single),
            pltpu.VMEM((seq, heads * rows), bfloat), pltpu.VMEM((seq, heads * rows), bfloat),
            pltpu.VMEM((rows, width), bfloat), pltpu.VMEM((heads, rows), single),
            pltpu.VMEM((seq, width), single), pltpu.VMEM((seq, width), single),
        ],
        cost_estimate=cost(2 * 2 * rows * seq * width * 5 * heads, projected, *out_shape),
        compiler_params=pltpu.CompilerParams(vmem_limit_bytes=32 * 2**20),
        name="attend_back",
    )(own, peer, w_out, projected, projected, projected, *attended, *lse, valid, *more, *after)


def gelu_pair(value):
    size = jnp.abs(value)
    ratio = 1.0 / (1.0 + (0.3275911 * 0.5**0.5) * size)
    bell = jnp.exp(-0.5 * value * value)
    series = 0.5 * 1.061405429 * ratio + 0.5 * -1.453152027
    series = series * ratio + 0.5 * 1.421413741
    series = series * ratio + 0.5 * -0.284496736
    series = series * ratio + 0.5 * 0.254829592
    tail = series * ratio * bell
    below = jnp.where(value >= 0.0, 1.0 - tail, tail)
    return value * below, below + value * bell * (1.0 / math.sqrt(2.0 * math.pi))


def feed_kernel(rows_ref, up_ref, bias_ref, down_ref, *refs):
    act_ref, slope_ref, out_ref, _, pre_ref, sum_ref = refs[-6:]
    step = pl.program_id(0)
    rows = rows_ref.shape[0]
    tile = 32
    pre_ref[...] = dot_of(rows_ref[...], up_ref[...], 1, 0)

    def activate(index, nothing):
        here = pl.ds(pl.multiple_of(index * tile, tile), tile)
        value, slope = gelu_pair(pre_ref[here, :] + bias_ref[...])
        act_ref[here, :] = value.astype(bfloat)
        slope_ref[here, :] = slope.astype(bfloat)
        return nothing

    lax.fori_loop(0, rows // tile, activate, 0, unroll=4)
    add_up(step, dot_of(act_ref[...], down_ref[...], 1, 0), sum_ref, out_ref)


def add_up(step, more, sum_ref, out_ref):
    last = pl.num_programs(0) - 1

    @pl.when(step == 0)
    def _():
        sum_ref[...] = more

    @pl.when((step > 0) & (step < last))
    def _():
        sum_ref[...] = sum_ref[...] + more

    @pl.when(step == last)
    def _():
        out_ref[...] = (sum_ref[...] + more).astype(out_ref.dtype)


def feed(block, w_up, bias, w_down, kind, after=()):
    rows, hidden = block.shape[0], w_up.shape[1]
    step = 256
    out_shape = [
        of((rows, hidden), bfloat), of((rows, hidden), bfloat), of((rows, D), kind), token_of()
    ]
    return pl.pallas_call(
        feed_kernel,
        grid=(hidden // step,),
        in_specs=[
            fixed(block.shape),
            pl.BlockSpec((D, step), lambda j: (0, j)),
            pl.BlockSpec((1, step), lambda j: (0, j)),
            pl.BlockSpec((step, D), lambda j: (j, 0)),
        ] + [anywhere()] * len(after),
        out_specs=[
            pl.BlockSpec((rows, step), lambda j: (0, j)),
            pl.BlockSpec((rows, step), lambda j: (0, j)),
            fixed((rows, D)), anywhere(),
        ],
        out_shape=out_shape,
        scratch_shapes=[pltpu.VMEM((rows, step), single), pltpu.VMEM((rows, D), single)],
        cost_estimate=cost(4 * rows * D * hidden, w_up, w_down, *out_shape),
        compiler_params=pltpu.CompilerParams(vmem_limit_bytes=20 * 2**20),
        name="feed",
    )(block, w_up, bias, w_down, *after)


def feed_back_kernel(rows_ref, down_ref, up_ref, slope_ref, *refs):
    grad_ref, bias_ref, out_ref, _, sum_ref = refs[-5:]
    grads = dot_of(rows_ref[...], down_ref[...], 1, 1) * slope_ref[...].astype(single)
    grads = grads.astype(bfloat)
    grad_ref[...] = grads
    bias_ref[...] = jnp.sum(grads.astype(single), 0, keepdims=True)
    add_up(pl.program_id(0), dot_of(grads, up_ref[...], 1, 1), sum_ref, out_ref)


def feed_back(block, w_down, w_up, slope, kind, after=()):
    rows, hidden = block.shape[0], w_up.shape[1]
    step = 256
    out_shape = [
        of((rows, hidden), bfloat), of((1, hidden), single), of((rows, D), kind), token_of()
    ]
    return pl.pallas_call(
        feed_back_kernel,
        grid=(hidden // step,),
        in_specs=[
            fixed(block.shape),
            pl.BlockSpec((step, D), lambda j: (j, 0)),
            pl.BlockSpec((D, step), lambda j: (0, j)),
            pl.BlockSpec((rows, step), lambda j: (0, j)),
        ] + [anywhere()] * len(after),
        out_specs=[
            pl.BlockSpec((rows, step), lambda j: (0, j)),
            pl.BlockSpec((1, step), lambda j: (0, j)),
            fixed((rows, D)), anywhere(),
        ],
        out_shape=out_shape,
        scratch_shapes=[pltpu.VMEM((rows, D), single)],
        cost_estimate=cost(4 * rows * D * hidden, w_up, w_down, *out_shape),
        compiler_params=pltpu.CompilerParams(vmem_limit_bytes=20 * 2**20),
        name="feed_back",
    )(block, w_down, w_up, slope, *after)


def chip_kernel(keep_ref, got_ref, *refs):
    refs[-2][...] = (keep_ref[...] + got_ref[...].astype(single)).astype(bfloat)


def standardise(value):
    centred = value - jnp.mean(value, -1, keepdims=True)
    inv_std = lax.rsqrt(jnp.mean(centred * centred, -1, keepdims=True) + norm_eps)
    return centred * inv_std, inv_std


def through_norm(grads, normed, inv_std, gain):
    scaled = grads * gain
    mean_grad = jnp.mean(scaled, -1, keepdims=True)
    mean_cross = jnp.mean(scaled * normed, -1, keepdims=True)
    return inv_std * (scaled - mean_grad - normed * mean_cross)


def gain_sums(grads, normed, rounded):
    total = lambda value: jnp.sum(value, 0, keepdims=True)
    blank = jnp.zeros((5, grads.shape[1]), single)
    return jnp.concatenate(
        [total(grads * normed), total(grads), total(rounded.astype(single)), blank], 0
    )


norm_tile = 64


def norm_one_kernel(chip_ref, across_ref, rows_ref, vectors_ref, *refs):
    normed_ref, inv_ref, hidden_ref = refs[-4:-1]
    branch = chip_ref[...].astype(single) + across_ref[...].astype(single)
    normed, inv_std = standardise(rows_ref[...].astype(single) + (branch + vectors_ref[2:3, :]))
    normed_ref[...] = normed
    inv_ref[...] = jnp.broadcast_to(inv_std, inv_ref.shape)
    hidden_ref[...] = (normed * vectors_ref[0:1, :] + vectors_ref[1:2, :]).astype(bfloat)


def norm_two_kernel(
    chip_ref, across_ref, normed_ref, cot_ref, valid_ref, one_ref, two_ref, *refs
):
    out_ref, grad_ref, low_ref, sums_ref = refs[-5:-1]

    @pl.when(pl.program_id(0) == 0)
    def _():
        sums_ref[...] = jnp.zeros_like(sums_ref)

    hidden = normed_ref[...] * one_ref[0:1, :] + one_ref[1:2, :]
    down = chip_ref[...].astype(single) + across_ref[...].astype(single)
    normed, inv_std = standardise(hidden + (down + two_ref[2:3, :]))
    gain = two_ref[0:1, :]
    out_ref[...] = (normed * gain + two_ref[1:2, :]).astype(bfloat)
    grads = cot_ref[...].astype(single) * valid_ref[:, 0:1]
    back = through_norm(grads, normed, inv_std, gain)
    grad_ref[...] = back
    low = back.astype(bfloat)
    low_ref[...] = low
    sums_ref[...] += gain_sums(grads, normed, low)


def norm_back_kernel(
    chip_ref, across_ref, second_ref, normed_ref, inv_ref, one_ref, *refs
):
    grad_ref, low_ref, sums_ref = refs[-4:-1]

    @pl.when(pl.program_id(0) == 0)
    def _():
        sums_ref[...] = jnp.zeros_like(sums_ref)

    grads = chip_ref[...].astype(single) + across_ref[...].astype(single) + second_ref[...]
    normed = normed_ref[...]
    back = through_norm(grads, normed, inv_ref[:, 0:1], one_ref[0:1, :])
    grad_ref[...] = back
    low = back.astype(bfloat)
    low_ref[...] = low
    sums_ref[...] += gain_sums(grads, normed, low)


def norm_call(kernel, name, rowed, fixed_in, row_outs, sums, after=()):
    rows = rowed[0].shape[0]
    by_row = lambda width: pl.BlockSpec((norm_tile, width), lambda i: (i, 0))
    out_shape = [of((rows, width), kind) for width, kind in row_outs]
    out_specs = [by_row(width) for width, _ in row_outs]
    if sums:
        out_shape.append(of((8, D), single))
        out_specs.append(fixed((8, D)))
    out_shape.append(token_of())
    out_specs.append(anywhere())
    return pl.pallas_call(
        kernel,
        grid=(rows // norm_tile,),
        in_specs=[by_row(value.shape[1]) for value in rowed]
        + [fixed(value.shape) for value in fixed_in]
        + [anywhere()] * len(after),
        out_specs=out_specs,
        out_shape=out_shape,
        cost_estimate=cost(20 * rows * D, *rowed, *out_shape),
        compiler_params=pltpu.CompilerParams(vmem_limit_bytes=16 * 2**20),
        name=name,
    )(*rowed, *fixed_in, *after)


def token_back_kernel(*refs):
    dq_refs, (dk_ref, dv_ref, w_ref), outs = refs[:2], refs[2:5], refs[-5:-1]
    width = dk_ref.shape[1]
    rows = dk_ref.shape[0] // 4
    for block in range(4):
        here = slice(block * rows, (block + 1) * rows)
        parts = [
            dq_refs[block // 2][block % 2 * rows : (block % 2 + 1) * rows, :],
            dk_ref[here, :], dv_ref[here, :],
        ]
        value = dot_of(jnp.concatenate(parts, 1), w_ref[...], 1, 1)
        outs[block][...] = value.astype(outs[block].dtype)


def token_back(dq_a, dq_b, dk, dv, w_qkv, after=()):
    rows = dk.shape[0] // 4
    out_shape = [of((rows, D), kind) for kind in (single, bfloat, single, bfloat)] + [token_of()]
    return pl.pallas_call(
        token_back_kernel,
        in_specs=[whole_spec()] * 5 + [anywhere()] * len(after),
        out_specs=[whole_spec()] * 4 + [anywhere()],
        out_shape=out_shape,
        cost_estimate=cost(8 * rows * D * w_qkv.shape[1], w_qkv, dk, *out_shape),
        compiler_params=pltpu.CompilerParams(vmem_limit_bytes=24 * 2**20),
        name="token_back",
    )(dq_a, dq_b, dk, dv, w_qkv, *after)


def pack_kernel(target_ref, *refs, jobs, scale, regions, count, resumed):
    outs = refs[-4 - len(regions) : -4]
    held_ref, sem, in_sem = refs[-3:]
    if resumed:
        start = pltpu.make_async_copy(refs[count], held_ref, in_sem)
        start.start()
    waited = not resumed
    for lefts, rights, layout, rows, cols in jobs:
        right = jnp.concatenate([refs[index][...] for index in rights], 0)
        for row in range(0, rows, 2):
            span = min(2, rows - row)
            left = jnp.concatenate(
                [refs[index][:, row * BLK : (row + span) * BLK] for index in lefts], 0
            )
            weights = (dot_of(left, right, 0, 0) * scale).astype(bfloat)
            if not waited:
                start.wait()
                waited = True
            for i in range(span):
                for col in range(cols):
                    held_ref[target_ref[layout(row + i, col)]] = weights[
                        i * BLK : (i + 1) * BLK, col * BLK : (col + 1) * BLK
                    ]
    copies = [
        pltpu.make_async_copy(held_ref.at[first : first + size], out, sem.at[index])
        for index, ((first, size), out) in enumerate(zip(regions, outs))
    ]
    for copy in copies:
        copy.start()
    for copy in copies:
        copy.wait()


def pack(target, pairs, scale, regions, earlier=None, after=()):
    operands, jobs, blocks, flops = [], [], 0, 0
    total = target.shape[0]

    def places(arrays):
        found = []
        for value in arrays:
            if not any(value is other for other in operands):
                operands.append(value)
            found.append([value is other for other in operands].index(True))
        return found

    for lefts, rights, layout in pairs:
        rows, cols = lefts[0].shape[1] // BLK, rights[0].shape[1] // BLK
        jobs.append((places(lefts), places(rights), layout, rows, cols))
        blocks += rows * cols
        flops += 2 * rows * cols * BLK * BLK * sum(value.shape[0] for value in lefts)
    more = [] if earlier is None else [earlier]
    return pl.pallas_call(
        functools.partial(
            pack_kernel, jobs=jobs, scale=scale, regions=regions, count=len(operands),
            resumed=bool(more),
        ),
        grid_spec=pltpu.PrefetchScalarGridSpec(
            num_scalar_prefetch=1,
            grid=(),
            in_specs=[whole_spec()] * len(operands)
            + [in_hbm()] * len(more)
            + [anywhere()] * len(after),
            out_specs=[in_hbm()] * len(regions) + [anywhere()],
            scratch_shapes=[
                pltpu.VMEM((total, BLK, BLK), bfloat),
                pltpu.SemaphoreType.DMA((len(regions),)),
                pltpu.SemaphoreType.DMA,
            ],
        ),
        out_shape=[of((size, BLK, BLK), bfloat) for _, size in regions] + [token_of()],
        cost_estimate=cost(flops, *operands, of((blocks, BLK, BLK), bfloat)),
        compiler_params=pltpu.CompilerParams(vmem_limit_bytes=40 * 2**20),
        name="pack",
    )(target, *operands, *more, *after)


def join_kernel(*refs, groups):
    out_ref = refs[-2]
    at = 0
    for index, terms in enumerate(groups):
        total = 0.0
        for ref in refs[at : at + terms]:
            value = ref[...].reshape(-1, BLK, BLK)
            total = total + value.astype(single)
        at += terms
        size = total.shape[0]
        out_ref[index * size : (index + 1) * size] = total.astype(bfloat)


def join(hop, groups, after=()):
    operands, specs = [], []
    for keep, got, *carried in groups:
        slots = keep.shape[0] // (lax.axis_size("dp") // 2)
        block = pl.BlockSpec((slots, BLK, BLK), lambda i: (hop, 0, 0))
        operands += [keep, got, *carried]
        specs += [block] + [fixed((slots, BLK, BLK))] * (1 + len(carried))
    out = of((slots * len(groups), BLK, BLK), bfloat)
    return pl.pallas_call(
        functools.partial(join_kernel, groups=[len(group) for group in groups]),
        grid=(1,),
        in_specs=specs + [anywhere()] * len(after),
        out_specs=[fixed(out.shape), anywhere()],
        out_shape=[out, token_of()],
        cost_estimate=cost(1, out),
        name="join",
    )(*operands, *after)


def block_counts(tensors):
    return (D * D // (tensors * BLK * BLK), D * FF // (tensors * BLK * BLK))


def rate_values(canon_index, tensors, seq_len):
    attn_count, ffn_count = block_counts(tensors)
    out_std = math.sqrt(seq_len / (3.0 * D))
    inner = jnp.where(canon_index < 4 * attn_count + ffn_count, D ** (-0.5), FF ** (-0.5))
    inner = jnp.where(canon_index < 4 * attn_count, out_std, inner)
    return jnp.where(canon_index < 3 * attn_count, D ** (-0.5), inner).astype(single)


def swap(value, axis, bit):
    count = lax.axis_size(axis)
    return lax.ppermute(value, axis, [(i, i ^ bit) for i in range(count)])


def ring(value):
    count = lax.axis_size("dp")
    return lax.ppermute(value, "dp", [(i, (i + 2) % count) for i in range(count)])


def gather_slots(local, parts):
    size = local.shape[0] // parts
    hops = lax.axis_size("dp") // 2
    pieces = [[[None] * parts for _ in range(2)] for _ in range(hops)]
    for part in range(parts):
        shard = local[part * size : (part + 1) * size] if parts > 1 else local
        for hop in range(hops):
            pieces[hop][0][part] = shard
            pieces[hop][1][part] = swap(shard, "dp", 1)
            if hop < hops - 1:
                shard = ring(shard)
    return [piece for pair in pieces for flip in pair for piece in flip]


def vector_kernel(rank_ref, one_ref, two_ref, up_a, up_b, up_c, up_d, dq_a, dq_b, dv_ref, *refs):
    out_ref = refs[-2]
    rank = rank_ref[0]
    out_ref[...] = jnp.zeros_like(out_ref)
    out_ref[0:2, :] = one_ref[0:2, :]
    out_ref[2:4, :] = two_ref[0:2, :]
    out_ref[6:7, :] = one_ref[2:3, :]
    out_ref[11:12, :] = two_ref[2:3, :]
    width = dv_ref.shape[1]
    query = jnp.sum(dq_a[...].astype(single), 0, keepdims=True) + jnp.sum(
        dq_b[...].astype(single), 0, keepdims=True
    )
    value = jnp.sum(dv_ref[...].astype(single), 0, keepdims=True)
    place = lax.broadcasted_iota(jnp.int32, (1, D), 1) // width == rank
    for row, total in ((4, query), (5, value)):
        wide = jnp.concatenate([total] * (D // width), 1)
        out_ref[row : row + 1, :] = jnp.where(place, wide, 0.0)
    bias = up_a[...] + up_b[...] + up_c[...] + up_d[...]
    size = bias.shape[1]
    for row in range(FF // D):
        for part in range(D // size if size < D else 1):
            here = (row * D + part * size) // size == rank
            out_ref[7 + row : 8 + row, part * size : (part + 1) * size] = jnp.where(here, bias, 0.0)


def vector_rows(rank, sums_one, sums_two, bias_parts, dq_a, dq_b, grad_value, after):
    operands = [sums_one, sums_two, *bias_parts, dq_a, dq_b, grad_value]
    return pl.pallas_call(
        vector_kernel,
        grid_spec=pltpu.PrefetchScalarGridSpec(
            num_scalar_prefetch=1,
            grid=(),
            in_specs=[whole_spec()] * len(operands) + [anywhere()] * len(after),
            out_specs=[whole_spec(), anywhere()],
        ),
        out_shape=[of((16, D), single), token_of()],
        cost_estimate=cost(1, *operands),
        name="vector_rows",
    )(rank, *operands, *after)


def hop_sum(value, axis, bit):
    return value + swap(value, axis, bit)


def assemble_kernel(source_ref, *refs, sizes, layouts):
    count = len(sizes)
    pieces, outs, (held, sems) = refs[:count], refs[-2 - len(set(job[0] for job in layouts)) : -2], refs[-2:]
    copies, start = [], 0
    for index, size in enumerate(sizes):
        copies.append(pltpu.make_async_copy(pieces[index], held.at[start : start + size], sems.at[index]))
        start += size
    for copy in copies:
        copy.start()
    for copy in copies:
        copy.wait()
    canon = 0
    for target, rows, cols, row_at, col_at in layouts:
        for row in range(rows):
            for col in range(cols):
                outs[target][
                    (row_at + row) * BLK : (row_at + row + 1) * BLK,
                    (col_at + col) * BLK : (col_at + col + 1) * BLK,
                ] = held[source_ref[canon]]
                canon += 1


def assemble(source, pieces, shapes, layouts, after=()):
    sizes = [piece.shape[0] for piece in pieces]
    return pl.pallas_call(
        functools.partial(assemble_kernel, sizes=sizes, layouts=layouts),
        grid_spec=pltpu.PrefetchScalarGridSpec(
            num_scalar_prefetch=1,
            grid=(1,),
            in_specs=[in_hbm()] * len(pieces) + [anywhere()] * len(after),
            out_specs=[pl.BlockSpec(shape, lambda i, *_: (0, 0)) for shape in shapes],
            scratch_shapes=[
                pltpu.VMEM((sum(sizes), BLK, BLK), bfloat),
                pltpu.SemaphoreType.DMA((len(sizes),)),
            ],
        ),
        out_shape=[jax.ShapeDtypeStruct(shape, bfloat) for shape in shapes],
        compiler_params=pltpu.CompilerParams(vmem_limit_bytes=40 * 2**20),
        name="assemble",
    )(source, *pieces, *after)


def chip_sum(keep, send, after=()):
    return norm_call(
        chip_kernel, "chip_sum", [keep, peer_of(send)], [], [(D, bfloat)], False, after
    )


def across(value):
    return swap(value, "tensor", 2)


def peer_of(value):
    return swap(value, "tensor", 1)


def body(
    tokens,
    cotangent,
    seq_lengths,
    block_owner,
    master_blocks,
    first_moment,
    second_moment,
    left_stats,
    right_stats,
    left_basis,
    right_basis,
    vector_master,
    vector_first,
    vector_second,
):
    tensors = lax.axis_size("tensor")
    data_ranks = lax.axis_size("dp")
    tensor_rank = lax.axis_index("tensor")
    data_rank = lax.axis_index("dp")
    local_rows = tokens.shape[0]
    seq_len = local_rows * tensors
    slice_width = D // tensors
    hidden_width = FF // tensors
    block_total = block_owner.shape[0]
    slots_here = master_blocks.shape[1]
    length = seq_lengths[0]
    attn_count, ffn_count = block_counts(tensors)
    permuted = data_ranks <= 16
    hops = data_ranks // 2
    canon_ids = jnp.arange(block_total, dtype=jnp.int32)
    holder, slot = block_owner // slots_here, block_owner % slots_here
    source = target = block_owner
    if permuted:
        flip = (holder % 2) ^ (data_rank % 2)
        down = (data_rank // 2 - holder // 2) % hops
        up = (holder // 2 - data_rank // 2) % hops
        source = (down * 2 + flip) * slots_here + slot
        target = (flip * hops + up) * slots_here + slot
    mine = block_owner[None, :] == data_rank * slots_here + jnp.arange(slots_here)[:, None]
    own_canon = jnp.sum(jnp.where(mine, canon_ids[None, :], 0), 1)
    own_slots = jnp.arange(slots_here, dtype=jnp.int32)

    cols = slice_width // BLK
    wide = hidden_width // BLK
    full = D // BLK
    local_weights = master_blocks[0].astype(bfloat)
    if permuted:
        pieces = gather_slots(local_weights, 3)
    else:
        pieces = [lax.all_gather(local_weights, "dp", axis=0, tiled=True)]
    w_qkv, w_out, w_up, w_down = assemble(
        source,
        pieces,
        [(D, 3 * slice_width), (slice_width, D), (D, hidden_width), (hidden_width, D)],
        [
            (0, full, cols, 0, 0),
            (0, full, cols, 0, cols),
            (0, full, cols, 0, 2 * cols),
            (1, cols, full, 0, 0),
            (2, full, wide, 0, 0),
            (3, wide, full, 0, 0),
        ],
    )
    gain_one, shift_one = (vector_master[0:D], vector_master[D : 2 * D])
    gain_two, shift_two = (vector_master[2 * D : 3 * D], vector_master[3 * D : 4 * D])
    bias_query = lax.dynamic_slice_in_dim(
        vector_master, 4 * D + tensor_rank * slice_width, slice_width
    )
    bias_value = lax.dynamic_slice_in_dim(
        vector_master, 5 * D + tensor_rank * slice_width, slice_width
    )
    bias_out = vector_master[6 * D : 7 * D]
    bias_up = lax.dynamic_slice_in_dim(
        vector_master, 7 * D + tensor_rank * hidden_width, hidden_width
    )
    bias_down = vector_master[7 * D + FF : 8 * D + FF]

    tokens_b = swap(tokens, "tensor", 2)
    cotangent_b = swap(cotangent, "tensor", 2)
    full_tokens = jnp.concatenate(
        [tokens, peer_of(tokens), tokens_b, peer_of(tokens_b)], axis=0
    )
    quarters = tensor_rank ^ jnp.arange(4, dtype=jnp.int32)
    positions = (quarters[:, None] * local_rows + jnp.arange(local_rows)[None, :]).reshape(-1)
    key_valid = positions < length
    row_valid = key_valid.astype(single)[:, None]
    chunk = 2 * local_rows

    bias_qkv = jnp.concatenate([bias_query, jnp.zeros((slice_width,), single), bias_value])
    projected = (jnp.dot(full_tokens, w_qkv, preferred_element_type=single) + bias_qkv).astype(
        bfloat
    )
    one = jnp.stack([gain_one, shift_one, bias_out])
    two = jnp.stack([gain_two, shift_two, bias_down])
    valid = jnp.broadcast_to(row_valid, (seq_len, 128))
    grad_scale = 1.0 / math.sqrt(seq_len * data_ranks)
    up_start = 4 * attn_count

    attended, lse, shares = [None] * 4, [None] * 4, [None] * 4
    attended[3], lse[3], shares[3], token = attend(
        projected, valid, w_out, 3, after=[cotangent_b]
    )
    attended[1], lse[1], shares[1], token = attend(projected, valid, w_out, 1, after=[token])
    for block in (2, 0):
        attended[block], lse[block], shares[block], token = attend(
            projected, valid, w_out, block, peer_of(shares[block + 1]),
            after=[token],
        )
    chip = [shares[0], shares[2]]
    other = [across(chip[1]), across(chip[0])]

    normed_one, inv_one = [None] * 2, [None] * 2
    hidden, activation, slope, chip_two = [None] * 4, [None] * 4, [None] * 4, [None] * 2
    bias_row = bias_up[None, :]

    def norm_up(part, after):
        normed_one[part], inv_one[part], hidden[2 * part], token = norm_call(
            norm_one_kernel, "norm_one", [chip[part], other[part], (tokens, tokens_b)[part]],
            [one], [(D, single), (128, single), (D, bfloat)], False, after,
        )
        hidden[2 * part + 1] = peer_of(hidden[2 * part])
        return token

    def feed_part(part, token):
        block = 2 * part
        activation[block], slope[block], keep, token = feed(
            hidden[block], w_up, bias_row, w_down, single, [token]
        )
        block += 1
        activation[block], slope[block], send, token = feed(
            hidden[block], w_up, bias_row, w_down, bfloat, [token]
        )
        return keep, send, token

    token = norm_up(0, [token])
    *sums, token = feed_part(0, token)
    token = norm_up(1, [token])
    chip_two[0], token = chip_sum(*sums, [token])
    other = [None, across(chip_two[0])]
    *sums, token = feed_part(1, token)
    chip_two[1], token = chip_sum(*sums, [token])
    other[0] = across(chip_two[1])

    grad_second, grad_down, grad_up = [None] * 2, [None] * 4, [None] * 4
    bias_parts, chip_three, outs, sums_two = [None] * 4, [None] * 2, [None] * 2, [None] * 2

    def norm_down(part, token):
        rows_valid = valid[part * chunk : part * chunk + local_rows]
        outs[part], grad_second[part], grad_down[2 * part], sums_two[part], token = norm_call(
            norm_two_kernel, "norm_two",
            [chip_two[part], other[part], normed_one[part], (cotangent, cotangent_b)[part],
             rows_valid],
            [one, two], [(D, bfloat), (D, single), (D, bfloat)], True, [token],
        )
        grad_down[2 * part + 1] = peer_of(grad_down[2 * part])
        return token

    def feed_back_part(part, token):
        block = 2 * part
        grad_up[block], bias_parts[block], keep, token = feed_back(
            grad_down[block], w_down, w_up, slope[block], single, [token]
        )
        block += 1
        grad_up[block], bias_parts[block], send, token = feed_back(
            grad_down[block], w_down, w_up, slope[block], bfloat, [token]
        )
        return keep, send, token

    token = norm_down(1, token)
    *sums, token = feed_back_part(1, token)
    token = norm_down(0, token)
    chip_three[1], token = chip_sum(*sums, [token])
    other = [across(chip_three[1]), None]
    *sums, token = feed_back_part(0, token)
    chip_three[0], token = chip_sum(*sums, [token])
    other[1] = across(chip_three[0])
    layer_output = outs[0]
    *sent, token = pack(
        target,
        [
            (hidden, grad_up, lambda row, col: up_start + row * wide + col),
            (activation, grad_down, lambda row, col: up_start + ffn_count + row * full + col),
        ],
        grad_scale,
        [(0, block_total)],
        after=[token],
    )

    grad_branch, grad_query, back, grad_rows, sums_one = [None] * 4, [None] * 2, None, [0, 0], [0, 0]
    for part in (0, 1):
        block = 2 * part
        grad_rows[part], grad_branch[block], sums_one[part], token = norm_call(
            norm_back_kernel, "norm_back",
            [chip_three[part], other[part], grad_second[part], normed_one[part], inv_one[part]],
            [one], [(D, single), (D, bfloat)], True, [token],
        )
        grad_branch[block + 1] = peer_of(grad_branch[block])
        grad_query[part], *back, token = attend_back(
            grad_branch[block], grad_branch[block + 1], w_out, projected,
            attended[block : block + 2], lse[block : block + 2], valid, part, back, [token],
        )
    grad_summed, sums_one = grad_rows[0], sums_one[0]
    grad_key, grad_value = back
    moved = hops * slots_here
    regions = [(0, block_total)]
    if permuted:
        regions = [(0, moved)] + [
            (moved + hop * slots_here, slots_here) for hop in range(hops)
        ]
    kept, *leaving, token = pack(
        target,
        [
            ([full_tokens], grad_query, lambda row, col: row * cols + col),
            ([full_tokens], [grad_key], lambda row, col: attn_count + row * cols + col),
            ([full_tokens], [grad_value], lambda row, col: 2 * attn_count + row * cols + col),
            (attended, grad_branch, lambda row, col: 3 * attn_count + row * full + col),
        ],
        grad_scale,
        regions,
        sent[0],
        [token],
    )
    vector_grad, token = vector_rows(
        tensor_rank.astype(jnp.int32)[None], sums_one, sums_two[0], bias_parts, *grad_query,
        grad_value, [token],
    )
    vector_grad = hop_sum(vector_grad, "tensor", 1)
    keep_a, send_a, keep_b, send_b, token = token_back(
        grad_query[0], grad_query[1], grad_key, grad_value, w_qkv, [token]
    )
    vector_grad = hop_sum(vector_grad, "tensor", 2)
    chip_b = chip_sum(keep_b, send_b, [token])[0]
    chip_a = chip_sum(keep_a, send_a, [token])[0]
    over = across(chip_b)
    token_grad = (chip_a.astype(single) + over.astype(single) + grad_summed).astype(bfloat)
    bits = []
    bit = 1
    while bit < data_ranks:
        bits.append(bit)
        bit *= 2
    bits = bits[1:] + bits[:1]
    if permuted:
        carried, after = [], [token]
        for bit in bits[:-1]:
            vector_grad = hop_sum(vector_grad, "dp", bit)
            after.append(vector_grad)
        bits = bits[-1:]
        for hop in range(hops - 1, -1, -1):
            got = swap(leaving[hop], "dp", 1)
            own_grad, token = join(hop, [[kept, got] + carried], after)
            carried, after = [ring(own_grad)] if hop else [], [token]
    else:
        own_grad = lax.psum_scatter(kept, "dp", scatter_dimension=0, tiled=True)
    for bit in bits:
        vector_grad = hop_sum(vector_grad, "dp", bit)
    vector_sum = vector_grad[: 8 + FF // D].reshape(-1) * grad_scale
    rates = rate_values(own_canon, tensors, seq_len)
    correction = 1.0 - moment_decay**STEP
    states = [
        first_moment[0], second_moment[0], master_blocks[0], left_stats[0], right_stats[0],
        left_basis[0], right_basis[0],
    ]
    *fresh, _ = optimise(own_slots, rates, [own_grad], states)
    fresh_first, fresh_second, fresh_master, fresh_left, fresh_right, basis_left, basis_right = fresh
    vec_first = moment_decay * vector_first + (1.0 - moment_decay) * vector_sum
    vec_second = moment_decay * vector_second + (1.0 - moment_decay) * vector_sum * vector_sum
    vec_master = vector_master - vector_rate * (vec_first / correction) / (
        jnp.sqrt(vec_second / correction) + adam_eps
    )
    return (
        layer_output,
        token_grad,
        fresh_first[None],
        fresh_second[None],
        fresh_master[None],
        fresh_left[None],
        fresh_right[None],
        basis_left[None],
        basis_right[None],
        vec_first,
        vec_second,
        vec_master,
    )


def solution(mesh):
    return jax.shard_map(
        body,
        mesh=mesh,
        in_specs=(
            P(("dp", "tensor"), None),
            P(("dp", "tensor"), None),
            P("dp"),
            P(),
            P("tensor", "dp", None, None),
            P("tensor", "dp", None, None),
            P("tensor", "dp", None, None),
            P("tensor", "dp", None, None),
            P("tensor", "dp", None, None),
            P("tensor", "dp", None, None),
            P("tensor", "dp", None, None),
            P(),
            P(),
            P(),
        ),
        out_specs=(
            P(("dp", "tensor"), None),
            P(("dp", "tensor"), None),
            P("tensor", "dp", None, None),
            P("tensor", "dp", None, None),
            P("tensor", "dp", None, None),
            P("tensor", "dp", None, None),
            P("tensor", "dp", None, None),
            P("tensor", "dp", None, None),
            P("tensor", "dp", None, None),
            P(),
            P(),
            P(),
        ),
        check_vma=False,
    )
```

```python
import functools
import math

import jax
import jax.numpy as jnp
from jax import lax
from jax.experimental import pallas as pl
from jax.experimental.pallas import tpu as pltpu
from jax.sharding import PartitionSpec as P

D = 1024
FF = 4096
HEAD_DIM = 64
BLK = 128
STEP = 10


norm_eps = 1e-05
adam_eps = 1e-08
moment_decay = 0.5
weight_decay = 0.01
vector_rate = 0.25
masked_score = -1000000000.0
bfloat = jnp.bfloat16
single = jnp.float32


PANEL = 32


def dot_of(left, right, left_dim, right_dim):
    return lax.dot_general(
        left, right, (((left_dim,), (right_dim,)), ((), ())), preferred_element_type=single
    )


def split_two(value):
    high = value.astype(bfloat)
    return high, (value - high.astype(single)).astype(bfloat)


def split_three(value):
    high = value.astype(bfloat)
    rest = value - high.astype(single)
    mid = rest.astype(bfloat)
    return high, mid, (rest - mid.astype(single)).astype(bfloat)


def dot_three(left, right, left_dim, right_dim):
    stacked_left = jnp.concatenate([left[0], left[0], left[1]], axis=left_dim)
    stacked_right = jnp.concatenate([right[0], right[1], right[0]], axis=right_dim)
    return dot_of(stacked_left, stacked_right, left_dim, right_dim)


def dot_two(pair, other, pair_dim, other_dim, swapped=False):
    stacked = jnp.concatenate(pair, axis=pair_dim)
    twice = jnp.concatenate([other, other], axis=other_dim)
    if swapped:
        return dot_of(twice, stacked, other_dim, pair_dim)
    return dot_of(stacked, twice, pair_dim, other_dim)


def gram_six(pieces):
    high, mid, low = pieces
    left = jnp.concatenate([high, high, high, mid, mid, low], axis=1)
    right = jnp.concatenate([high, mid, low, high, mid, high], axis=1)
    return dot_of(left, right, 1, 1)


def adam_group(items, grads, states, rates, gram_ref, product_ref, count):
    correction = 1.0 - moment_decay**STEP
    scale = (1.0 - moment_decay) / BLK
    first, second, master, left_stat, right_stat, left, right = zip(*states)
    left_t = [split_two(value.T) for value in left]
    right_t = [split_two(value.T) for value in right]
    left = [split_two(value) for value in left]
    right = [split_two(value) for value in right]
    half = [dot_two(r, g, 0, 1, True).astype(bfloat) for r, g in zip(right, grads)]
    new_left = [
        moment_decay * old + scale * dot_of(g, g, 1, 1) for old, g in zip(left_stat, grads)
    ]
    new_right = [
        moment_decay * old + scale * dot_of(g, g, 0, 0) for old, g in zip(right_stat, grads)
    ]
    rotated = [dot_two(t, value, 1, 0) for t, value in zip(left_t, half)]
    sides = []
    for stats, basis in ((new_left, left_t), (new_right, right_t)):
        sides.append([dot_three(b, split_two(value), 1, 0) for b, value in zip(basis, stats)])
    new_first = [moment_decay * old + (1.0 - moment_decay) * r for old, r in zip(first, rotated)]
    new_second = [
        moment_decay * old + (1.0 - moment_decay) * r * r for old, r in zip(second, rotated)
    ]
    direction = [
        ((m / correction) / (jnp.sqrt(v / correction) + adam_eps)).astype(bfloat)
        for m, v in zip(new_first, new_second)
    ]
    half = [
        dot_two(t, value, 0, 1, True).astype(bfloat) for t, value in zip(right_t, direction)
    ]
    grams = [[gram_six(split_three(value)) for value in side] for side in sides]
    turned = [dot_two(b, value, 1, 0) for b, value in zip(left, half)]
    new_master = [
        old - rate * (value + weight_decay * old)
        for old, rate, value in zip(master, rates, turned)
    ]
    for side in range(2):
        for item, product, gram in zip(items, sides[side], grams[side]):
            here = pl.ds(pl.multiple_of((side * count + item) * BLK, BLK), BLK)
            product_ref[here, :] = product
            gram_ref[here, :] = gram
    return list(zip(new_first, new_second, new_master, new_left, new_right))


def factor_panel(rows):
    pieces = PANEL // 8
    batch = rows[0].shape[1]
    work = [
        [rows[j][8 * i : 8 * i + 8] if i >= j // 8 else None for i in range(pieces)]
        for j in range(PANEL)
    ]
    sublane = lax.broadcasted_iota(jnp.int32, (8, batch), 0)
    zero = jnp.zeros((8, batch), single)
    inverse = [[None] * pieces for _ in range(PANEL)]
    for k in range(PANEL):
        group, lane = divmod(k, 8)
        pivot = work[k][group][lane : lane + 1]
        root = lax.rsqrt(pivot)
        root = root * (1.5 - 0.5 * pivot * root * root)
        root = jnp.broadcast_to(root, (8, batch))
        column = [work[k][i] * root if i >= group else None for i in range(pieces)]
        done = []
        for i in range(group + 1):
            value = inverse[k][i]
            value = zero if value is None else value * root
            done.append(jnp.where(sublane == lane, root, value) if i == group else value)
        inverse[k] = done + [zero] * (pieces - group - 1)
        for j in range(k + 1, PANEL):
            row_group, row_lane = divmod(j, 8)
            factor = jnp.broadcast_to(column[row_group][row_lane : row_lane + 1], (8, batch))
            for i in range(row_group, pieces):
                work[j][i] = work[j][i] - factor * column[i]
            for i in range(group + 1):
                term = factor * done[i]
                inverse[j][i] = -term if inverse[j][i] is None else inverse[j][i] - term
    return inverse


def renew(gram_ref, product_ref, inverse_ref, count):
    group = math.gcd(count, 16)
    lane = lax.broadcasted_iota(jnp.int32, (PANEL, BLK), 1)
    for panel in range(BLK // PANEL):
        top = panel * PANEL
        last = panel == BLK // PANEL - 1
        rows = []
        for j in range(PANEL):
            row = gram_ref[pl.ds(top + j, count, stride=BLK), :]
            rows.append(row.T[top : top + PANEL])
        inverse = factor_panel(rows)
        for i in range(PANEL):
            row = jnp.concatenate(inverse[i], 0)
            inverse_ref[pl.ds(i, count, stride=PANEL), :] = jnp.concatenate([row] * 4, 0).T

        def step(index, nothing):
            bases = [pl.multiple_of((index * group + g) * BLK, BLK) for g in range(group)]
            lefts, wholes = [], []
            for g in range(group):
                here = pl.ds(pl.multiple_of((index * group + g) * PANEL, PANEL), PANEL)
                lefts.append(inverse_ref[here, :])
                rows_at = pl.ds(bases[g] + top, PANEL)
                whole = product_ref[rows_at, :]
                if not last:
                    whole = jnp.concatenate([gram_ref[rows_at, :], whole], 1)
                wholes.append(whole)
            rest = [pl.ds(base + top + PANEL, BLK - top - PANEL) for base in bases]
            if not last:
                old = [(gram_ref[at, :], product_ref[at, :]) for at in rest]
            lefts = [six_rows(split_three(left), lane) for left in lefts]
            wholes = [jnp.concatenate(split_three(whole), 0) for whole in wholes]
            solved = [dot_of(left, whole, 1, 0) for left, whole in zip(lefts, wholes)]
            solved = [
                value[:PANEL] + (value[PANEL : 2 * PANEL] + value[2 * PANEL :])
                for value in solved
            ]
            if not last:
                pieces = [split_three(value) for value in solved]
                lefts = [
                    jnp.concatenate([high, high, high, mid, mid, low], 0)[:, top + PANEL : BLK]
                    for high, mid, low in pieces
                ]
                rights = [
                    jnp.concatenate([high, mid, low, high, mid, high], 0)
                    for high, mid, low in pieces
                ]
                update = [dot_of(left, right, 0, 0) for left, right in zip(lefts, rights)]
            for g in range(group):
                product_ref[pl.ds(bases[g] + top, PANEL), :] = solved[g][:, -BLK:]
                if not last:
                    gram_ref[rest[g], :] = old[g][0] - update[g][:, :BLK]
                    product_ref[rest[g], :] = old[g][1] - update[g][:, BLK:]
            return nothing

        lax.fori_loop(0, count // group, step, 0)


def six_rows(pieces, lane):
    high, mid, low = pieces
    none = jnp.zeros_like(high)
    return jnp.concatenate(
        [
            jnp.where(lane < 3 * PANEL, high, none),
            jnp.where(lane < 2 * PANEL, mid, none),
            jnp.where(lane < PANEL, low, none),
        ],
        0,
    )[:, : 3 * PANEL]


def optimise_kernel(slots_ref, rates_ref, *refs, count, adds):
    grads, states = refs[:adds], refs[adds : adds + 7]
    outs = refs[-17:-10]
    in_ref, out_ref, gram_ref, product_ref, inverse_ref, grad_ref, in_sems, out_sem, grad_sem = refs[
        -9:
    ]
    for index, grad in enumerate(grads):
        pltpu.make_async_copy(grad.at[0:count], grad_ref.at[index], grad_sem).start()
    for item in range(count):
        for index, state in enumerate(states):
            pltpu.make_async_copy(
                state.at[slots_ref[item]], in_ref.at[item, index], in_sems.at[item]
            ).start()

    group = math.gcd(count, 4)
    pltpu.make_async_copy(grad_ref, grad_ref, grad_sem).wait()

    def update(step, nothing):
        items = [step * group + index for index in range(group)]
        gradients = []
        for item in items:
            pltpu.make_async_copy(in_ref.at[item], in_ref.at[item], in_sems.at[item]).wait()
            grad = sum(grad_ref[index, item].astype(single) for index in range(adds))
            gradients.append(grad.astype(bfloat))
        results = adam_group(
            items, gradients, [[in_ref[item, index] for index in range(7)] for item in items],
            [rates_ref[item] for item in items], gram_ref, product_ref, count,
        )
        for item, values in zip(items, results):
            for index, value in enumerate(values):
                out_ref[item, index] = value
        for item in items:
            for index in range(5):
                pltpu.make_async_copy(
                    out_ref.at[item, index], outs[index].at[slots_ref[item]], out_sem
                ).start()
        return nothing

    lax.fori_loop(0, count // group, update, 0)
    renew(gram_ref, product_ref, inverse_ref, 2 * count)

    def finish(item, nothing):
        for side in range(2):
            base = pl.multiple_of((side * count + item) * BLK, BLK)
            out_ref[item, 5 + side] = product_ref[pl.ds(base, BLK), :].T
            pltpu.make_async_copy(
                out_ref.at[item, 5 + side], outs[5 + side].at[slots_ref[item]], out_sem
            ).start()
        return nothing

    lax.fori_loop(0, count, finish, 0, unroll=math.gcd(count, 4))
    pltpu.make_async_copy(out_ref, out_ref, out_sem).wait()


def optimise(slots, rates, grads, states, earlier=None, after=()):
    count, total = slots.shape[0], states[0].shape[0]
    more = [] if earlier is None else list(earlier)
    skip = 2 + len(grads) + 7
    return pl.pallas_call(
        functools.partial(optimise_kernel, count=count, adds=len(grads)),
        grid_spec=pltpu.PrefetchScalarGridSpec(
            num_scalar_prefetch=2,
            grid=(),
            in_specs=[in_hbm()] * (len(grads) + 7 + len(more))
            + [anywhere()] * len(after),
            out_specs=[in_hbm()] * 7 + [anywhere()],
            scratch_shapes=[
                pltpu.VMEM((count, 7, BLK, BLK), single),
                pltpu.VMEM((count, 7, BLK, BLK), single),
                pltpu.VMEM((2 * count * BLK, BLK), single),
                pltpu.VMEM((2 * count * BLK, BLK), single),
                pltpu.VMEM((2 * count * PANEL, BLK), single),
                pltpu.VMEM((len(grads), count, BLK, BLK), bfloat),
                pltpu.SemaphoreType.DMA((count,)),
                pltpu.SemaphoreType.DMA,
                pltpu.SemaphoreType.DMA,
            ],
        ),
        out_shape=[of((total, BLK, BLK), single)] * 7 + [token_of()],
        input_output_aliases={skip + index: index for index in range(7)} if more else {},
        cost_estimate=cost(count * 40 * BLK**3, *grads, *states),
        compiler_params=pltpu.CompilerParams(vmem_limit_bytes=56 * 2**20),
        name="optimise",
    )(slots, rates, *grads, *states, *more, *after)


def whole_spec():
    return pl.BlockSpec(memory_space=pltpu.VMEM)


def fixed(shape):
    return pl.BlockSpec(shape, lambda *_: (0,) * len(shape))


def anywhere():
    return pl.BlockSpec(memory_space=pl.ANY)


def token_of():
    return of((8, 128), single)


def in_hbm():
    return pl.BlockSpec(memory_space=pltpu.HBM)


def cost(flops, *arrays):
    moved = sum(math.prod(a.shape) * jnp.dtype(a.dtype).itemsize for a in arrays)
    return pl.CostEstimate(flops=flops // 16, bytes_accessed=moved // 16, transcendentals=0)


def of(shape, dtype):
    return jax.ShapeDtypeStruct(shape, dtype)


def flip_rows(value):
    return value.astype(single).T.astype(bfloat)


def attend_kernel(q_ref, k_ref, v_ref, valid_ref, w_ref, *refs, heads, own):
    attended_ref, lse_ref, branch_ref, _, flipped_ref, score_ref, prob_ref = refs[-7:]
    keys, width = k_ref.shape
    rows = q_ref.shape[0]
    tile = 128

    flipped_ref[...] = flip_rows(v_ref[...])
    queries = flip_rows(q_ref[...]) * (HEAD_DIM ** (-0.5))
    queries = queries.astype(bfloat)
    head_of = lax.broadcasted_iota(jnp.int32, (width, rows), 0) // HEAD_DIM
    mixed = []
    for head in range(heads):
        score_ref[...] = dot_of(
            k_ref[...], jnp.where(head_of == head, queries, jnp.zeros_like(queries)), 1, 0
        )

        def masked(index):
            here = pl.ds(pl.multiple_of(index * tile, tile), tile)
            valid = valid_ref[here, :]
            valid = jnp.concatenate([valid] * (rows // 128), 1)
            return here, jnp.where(valid > 0.0, score_ref[here, :], masked_score)

        def highest_of(index, best):
            _, value = masked(index)
            return jnp.maximum(best, jnp.max(value.reshape(tile // 8, 8, rows), 0))

        best = lax.fori_loop(
            0, keys // tile, highest_of, jnp.full((8, rows), -jnp.inf, single), unroll=True
        )
        best = jnp.max(best, 0, keepdims=True)

        def weigh(index, total):
            here, value = masked(index)
            value = jnp.exp(value - best)
            prob_ref[here, :] = value.astype(bfloat)
            return total + jnp.sum(value.reshape(tile // 8, 8, rows), 0)

        total = lax.fori_loop(
            0, keys // tile, weigh, jnp.zeros((8, rows), single), unroll=True
        )
        total = jnp.sum(total, 0, keepdims=True)
        out = dot_of(
            flipped_ref[head * HEAD_DIM : (head + 1) * HEAD_DIM, :], prob_ref[...], 1, 0
        )
        mixed.append(out * (1.0 / total))
        lse_ref[head : head + 1, :] = best + jnp.log(total)
    attended = jnp.concatenate(mixed, 0).T.astype(bfloat)
    attended_ref[...] = attended
    branch = dot_of(attended, w_ref[...], 1, 0)
    if own:
        branch = branch + refs[0][...].astype(single)
    branch_ref[...] = branch.astype(bfloat)


def attend(projected, valid, w_out, block, received=None, after=()):
    seq, width = projected.shape[0], w_out.shape[0]
    rows = seq // 4
    heads = width // HEAD_DIM
    own = received is not None
    more = [received] if own else []
    out_shape = [
        of((rows, width), bfloat), of((heads, rows), single), of((rows, D), bfloat), token_of()
    ]
    return pl.pallas_call(
        functools.partial(attend_kernel, heads=heads, own=own),
        grid=(1,),
        in_specs=[
            pl.BlockSpec((rows, width), lambda i: (block, 0)),
            pl.BlockSpec((seq, width), lambda i: (0, 1)),
            pl.BlockSpec((seq, width), lambda i: (0, 2)),
            fixed(valid.shape),
            fixed(w_out.shape),
        ] + [fixed(value.shape) for value in more] + [anywhere()] * len(after),
        out_specs=[fixed(value.shape) for value in out_shape[:-1]] + [anywhere()],
        out_shape=out_shape,
        scratch_shapes=[
            pltpu.VMEM((width, seq), bfloat), pltpu.VMEM((seq, rows), single),
            pltpu.VMEM((seq, rows), bfloat),
        ],
        cost_estimate=cost(2 * 2 * rows * seq * width * heads, projected, *out_shape),
        compiler_params=pltpu.CompilerParams(vmem_limit_bytes=24 * 2**20),
        name="attend",
    )(projected, projected, projected, valid, w_out, *more, *after)


def attend_back_kernel(*refs, heads, first, extra):
    inputs = 11 if first else 13
    refs = refs[:inputs] + refs[inputs + extra :]
    if first:
        (own_ref, peer_ref, w_ref, q_ref, k_ref, v_ref, att_own, att_peer, lse_own, lse_peer,
         valid_ref, dq_ref, dk_ref, dv_ref, _, flipped_ref, grad_ref, score_ref, cross_ref, prob_ref, back_ref,
         att_ref, log_ref, dk_sum, dv_sum) = refs
    else:
        (own_ref, peer_ref, w_ref, q_ref, k_ref, v_ref, att_own, att_peer, lse_own, lse_peer,
         valid_ref, dk_in_ref, dv_in_ref, dq_ref, dk_ref, dv_ref, _, flipped_ref, grad_ref, score_ref,
         cross_ref, prob_ref, back_ref, att_ref, log_ref, dk_sum, dv_sum) = refs
    step = pl.program_id(0)
    keys, width = k_ref.shape
    rows = q_ref.shape[0]
    scale = HEAD_DIM ** (-0.5)
    tile = 128

    @pl.when(step == 0)
    def _():
        flipped_ref[...] = flip_rows(k_ref[...])
        grad_ref[...] = own_ref[...]
        att_ref[...] = att_own[...]
        log_ref[...] = lse_own[...]
        if first:
            dk_sum[...] = jnp.zeros_like(dk_sum)
            dv_sum[...] = jnp.zeros_like(dv_sum)
        else:
            dk_sum[...] = dk_in_ref[...]
            dv_sum[...] = dv_in_ref[...]

    @pl.when(step == 1)
    def _():
        grad_ref[...] = peer_ref[...]
        att_ref[...] = att_peer[...]
        log_ref[...] = lse_peer[...]

    grads = dot_of(grad_ref[...], w_ref[...], 1, 1).astype(bfloat)
    flat = grads.astype(single).T
    cross = flat * att_ref[...].astype(single).T
    grads_t = flat.astype(bfloat)
    queries = q_ref[...]
    queries_t = (flip_rows(queries) * scale).astype(bfloat)
    head_of = lax.broadcasted_iota(jnp.int32, (width, rows), 0) // HEAD_DIM
    none = jnp.zeros_like(grads_t)
    dq = []
    for head in range(heads):
        score_ref[...] = dot_of(k_ref[...], jnp.where(head_of == head, queries_t, none), 1, 0)
        cross_ref[...] = dot_of(v_ref[...], jnp.where(head_of == head, grads_t, none), 1, 0)
        lse = log_ref[head : head + 1, :]
        mean = jnp.sum(cross[head * HEAD_DIM : (head + 1) * HEAD_DIM], 0, keepdims=True)
        at = slice(head * rows, (head + 1) * rows)

        def weigh(index, nothing):
            here = pl.ds(pl.multiple_of(index * tile, tile), tile)
            valid = jnp.concatenate([valid_ref[here, :]] * (rows // 128), 1)
            value = jnp.where(valid > 0.0, score_ref[here, :], masked_score)
            prob = jnp.exp(value - lse)
            prob_ref[here, at] = prob.astype(bfloat)
            back_ref[here, at] = (prob * (cross_ref[here, :] - mean)).astype(bfloat)
            return nothing

        lax.fori_loop(0, keys // tile, weigh, 0, unroll=True)
        dq.append(
            dot_of(flipped_ref[head * HEAD_DIM : (head + 1) * HEAD_DIM, :], back_ref[:, at], 1, 0)
        )
    dq_ref[...] = (jnp.concatenate(dq, 0).T * scale).astype(bfloat)
    lane_head = lax.broadcasted_iota(jnp.int32, (rows, width), 1) // HEAD_DIM
    query_rows = jnp.concatenate(
        [jnp.where(lane_head == head, queries, jnp.zeros_like(queries)) for head in range(heads)], 0
    )
    grad_rows = jnp.concatenate(
        [jnp.where(lane_head == head, grads, jnp.zeros_like(grads)) for head in range(heads)], 0
    )

    def total(index, nothing):
        here = pl.ds(pl.multiple_of(index * 256, 256), 256)
        dk_sum[here, :] = dk_sum[here, :] + dot_of(back_ref[here, :], query_rows, 1, 0) * scale
        dv_sum[here, :] = dv_sum[here, :] + dot_of(prob_ref[here, :], grad_rows, 1, 0)
        return nothing

    lax.fori_loop(0, keys // 256, total, 0, unroll=True)

    @pl.when(step == 1)
    def _():
        dk_ref[...] = dk_sum[...].astype(dk_ref.dtype)
        dv_ref[...] = dv_sum[...].astype(dv_ref.dtype)


def attend_back(own, peer, w_out, projected, attended, lse, valid, part, earlier=None, after=()):
    seq, width = projected.shape[0], w_out.shape[0]
    rows = seq // 4
    heads = width // HEAD_DIM
    first = earlier is None
    kind = single if first else bfloat
    more = [] if first else list(earlier)
    out_shape = [
        of((2 * rows, width), bfloat), of((seq, width), kind), of((seq, width), kind), token_of()
    ]
    return pl.pallas_call(
        functools.partial(attend_back_kernel, heads=heads, first=first, extra=len(after)),
        grid=(2,),
        in_specs=[
            fixed(own.shape), fixed(peer.shape), fixed(w_out.shape),
            pl.BlockSpec((rows, width), lambda i: (2 * part + i, 0)),
            pl.BlockSpec((seq, width), lambda i: (0, 1)),
            pl.BlockSpec((seq, width), lambda i: (0, 2)),
            fixed((rows, width)), fixed((rows, width)), fixed((heads, rows)), fixed((heads, rows)),
            fixed(valid.shape),
        ] + [fixed((seq, width))] * len(more) + [anywhere()] * len(after),
        out_specs=[
            pl.BlockSpec((rows, width), lambda i: (i, 0)),
            fixed((seq, width)), fixed((seq, width)), anywhere(),
        ],
        out_shape=out_shape,
        scratch_shapes=[
            pltpu.VMEM((width, seq), bfloat), pltpu.VMEM((rows, D), bfloat),
            pltpu.VMEM((seq, rows), single), pltpu.VMEM((seq, rows), single),
            pltpu.VMEM((seq, heads * rows), bfloat), pltpu.VMEM((seq, heads * rows), bfloat),
            pltpu.VMEM((rows, width), bfloat), pltpu.VMEM((heads, rows), single),
            pltpu.VMEM((seq, width), single), pltpu.VMEM((seq, width), single),
        ],
        cost_estimate=cost(2 * 2 * rows * seq * width * 5 * heads, projected, *out_shape),
        compiler_params=pltpu.CompilerParams(vmem_limit_bytes=28 * 2**20),
        name="attend_back",
    )(own, peer, w_out, projected, projected, projected, *attended, *lse, valid, *more, *after)


def gelu_pair(value):
    size = jnp.abs(value)
    ratio = 1.0 / (1.0 + (0.3275911 * 0.5**0.5) * size)
    bell = jnp.exp(-0.5 * value * value)
    series = 0.5 * 1.061405429 * ratio + 0.5 * -1.453152027
    series = series * ratio + 0.5 * 1.421413741
    series = series * ratio + 0.5 * -0.284496736
    series = series * ratio + 0.5 * 0.254829592
    tail = series * ratio * bell
    below = jnp.where(value >= 0.0, 1.0 - tail, tail)
    return value * below, below + value * bell * (1.0 / math.sqrt(2.0 * math.pi))


def feed_kernel(rows_ref, up_ref, bias_ref, down_ref, *refs):
    act_ref, slope_ref, out_ref, _, pre_ref, sum_ref = refs[-6:]
    step = pl.program_id(0)
    rows = rows_ref.shape[0]
    tile = 32
    pre_ref[...] = dot_of(rows_ref[...], up_ref[...], 1, 0)

    def activate(index, nothing):
        here = pl.ds(pl.multiple_of(index * tile, tile), tile)
        value, slope = gelu_pair(pre_ref[here, :] + bias_ref[...])
        act_ref[here, :] = value.astype(bfloat)
        slope_ref[here, :] = slope.astype(bfloat)
        return nothing

    lax.fori_loop(0, rows // tile, activate, 0, unroll=4)
    add_up(step, dot_of(act_ref[...], down_ref[...], 1, 0), sum_ref, out_ref)


def add_up(step, more, sum_ref, out_ref):
    last = pl.num_programs(0) - 1

    @pl.when(step == 0)
    def _():
        sum_ref[...] = more

    @pl.when((step > 0) & (step < last))
    def _():
        sum_ref[...] = sum_ref[...] + more

    @pl.when(step == last)
    def _():
        out_ref[...] = (sum_ref[...] + more).astype(out_ref.dtype)


def feed(block, w_up, bias, w_down, kind, after=()):
    rows, hidden = block.shape[0], w_up.shape[1]
    step = 256
    out_shape = [
        of((rows, hidden), bfloat), of((rows, hidden), bfloat), of((rows, D), kind), token_of()
    ]
    return pl.pallas_call(
        feed_kernel,
        grid=(hidden // step,),
        in_specs=[
            fixed(block.shape),
            pl.BlockSpec((D, step), lambda j: (0, j)),
            pl.BlockSpec((1, step), lambda j: (0, j)),
            pl.BlockSpec((step, D), lambda j: (j, 0)),
        ] + [anywhere()] * len(after),
        out_specs=[
            pl.BlockSpec((rows, step), lambda j: (0, j)),
            pl.BlockSpec((rows, step), lambda j: (0, j)),
            fixed((rows, D)), anywhere(),
        ],
        out_shape=out_shape,
        scratch_shapes=[pltpu.VMEM((rows, step), single), pltpu.VMEM((rows, D), single)],
        cost_estimate=cost(4 * rows * D * hidden, w_up, w_down, *out_shape),
        compiler_params=pltpu.CompilerParams(vmem_limit_bytes=20 * 2**20),
        name="feed",
    )(block, w_up, bias, w_down, *after)


def feed_back_kernel(rows_ref, down_ref, up_ref, slope_ref, *refs):
    grad_ref, bias_ref, out_ref, _, sum_ref = refs[-5:]
    grads = dot_of(rows_ref[...], down_ref[...], 1, 1) * slope_ref[...].astype(single)
    grads = grads.astype(bfloat)
    grad_ref[...] = grads
    bias_ref[...] = jnp.sum(grads.astype(single), 0, keepdims=True)
    add_up(pl.program_id(0), dot_of(grads, up_ref[...], 1, 1), sum_ref, out_ref)


def feed_back(block, w_down, w_up, slope, kind, after=()):
    rows, hidden = block.shape[0], w_up.shape[1]
    step = 256
    out_shape = [
        of((rows, hidden), bfloat), of((1, hidden), single), of((rows, D), kind), token_of()
    ]
    return pl.pallas_call(
        feed_back_kernel,
        grid=(hidden // step,),
        in_specs=[
            fixed(block.shape),
            pl.BlockSpec((step, D), lambda j: (j, 0)),
            pl.BlockSpec((D, step), lambda j: (0, j)),
            pl.BlockSpec((rows, step), lambda j: (0, j)),
        ] + [anywhere()] * len(after),
        out_specs=[
            pl.BlockSpec((rows, step), lambda j: (0, j)),
            pl.BlockSpec((1, step), lambda j: (0, j)),
            fixed((rows, D)), anywhere(),
        ],
        out_shape=out_shape,
        scratch_shapes=[pltpu.VMEM((rows, D), single)],
        cost_estimate=cost(4 * rows * D * hidden, w_up, w_down, *out_shape),
        compiler_params=pltpu.CompilerParams(vmem_limit_bytes=20 * 2**20),
        name="feed_back",
    )(block, w_down, w_up, slope, *after)


def chip_kernel(keep_ref, got_ref, *refs):
    refs[-2][...] = (keep_ref[...] + got_ref[...].astype(single)).astype(bfloat)


def standardise(value):
    centred = value - jnp.mean(value, -1, keepdims=True)
    inv_std = lax.rsqrt(jnp.mean(centred * centred, -1, keepdims=True) + norm_eps)
    return centred * inv_std, inv_std


def through_norm(grads, normed, inv_std, gain):
    scaled = grads * gain
    mean_grad = jnp.mean(scaled, -1, keepdims=True)
    mean_cross = jnp.mean(scaled * normed, -1, keepdims=True)
    return inv_std * (scaled - mean_grad - normed * mean_cross)


def gain_sums(grads, normed, rounded):
    total = lambda value: jnp.sum(value, 0, keepdims=True)
    blank = jnp.zeros((5, grads.shape[1]), single)
    return jnp.concatenate(
        [total(grads * normed), total(grads), total(rounded.astype(single)), blank], 0
    )


norm_tile = 128


def norm_one_kernel(chip_ref, across_ref, rows_ref, vectors_ref, *refs):
    normed_ref, inv_ref, hidden_ref = refs[-4:-1]
    branch = chip_ref[...].astype(single) + across_ref[...].astype(single)
    normed, inv_std = standardise(rows_ref[...].astype(single) + (branch + vectors_ref[2:3, :]))
    normed_ref[...] = normed
    inv_ref[...] = jnp.broadcast_to(inv_std, inv_ref.shape)
    hidden_ref[...] = (normed * vectors_ref[0:1, :] + vectors_ref[1:2, :]).astype(bfloat)


def norm_two_kernel(
    chip_ref, across_ref, normed_ref, cot_ref, valid_ref, one_ref, two_ref, *refs
):
    out_ref, grad_ref, low_ref, sums_ref = refs[-5:-1]

    @pl.when(pl.program_id(0) == 0)
    def _():
        sums_ref[...] = jnp.zeros_like(sums_ref)

    hidden = normed_ref[...] * one_ref[0:1, :] + one_ref[1:2, :]
    down = chip_ref[...].astype(single) + across_ref[...].astype(single)
    normed, inv_std = standardise(hidden + (down + two_ref[2:3, :]))
    gain = two_ref[0:1, :]
    out_ref[...] = (normed * gain + two_ref[1:2, :]).astype(bfloat)
    grads = cot_ref[...].astype(single) * valid_ref[:, 0:1]
    back = through_norm(grads, normed, inv_std, gain)
    grad_ref[...] = back
    low = back.astype(bfloat)
    low_ref[...] = low
    sums_ref[...] += gain_sums(grads, normed, low)


def norm_back_kernel(
    chip_ref, across_ref, second_ref, normed_ref, inv_ref, one_ref, *refs
):
    grad_ref, low_ref, sums_ref = refs[-4:-1]

    @pl.when(pl.program_id(0) == 0)
    def _():
        sums_ref[...] = jnp.zeros_like(sums_ref)

    grads = chip_ref[...].astype(single) + across_ref[...].astype(single) + second_ref[...]
    normed = normed_ref[...]
    back = through_norm(grads, normed, inv_ref[:, 0:1], one_ref[0:1, :])
    grad_ref[...] = back
    low = back.astype(bfloat)
    low_ref[...] = low
    sums_ref[...] += gain_sums(grads, normed, low)


def norm_call(kernel, name, rowed, fixed_in, row_outs, sums, after=()):
    rows = rowed[0].shape[0]
    by_row = lambda width: pl.BlockSpec((norm_tile, width), lambda i: (i, 0))
    out_shape = [of((rows, width), kind) for width, kind in row_outs]
    out_specs = [by_row(width) for width, _ in row_outs]
    if sums:
        out_shape.append(of((8, D), single))
        out_specs.append(fixed((8, D)))
    out_shape.append(token_of())
    out_specs.append(anywhere())
    return pl.pallas_call(
        kernel,
        grid=(rows // norm_tile,),
        in_specs=[by_row(value.shape[1]) for value in rowed]
        + [fixed(value.shape) for value in fixed_in]
        + [anywhere()] * len(after),
        out_specs=out_specs,
        out_shape=out_shape,
        cost_estimate=cost(20 * rows * D, *rowed, *out_shape),
        compiler_params=pltpu.CompilerParams(vmem_limit_bytes=16 * 2**20),
        name=name,
    )(*rowed, *fixed_in, *after)


def token_back_kernel(*refs):
    dq_refs, (dk_ref, dv_ref, w_ref), outs = refs[:2], refs[2:5], refs[-5:-1]
    width = dk_ref.shape[1]
    rows = dk_ref.shape[0] // 4
    for block in range(4):
        here = slice(block * rows, (block + 1) * rows)
        parts = [
            dq_refs[block // 2][block % 2 * rows : (block % 2 + 1) * rows, :],
            dk_ref[here, :], dv_ref[here, :],
        ]
        value = dot_of(jnp.concatenate(parts, 1), w_ref[...], 1, 1)
        outs[block][...] = value.astype(outs[block].dtype)


def token_back(dq_a, dq_b, dk, dv, w_qkv, after=()):
    rows = dk.shape[0] // 4
    out_shape = [of((rows, D), kind) for kind in (single, bfloat, single, bfloat)] + [token_of()]
    return pl.pallas_call(
        token_back_kernel,
        in_specs=[whole_spec()] * 5 + [anywhere()] * len(after),
        out_specs=[whole_spec()] * 4 + [anywhere()],
        out_shape=out_shape,
        cost_estimate=cost(8 * rows * D * w_qkv.shape[1], w_qkv, dk, *out_shape),
        compiler_params=pltpu.CompilerParams(vmem_limit_bytes=12 * 2**20),
        name="token_back",
    )(dq_a, dq_b, dk, dv, w_qkv, *after)


def pack_kernel(target_ref, *refs, jobs, scale, regions, count, resumed):
    outs = refs[-4 - len(regions) : -4]
    held_ref, sem, in_sem = refs[-3:]
    if resumed:
        start = pltpu.make_async_copy(refs[count], held_ref, in_sem)
        start.start()
    waited = not resumed
    for lefts, rights, layout, rows, cols in jobs:
        right = jnp.concatenate([refs[index][...] for index in rights], 0)
        for row in range(0, rows, 2):
            span = min(2, rows - row)
            left = jnp.concatenate(
                [refs[index][:, row * BLK : (row + span) * BLK] for index in lefts], 0
            )
            weights = (dot_of(left, right, 0, 0) * scale).astype(bfloat)
            if not waited:
                start.wait()
                waited = True
            for i in range(span):
                for col in range(cols):
                    held_ref[target_ref[layout(row + i, col)]] = weights[
                        i * BLK : (i + 1) * BLK, col * BLK : (col + 1) * BLK
                    ]
    copies = [
        pltpu.make_async_copy(held_ref.at[first : first + size], out, sem.at[index])
        for index, ((first, size), out) in enumerate(zip(regions, outs))
    ]
    for copy in copies:
        copy.start()
    for copy in copies:
        copy.wait()


def pack(target, pairs, scale, regions, earlier=None, after=()):
    operands, jobs, blocks, flops = [], [], 0, 0
    total = target.shape[0]

    def places(arrays):
        found = []
        for value in arrays:
            if not any(value is other for other in operands):
                operands.append(value)
            found.append([value is other for other in operands].index(True))
        return found

    for lefts, rights, layout in pairs:
        rows, cols = lefts[0].shape[1] // BLK, rights[0].shape[1] // BLK
        jobs.append((places(lefts), places(rights), layout, rows, cols))
        blocks += rows * cols
        flops += 2 * rows * cols * BLK * BLK * sum(value.shape[0] for value in lefts)
    more = [] if earlier is None else [earlier]
    return pl.pallas_call(
        functools.partial(
            pack_kernel, jobs=jobs, scale=scale, regions=regions, count=len(operands),
            resumed=bool(more),
        ),
        grid_spec=pltpu.PrefetchScalarGridSpec(
            num_scalar_prefetch=1,
            grid=(),
            in_specs=[whole_spec()] * len(operands)
            + [in_hbm()] * len(more)
            + [anywhere()] * len(after),
            out_specs=[anywhere()] * (len(regions) + 1),
            scratch_shapes=[
                pltpu.VMEM((total, BLK, BLK), bfloat),
                pltpu.SemaphoreType.DMA((len(regions),)),
                pltpu.SemaphoreType.DMA,
            ],
        ),
        out_shape=[of((size, BLK, BLK), bfloat) for _, size in regions] + [token_of()],
        cost_estimate=cost(flops, *operands, of((blocks, BLK, BLK), bfloat)),
        compiler_params=pltpu.CompilerParams(vmem_limit_bytes=28 * 2**20),
        name="pack",
    )(target, *operands, *more, *after)


def join_kernel(*refs, groups):
    out_ref = refs[-2]
    at = 0
    for index, terms in enumerate(groups):
        total = 0.0
        for ref in refs[at : at + terms]:
            value = ref[...].reshape(-1, BLK, BLK)
            total = total + value.astype(single)
        at += terms
        size = total.shape[0]
        out_ref[index * size : (index + 1) * size] = total.astype(bfloat)


def join(hop, groups, after=()):
    operands, specs = [], []
    for keep, got, *carried in groups:
        slots = keep.shape[0] // (lax.axis_size("dp") // 2)
        block = pl.BlockSpec((slots, BLK, BLK), lambda i: (hop, 0, 0))
        operands += [keep, got, *carried]
        specs += [block] + [fixed((slots, BLK, BLK))] * (1 + len(carried))
    out = of((slots * len(groups), BLK, BLK), bfloat)
    return pl.pallas_call(
        functools.partial(join_kernel, groups=[len(group) for group in groups]),
        grid=(1,),
        in_specs=specs + [anywhere()] * len(after),
        out_specs=[fixed(out.shape), anywhere()],
        out_shape=[out, token_of()],
        cost_estimate=cost(1, out),
        compiler_params=pltpu.CompilerParams(vmem_limit_bytes=10 * 2**20),
        name="join",
    )(*operands, *after)


def block_counts(tensors):
    return (D * D // (tensors * BLK * BLK), D * FF // (tensors * BLK * BLK))


def rate_values(canon_index, tensors, seq_len):
    attn_count, ffn_count = block_counts(tensors)
    out_std = math.sqrt(seq_len / (3.0 * D))
    inner = jnp.where(canon_index < 4 * attn_count + ffn_count, D ** (-0.5), FF ** (-0.5))
    inner = jnp.where(canon_index < 4 * attn_count, out_std, inner)
    return jnp.where(canon_index < 3 * attn_count, D ** (-0.5), inner).astype(single)


def swap(value, axis, bit):
    count = lax.axis_size(axis)
    return lax.ppermute(value, axis, [(i, i ^ bit) for i in range(count)])


def ring(value):
    count = lax.axis_size("dp")
    return lax.ppermute(value, "dp", [(i, (i + 2) % count) for i in range(count)])


def gather_slots(local, parts):
    size = local.shape[0] // parts
    hops = lax.axis_size("dp") // 2
    pieces = [[[None] * parts for _ in range(2)] for _ in range(hops)]
    for part in range(parts):
        shard = local[part * size : (part + 1) * size] if parts > 1 else local
        for hop in range(hops):
            pieces[hop][0][part] = shard
            pieces[hop][1][part] = swap(shard, "dp", 1)
            if hop < hops - 1:
                shard = ring(shard)
    return [piece for pair in pieces for flip in pair for piece in flip]


def vector_kernel(rank_ref, one_ref, two_ref, up_a, up_b, up_c, up_d, dq_a, dq_b, dv_ref, *refs):
    out_ref = refs[-2]
    rank = rank_ref[0]
    out_ref[...] = jnp.zeros_like(out_ref)
    out_ref[0:2, :] = one_ref[0:2, :]
    out_ref[2:4, :] = two_ref[0:2, :]
    out_ref[6:7, :] = one_ref[2:3, :]
    out_ref[11:12, :] = two_ref[2:3, :]
    width = dv_ref.shape[1]
    query = jnp.sum(dq_a[...].astype(single), 0, keepdims=True) + jnp.sum(
        dq_b[...].astype(single), 0, keepdims=True
    )
    value = jnp.sum(dv_ref[...].astype(single), 0, keepdims=True)
    place = lax.broadcasted_iota(jnp.int32, (1, D), 1) // width == rank
    for row, total in ((4, query), (5, value)):
        wide = jnp.concatenate([total] * (D // width), 1)
        out_ref[row : row + 1, :] = jnp.where(place, wide, 0.0)
    bias = up_a[...] + up_b[...] + up_c[...] + up_d[...]
    size = bias.shape[1]
    for row in range(FF // D):
        for part in range(D // size if size < D else 1):
            here = (row * D + part * size) // size == rank
            out_ref[7 + row : 8 + row, part * size : (part + 1) * size] = jnp.where(here, bias, 0.0)


def vector_rows(rank, sums_one, sums_two, bias_parts, dq_a, dq_b, grad_value, after):
    operands = [sums_one, sums_two, *bias_parts, dq_a, dq_b, grad_value]
    return pl.pallas_call(
        vector_kernel,
        grid_spec=pltpu.PrefetchScalarGridSpec(
            num_scalar_prefetch=1,
            grid=(),
            in_specs=[whole_spec()] * len(operands) + [anywhere()] * len(after),
            out_specs=[whole_spec(), anywhere()],
        ),
        out_shape=[of((16, D), single), token_of()],
        cost_estimate=cost(1, *operands),
        compiler_params=pltpu.CompilerParams(vmem_limit_bytes=5 * 2**20),
        name="vector_rows",
    )(rank, *operands, *after)


def hop_sum(value, axis, bit):
    return value + swap(value, axis, bit)


def assemble_kernel(source_ref, *refs, sizes, layouts):
    count = len(sizes)
    pieces, outs, (held, sems) = refs[:count], refs[-2 - len(set(job[0] for job in layouts)) : -2], refs[-2:]
    copies, start = [], 0
    for index, size in enumerate(sizes):
        copies.append(pltpu.make_async_copy(pieces[index], held.at[start : start + size], sems.at[index]))
        start += size
    for copy in copies:
        copy.start()
    for copy in copies:
        copy.wait()
    canon = 0
    for target, rows, cols, row_at, col_at in layouts:
        for row in range(rows):
            for col in range(cols):
                outs[target][
                    (row_at + row) * BLK : (row_at + row + 1) * BLK,
                    (col_at + col) * BLK : (col_at + col + 1) * BLK,
                ] = held[source_ref[canon]]
                canon += 1


def assemble(source, pieces, shapes, layouts, after=()):
    sizes = [piece.shape[0] for piece in pieces]
    return pl.pallas_call(
        functools.partial(assemble_kernel, sizes=sizes, layouts=layouts),
        grid_spec=pltpu.PrefetchScalarGridSpec(
            num_scalar_prefetch=1,
            grid=(1,),
            in_specs=[in_hbm()] * len(pieces) + [anywhere()] * len(after),
            out_specs=[pl.BlockSpec(shape, lambda i, *_: (0, 0)) for shape in shapes],
            scratch_shapes=[
                pltpu.VMEM((sum(sizes), BLK, BLK), bfloat),
                pltpu.SemaphoreType.DMA((len(sizes),)),
            ],
        ),
        out_shape=[jax.ShapeDtypeStruct(shape, bfloat) for shape in shapes],
        compiler_params=pltpu.CompilerParams(vmem_limit_bytes=40 * 2**20),
        name="assemble",
    )(source, *pieces, *after)


def chip_sum(keep, send, after=()):
    return norm_call(
        chip_kernel, "chip_sum", [keep, peer_of(send)], [], [(D, bfloat)], False, after
    )


def across(value):
    return swap(value, "tensor", 2)


def peer_of(value):
    return swap(value, "tensor", 1)


def body(
    tokens,
    cotangent,
    seq_lengths,
    block_owner,
    master_blocks,
    first_moment,
    second_moment,
    left_stats,
    right_stats,
    left_basis,
    right_basis,
    vector_master,
    vector_first,
    vector_second,
):
    tensors = lax.axis_size("tensor")
    data_ranks = lax.axis_size("dp")
    tensor_rank = lax.axis_index("tensor")
    data_rank = lax.axis_index("dp")
    local_rows = tokens.shape[0]
    seq_len = local_rows * tensors
    slice_width = D // tensors
    hidden_width = FF // tensors
    block_total = block_owner.shape[0]
    slots_here = master_blocks.shape[1]
    length = seq_lengths[0]
    attn_count, ffn_count = block_counts(tensors)
    permuted = data_ranks <= 16
    hops = data_ranks // 2
    canon_ids = jnp.arange(block_total, dtype=jnp.int32)
    holder, slot = block_owner // slots_here, block_owner % slots_here
    source = target = block_owner
    if permuted:
        flip = (holder % 2) ^ (data_rank % 2)
        down = (data_rank // 2 - holder // 2) % hops
        up = (holder // 2 - data_rank // 2) % hops
        source = (down * 2 + flip) * slots_here + slot
        target = (flip * hops + up) * slots_here + slot
    mine = block_owner[None, :] == data_rank * slots_here + jnp.arange(slots_here)[:, None]
    own_canon = jnp.sum(jnp.where(mine, canon_ids[None, :], 0), 1)
    own_slots = jnp.arange(slots_here, dtype=jnp.int32)

    cols = slice_width // BLK
    wide = hidden_width // BLK
    full = D // BLK
    local_weights = master_blocks[0].astype(bfloat)
    if permuted:
        pieces = gather_slots(local_weights, 3)
    else:
        pieces = [lax.all_gather(local_weights, "dp", axis=0, tiled=True)]
    w_qkv, w_out, w_up, w_down = assemble(
        source,
        pieces,
        [(D, 3 * slice_width), (slice_width, D), (D, hidden_width), (hidden_width, D)],
        [
            (0, full, cols, 0, 0),
            (0, full, cols, 0, cols),
            (0, full, cols, 0, 2 * cols),
            (1, cols, full, 0, 0),
            (2, full, wide, 0, 0),
            (3, wide, full, 0, 0),
        ],
    )
    gain_one, shift_one = (vector_master[0:D], vector_master[D : 2 * D])
    gain_two, shift_two = (vector_master[2 * D : 3 * D], vector_master[3 * D : 4 * D])
    bias_query = lax.dynamic_slice_in_dim(
        vector_master, 4 * D + tensor_rank * slice_width, slice_width
    )
    bias_value = lax.dynamic_slice_in_dim(
        vector_master, 5 * D + tensor_rank * slice_width, slice_width
    )
    bias_out = vector_master[6 * D : 7 * D]
    bias_up = lax.dynamic_slice_in_dim(
        vector_master, 7 * D + tensor_rank * hidden_width, hidden_width
    )
    bias_down = vector_master[7 * D + FF : 8 * D + FF]

    tokens_b = swap(tokens, "tensor", 2)
    cotangent_b = swap(cotangent, "tensor", 2)
    full_tokens = jnp.concatenate(
        [tokens, peer_of(tokens), tokens_b, peer_of(tokens_b)], axis=0
    )
    quarters = tensor_rank ^ jnp.arange(4, dtype=jnp.int32)
    positions = (quarters[:, None] * local_rows + jnp.arange(local_rows)[None, :]).reshape(-1)
    key_valid = positions < length
    row_valid = key_valid.astype(single)[:, None]
    chunk = 2 * local_rows

    bias_qkv = jnp.concatenate([bias_query, jnp.zeros((slice_width,), single), bias_value])
    projected = (jnp.dot(full_tokens, w_qkv, preferred_element_type=single) + bias_qkv).astype(
        bfloat
    )
    one = jnp.stack([gain_one, shift_one, bias_out])
    two = jnp.stack([gain_two, shift_two, bias_down])
    valid = jnp.broadcast_to(row_valid, (seq_len, 128))
    grad_scale = 1.0 / math.sqrt(seq_len * data_ranks)
    up_start = 4 * attn_count

    attended, lse, shares = [None] * 4, [None] * 4, [None] * 4
    attended[3], lse[3], shares[3], token = attend(
        projected, valid, w_out, 3, after=[cotangent_b]
    )
    attended[1], lse[1], shares[1], token = attend(projected, valid, w_out, 1, after=[token])
    for block in (2, 0):
        attended[block], lse[block], shares[block], token = attend(
            projected, valid, w_out, block, peer_of(shares[block + 1]),
            after=[token],
        )
    chip = [shares[0], shares[2]]
    other = [across(chip[1]), across(chip[0])]

    normed_one, inv_one = [None] * 2, [None] * 2
    hidden, activation, slope, chip_two = [None] * 4, [None] * 4, [None] * 4, [None] * 2
    bias_row = bias_up[None, :]

    def norm_up(part, after):
        normed_one[part], inv_one[part], hidden[2 * part], token = norm_call(
            norm_one_kernel, "norm_one", [chip[part], other[part], (tokens, tokens_b)[part]],
            [one], [(D, single), (128, single), (D, bfloat)], False, after,
        )
        hidden[2 * part + 1] = peer_of(hidden[2 * part])
        return token

    def feed_part(part, token, arrived=()):
        block = 2 * part
        activation[block], slope[block], keep, token = feed(
            hidden[block], w_up, bias_row, w_down, single, [token]
        )
        block += 1
        activation[block], slope[block], send, token = feed(
            hidden[block], w_up, bias_row, w_down, bfloat, [token, *arrived]
        )
        return keep, send, token

    token = norm_up(0, [token])
    *sums, token = feed_part(0, token)
    token = norm_up(1, [token])
    chip_two[0], token = chip_sum(*sums, [token])
    other = [None, across(chip_two[0])]
    *sums, token = feed_part(1, token, [other[1]])
    chip_two[1], token = chip_sum(*sums, [token])
    other[0] = across(chip_two[1])

    grad_second, grad_down, grad_up = [None] * 2, [None] * 4, [None] * 4
    bias_parts, chip_three, outs, sums_two = [None] * 4, [None] * 2, [None] * 2, [None] * 2

    def norm_down(part, token):
        rows_valid = valid[part * chunk : part * chunk + local_rows]
        outs[part], grad_second[part], grad_down[2 * part], sums_two[part], token = norm_call(
            norm_two_kernel, "norm_two",
            [chip_two[part], other[part], normed_one[part], (cotangent, cotangent_b)[part],
             rows_valid],
            [one, two], [(D, bfloat), (D, single), (D, bfloat)], True, [token],
        )
        grad_down[2 * part + 1] = peer_of(grad_down[2 * part])
        return token

    def feed_back_part(part, token):
        block = 2 * part
        grad_up[block], bias_parts[block], keep, token = feed_back(
            grad_down[block], w_down, w_up, slope[block], single, [token]
        )
        block += 1
        grad_up[block], bias_parts[block], send, token = feed_back(
            grad_down[block], w_down, w_up, slope[block], bfloat, [token]
        )
        return keep, send, token

    token = norm_down(1, token)
    *sums, token = feed_back_part(1, token)
    token = norm_down(0, token)
    chip_three[1], token = chip_sum(*sums, [token])
    other = [across(chip_three[1]), None]
    *sums, token = feed_back_part(0, token)
    chip_three[0], token = chip_sum(*sums, [token])
    other[1] = across(chip_three[0])
    layer_output = outs[0]
    *sent, token = pack(
        target,
        [
            (hidden, grad_up, lambda row, col: up_start + row * wide + col),
            (activation, grad_down, lambda row, col: up_start + ffn_count + row * full + col),
        ],
        grad_scale,
        [(0, block_total)],
        after=[token],
    )

    grad_branch, grad_query, back, grad_rows, sums_one = [None] * 4, [None] * 2, None, [0, 0], [0, 0]
    for part in (0, 1):
        block = 2 * part
        grad_rows[part], grad_branch[block], sums_one[part], token = norm_call(
            norm_back_kernel, "norm_back",
            [chip_three[part], other[part], grad_second[part], normed_one[part], inv_one[part]],
            [one], [(D, single), (D, bfloat)], True, [token],
        )
        grad_branch[block + 1] = peer_of(grad_branch[block])
        grad_query[part], *back, token = attend_back(
            grad_branch[block], grad_branch[block + 1], w_out, projected,
            attended[block : block + 2], lse[block : block + 2], valid, part, back, [token],
        )
    grad_summed, sums_one = grad_rows[0], sums_one[0]
    grad_key, grad_value = back
    moved = hops * slots_here
    regions = [(0, block_total)]
    if permuted:
        regions = [(0, moved)] + [
            (moved + hop * slots_here, slots_here) for hop in range(hops)
        ]
    kept, *leaving, token = pack(
        target,
        [
            ([full_tokens], grad_query, lambda row, col: row * cols + col),
            ([full_tokens], [grad_key], lambda row, col: attn_count + row * cols + col),
            ([full_tokens], [grad_value], lambda row, col: 2 * attn_count + row * cols + col),
            (attended, grad_branch, lambda row, col: 3 * attn_count + row * full + col),
        ],
        grad_scale,
        regions,
        sent[0],
        [token],
    )
    vector_grad, token = vector_rows(
        tensor_rank.astype(jnp.int32)[None], sums_one, sums_two[0], bias_parts, *grad_query,
        grad_value, [token],
    )
    vector_grad = hop_sum(vector_grad, "tensor", 1)
    vector_grad = hop_sum(vector_grad, "tensor", 2)
    def finish_tokens(token):
        keep_a, send_a, keep_b, send_b, token = token_back(
            grad_query[0], grad_query[1], grad_key, grad_value, w_qkv, [token]
        )
        chip_b = chip_sum(keep_b, send_b, [token])[0]
        chip_a = chip_sum(keep_a, send_a, [token])[0]
        over = across(chip_b)
        token_grad = (chip_a.astype(single) + over.astype(single) + grad_summed).astype(bfloat)
        return token_grad, token

    bits = []
    bit = 1
    while bit < data_ranks:
        bits.append(bit)
        bit *= 2
    bits = bits[1:] + bits[:1]
    if permuted:
        carried, after = [], [token]
        for bit in bits[:-1]:
            vector_grad = hop_sum(vector_grad, "dp", bit)
            after.append(vector_grad)
        bits = bits[-1:]
        for hop in range(hops - 1, 0, -1):
            got = swap(leaving[hop], "dp", 1)
            total, token = join(hop, [[kept, got] + carried], after)
            if hop == hops - 1:
                token_grad, token = finish_tokens(token)
            carried, after = [ring(total)], [token]
        own_grad = [kept, swap(leaving[0], "dp", 1)] + carried
    else:
        token_grad, token = finish_tokens(token)
        own_grad = [lax.psum_scatter(kept, "dp", scatter_dimension=0, tiled=True)]
    for bit in bits:
        vector_grad = hop_sum(vector_grad, "dp", bit)
    vector_sum = vector_grad[: 8 + FF // D].reshape(-1) * grad_scale
    rates = rate_values(own_canon, tensors, seq_len)
    correction = 1.0 - moment_decay**STEP
    states = [
        first_moment[0], second_moment[0], master_blocks[0], left_stats[0], right_stats[0],
        left_basis[0], right_basis[0],
    ]
    *fresh, _ = optimise(own_slots, rates, own_grad, states)
    fresh_first, fresh_second, fresh_master, fresh_left, fresh_right, basis_left, basis_right = fresh
    vec_first = moment_decay * vector_first + (1.0 - moment_decay) * vector_sum
    vec_second = moment_decay * vector_second + (1.0 - moment_decay) * vector_sum * vector_sum
    vec_master = vector_master - vector_rate * (vec_first / correction) / (
        jnp.sqrt(vec_second / correction) + adam_eps
    )
    return (
        layer_output,
        token_grad,
        fresh_first[None],
        fresh_second[None],
        fresh_master[None],
        fresh_left[None],
        fresh_right[None],
        basis_left[None],
        basis_right[None],
        vec_first,
        vec_second,
        vec_master,
    )


def solution(mesh):
    return jax.shard_map(
        body,
        mesh=mesh,
        in_specs=(
            P(("dp", "tensor"), None),
            P(("dp", "tensor"), None),
            P("dp"),
            P(),
            P("tensor", "dp", None, None),
            P("tensor", "dp", None, None),
            P("tensor", "dp", None, None),
            P("tensor", "dp", None, None),
            P("tensor", "dp", None, None),
            P("tensor", "dp", None, None),
            P("tensor", "dp", None, None),
            P(),
            P(),
            P(),
        ),
        out_specs=(
            P(("dp", "tensor"), None),
            P(("dp", "tensor"), None),
            P("tensor", "dp", None, None),
            P("tensor", "dp", None, None),
            P("tensor", "dp", None, None),
            P("tensor", "dp", None, None),
            P("tensor", "dp", None, None),
            P("tensor", "dp", None, None),
            P("tensor", "dp", None, None),
            P(),
            P(),
            P(),
        ),
        check_vma=False,
    )
```

```python
import functools
import math

import jax
import jax.numpy as jnp
from jax import lax
from jax.experimental import pallas as pl
from jax.experimental.pallas import tpu as pltpu
from jax.sharding import PartitionSpec as P

D = 1024
FF = 4096
HEAD_DIM = 64
BLK = 128
STEP = 10


norm_eps = 1e-05
adam_eps = 1e-08
moment_decay = 0.5
weight_decay = 0.01
vector_rate = 0.25
masked_score = -1000000000.0
bfloat = jnp.bfloat16
single = jnp.float32


PANEL = 32


def dot_of(left, right, left_dim, right_dim):
    return lax.dot_general(
        left, right, (((left_dim,), (right_dim,)), ((), ())), preferred_element_type=single
    )


def split_two(value):
    high = value.astype(bfloat)
    return high, (value - high.astype(single)).astype(bfloat)


def split_three(value):
    high = value.astype(bfloat)
    rest = value - high.astype(single)
    mid = rest.astype(bfloat)
    return high, mid, (rest - mid.astype(single)).astype(bfloat)


def dot_three(left, right, left_dim, right_dim):
    stacked_left = jnp.concatenate([left[0], left[0], left[1]], axis=left_dim)
    stacked_right = jnp.concatenate([right[0], right[1], right[0]], axis=right_dim)
    return dot_of(stacked_left, stacked_right, left_dim, right_dim)


def dot_two(pair, other, pair_dim, other_dim, swapped=False):
    stacked = jnp.concatenate(pair, axis=pair_dim)
    twice = jnp.concatenate([other, other], axis=other_dim)
    if swapped:
        return dot_of(twice, stacked, other_dim, pair_dim)
    return dot_of(stacked, twice, pair_dim, other_dim)


def gram_six(pieces):
    high, mid, low = pieces
    left = jnp.concatenate([high, high, high, mid, mid, low], axis=1)
    right = jnp.concatenate([high, mid, low, high, mid, high], axis=1)
    return dot_of(left, right, 1, 1)


def adam_group(items, grads, states, rates, gram_ref, product_ref, count):
    correction = 1.0 - moment_decay**STEP
    scale = (1.0 - moment_decay) / BLK
    first, second, master, left_stat, right_stat, left, right = zip(*states)
    left_t = [split_two(value.T) for value in left]
    right_t = [split_two(value.T) for value in right]
    left = [split_two(value) for value in left]
    right = [split_two(value) for value in right]
    half = [dot_two(r, g, 0, 1, True).astype(bfloat) for r, g in zip(right, grads)]
    new_left = [
        moment_decay * old + scale * dot_of(g, g, 1, 1) for old, g in zip(left_stat, grads)
    ]
    new_right = [
        moment_decay * old + scale * dot_of(g, g, 0, 0) for old, g in zip(right_stat, grads)
    ]
    rotated = [dot_two(t, value, 1, 0) for t, value in zip(left_t, half)]
    sides = []
    for stats, basis in ((new_left, left_t), (new_right, right_t)):
        sides.append([dot_three(b, split_two(value), 1, 0) for b, value in zip(basis, stats)])
    new_first = [moment_decay * old + (1.0 - moment_decay) * r for old, r in zip(first, rotated)]
    new_second = [
        moment_decay * old + (1.0 - moment_decay) * r * r for old, r in zip(second, rotated)
    ]
    direction = [
        ((m / correction) / (jnp.sqrt(v / correction) + adam_eps)).astype(bfloat)
        for m, v in zip(new_first, new_second)
    ]
    half = [
        dot_two(t, value, 0, 1, True).astype(bfloat) for t, value in zip(right_t, direction)
    ]
    grams = [[gram_six(split_three(value)) for value in side] for side in sides]
    turned = [dot_two(b, value, 1, 0) for b, value in zip(left, half)]
    new_master = [
        old - rate * (value + weight_decay * old)
        for old, rate, value in zip(master, rates, turned)
    ]
    for side in range(2):
        for item, product, gram in zip(items, sides[side], grams[side]):
            here = pl.ds(pl.multiple_of((side * count + item) * BLK, BLK), BLK)
            product_ref[here, :] = product
            gram_ref[here, :] = gram
    return list(zip(new_first, new_second, new_master, new_left, new_right))


def factor_panel(rows):
    pieces = PANEL // 8
    batch = rows[0].shape[1]
    work = [
        [rows[j][8 * i : 8 * i + 8] if i >= j // 8 else None for i in range(pieces)]
        for j in range(PANEL)
    ]
    sublane = lax.broadcasted_iota(jnp.int32, (8, batch), 0)
    zero = jnp.zeros((8, batch), single)
    inverse = [[None] * pieces for _ in range(PANEL)]
    for k in range(PANEL):
        group, lane = divmod(k, 8)
        pivot = work[k][group][lane : lane + 1]
        root = lax.rsqrt(pivot)
        root = root * (1.5 - 0.5 * pivot * root * root)
        root = jnp.broadcast_to(root, (8, batch))
        column = [work[k][i] * root if i >= group else None for i in range(pieces)]
        done = []
        for i in range(group + 1):
            value = inverse[k][i]
            value = zero if value is None else value * root
            done.append(jnp.where(sublane == lane, root, value) if i == group else value)
        inverse[k] = done + [zero] * (pieces - group - 1)
        for j in range(k + 1, PANEL):
            row_group, row_lane = divmod(j, 8)
            factor = jnp.broadcast_to(column[row_group][row_lane : row_lane + 1], (8, batch))
            for i in range(row_group, pieces):
                work[j][i] = work[j][i] - factor * column[i]
            for i in range(group + 1):
                term = factor * done[i]
                inverse[j][i] = -term if inverse[j][i] is None else inverse[j][i] - term
    return inverse


def renew(gram_ref, product_ref, inverse_ref, count):
    group = math.gcd(count, 16)
    lane = lax.broadcasted_iota(jnp.int32, (PANEL, BLK), 1)
    for panel in range(BLK // PANEL):
        top = panel * PANEL
        last = panel == BLK // PANEL - 1
        rows = []
        for j in range(PANEL):
            row = gram_ref[pl.ds(top + j, count, stride=BLK), :]
            rows.append(row.T[top : top + PANEL])
        inverse = factor_panel(rows)
        for i in range(PANEL):
            row = jnp.concatenate(inverse[i], 0)
            inverse_ref[pl.ds(i, count, stride=PANEL), :] = jnp.concatenate([row] * 4, 0).T

        def step(index, nothing):
            bases = [pl.multiple_of((index * group + g) * BLK, BLK) for g in range(group)]
            lefts, wholes = [], []
            for g in range(group):
                here = pl.ds(pl.multiple_of((index * group + g) * PANEL, PANEL), PANEL)
                lefts.append(inverse_ref[here, :])
                rows_at = pl.ds(bases[g] + top, PANEL)
                whole = product_ref[rows_at, :]
                if not last:
                    whole = jnp.concatenate([gram_ref[rows_at, :], whole], 1)
                wholes.append(whole)
            rest = [pl.ds(base + top + PANEL, BLK - top - PANEL) for base in bases]
            if not last:
                old = [(gram_ref[at, :], product_ref[at, :]) for at in rest]
            lefts = [six_rows(split_three(left), lane) for left in lefts]
            wholes = [jnp.concatenate(split_three(whole), 0) for whole in wholes]
            solved = [dot_of(left, whole, 1, 0) for left, whole in zip(lefts, wholes)]
            solved = [
                value[:PANEL] + (value[PANEL : 2 * PANEL] + value[2 * PANEL :])
                for value in solved
            ]
            if not last:
                pieces = [split_three(value) for value in solved]
                lefts = [
                    jnp.concatenate([high, high, high, mid, mid, low], 0)[:, top + PANEL : BLK]
                    for high, mid, low in pieces
                ]
                rights = [
                    jnp.concatenate([high, mid, low, high, mid, high], 0)
                    for high, mid, low in pieces
                ]
                update = [dot_of(left, right, 0, 0) for left, right in zip(lefts, rights)]
            for g in range(group):
                product_ref[pl.ds(bases[g] + top, PANEL), :] = solved[g][:, -BLK:]
                if not last:
                    gram_ref[rest[g], :] = old[g][0] - update[g][:, :BLK]
                    product_ref[rest[g], :] = old[g][1] - update[g][:, BLK:]
            return nothing

        lax.fori_loop(0, count // group, step, 0)


def six_rows(pieces, lane):
    high, mid, low = pieces
    none = jnp.zeros_like(high)
    return jnp.concatenate(
        [
            jnp.where(lane < 3 * PANEL, high, none),
            jnp.where(lane < 2 * PANEL, mid, none),
            jnp.where(lane < PANEL, low, none),
        ],
        0,
    )[:, : 3 * PANEL]


def optimise_kernel(slots_ref, rates_ref, *refs, count, adds):
    grads, states = refs[:adds], refs[adds : adds + 7]
    outs = refs[-17:-10]
    in_ref, out_ref, gram_ref, product_ref, inverse_ref, grad_ref, in_sems, out_sem, grad_sem = refs[
        -9:
    ]
    for index, grad in enumerate(grads):
        pltpu.make_async_copy(grad.at[0:count], grad_ref.at[index], grad_sem).start()
    for item in range(count):
        for index, state in enumerate(states):
            pltpu.make_async_copy(
                state.at[slots_ref[item]], in_ref.at[item, index], in_sems.at[item]
            ).start()

    group = math.gcd(count, 4)
    pltpu.make_async_copy(grad_ref, grad_ref, grad_sem).wait()

    def update(step, nothing):
        items = [step * group + index for index in range(group)]
        gradients = []
        for item in items:
            pltpu.make_async_copy(in_ref.at[item], in_ref.at[item], in_sems.at[item]).wait()
            grad = sum(grad_ref[index, item].astype(single) for index in range(adds))
            gradients.append(grad.astype(bfloat))
        results = adam_group(
            items, gradients, [[in_ref[item, index] for index in range(7)] for item in items],
            [rates_ref[item] for item in items], gram_ref, product_ref, count,
        )
        for item, values in zip(items, results):
            for index, value in enumerate(values):
                out_ref[item, index] = value
        for item in items:
            for index in range(5):
                pltpu.make_async_copy(
                    out_ref.at[item, index], outs[index].at[slots_ref[item]], out_sem
                ).start()
        return nothing

    lax.fori_loop(0, count // group, update, 0)
    renew(gram_ref, product_ref, inverse_ref, 2 * count)

    def finish(item, nothing):
        for side in range(2):
            base = pl.multiple_of((side * count + item) * BLK, BLK)
            out_ref[item, 5 + side] = product_ref[pl.ds(base, BLK), :].T
            pltpu.make_async_copy(
                out_ref.at[item, 5 + side], outs[5 + side].at[slots_ref[item]], out_sem
            ).start()
        return nothing

    lax.fori_loop(0, count, finish, 0, unroll=math.gcd(count, 4))
    pltpu.make_async_copy(out_ref, out_ref, out_sem).wait()


def optimise(slots, rates, grads, states, earlier=None, after=()):
    count, total = slots.shape[0], states[0].shape[0]
    more = [] if earlier is None else list(earlier)
    skip = 2 + len(grads) + 7
    return pl.pallas_call(
        functools.partial(optimise_kernel, count=count, adds=len(grads)),
        grid_spec=pltpu.PrefetchScalarGridSpec(
            num_scalar_prefetch=2,
            grid=(),
            in_specs=[in_hbm()] * (len(grads) + 7 + len(more))
            + [anywhere()] * len(after),
            out_specs=[in_hbm()] * 7 + [anywhere()],
            scratch_shapes=[
                pltpu.VMEM((count, 7, BLK, BLK), single),
                pltpu.VMEM((count, 7, BLK, BLK), single),
                pltpu.VMEM((2 * count * BLK, BLK), single),
                pltpu.VMEM((2 * count * BLK, BLK), single),
                pltpu.VMEM((2 * count * PANEL, BLK), single),
                pltpu.VMEM((len(grads), count, BLK, BLK), bfloat),
                pltpu.SemaphoreType.DMA((count,)),
                pltpu.SemaphoreType.DMA,
                pltpu.SemaphoreType.DMA,
            ],
        ),
        out_shape=[of((total, BLK, BLK), single)] * 7 + [token_of()],
        input_output_aliases={skip + index: index for index in range(7)} if more else {},
        cost_estimate=cost(count * 40 * BLK**3, *grads, *states),
        compiler_params=pltpu.CompilerParams(vmem_limit_bytes=56 * 2**20),
        name="optimise",
    )(slots, rates, *grads, *states, *more, *after)


def whole_spec():
    return pl.BlockSpec(memory_space=pltpu.VMEM)


def fixed(shape):
    return pl.BlockSpec(shape, lambda *_: (0,) * len(shape))


def anywhere():
    return pl.BlockSpec(memory_space=pl.ANY)


def token_of():
    return of((8, 128), single)


def in_hbm():
    return pl.BlockSpec(memory_space=pltpu.HBM)


def cost(flops, *arrays):
    moved = sum(math.prod(a.shape) * jnp.dtype(a.dtype).itemsize for a in arrays)
    return pl.CostEstimate(flops=flops // 16, bytes_accessed=moved // 16, transcendentals=0)


def of(shape, dtype):
    return jax.ShapeDtypeStruct(shape, dtype)


def flip_rows(value):
    return value.astype(single).T.astype(bfloat)


def attend_kernel(q_ref, k_ref, v_ref, valid_ref, w_ref, *refs, heads, own):
    attended_ref, lse_ref, branch_ref, _, flipped_ref, score_ref, prob_ref = refs[-7:]
    keys, width = k_ref.shape
    rows = q_ref.shape[0]
    tile = 128

    flipped_ref[...] = flip_rows(v_ref[...])
    queries = flip_rows(q_ref[...]) * (HEAD_DIM ** (-0.5))
    queries = queries.astype(bfloat)
    head_of = lax.broadcasted_iota(jnp.int32, (width, rows), 0) // HEAD_DIM
    mixed = []
    for head in range(heads):
        score_ref[...] = dot_of(
            k_ref[...], jnp.where(head_of == head, queries, jnp.zeros_like(queries)), 1, 0
        )

        def masked(index):
            here = pl.ds(pl.multiple_of(index * tile, tile), tile)
            valid = valid_ref[here, :]
            valid = jnp.concatenate([valid] * (rows // 128), 1)
            return here, jnp.where(valid > 0.0, score_ref[here, :], masked_score)

        def highest_of(index, best):
            _, value = masked(index)
            return jnp.maximum(best, jnp.max(value.reshape(tile // 8, 8, rows), 0))

        best = lax.fori_loop(
            0, keys // tile, highest_of, jnp.full((8, rows), -jnp.inf, single), unroll=True
        )
        best = jnp.max(best, 0, keepdims=True)

        def weigh(index, total):
            here, value = masked(index)
            value = jnp.exp(value - best)
            prob_ref[here, :] = value.astype(bfloat)
            return total + jnp.sum(value.reshape(tile // 8, 8, rows), 0)

        total = lax.fori_loop(
            0, keys // tile, weigh, jnp.zeros((8, rows), single), unroll=True
        )
        total = jnp.sum(total, 0, keepdims=True)
        out = dot_of(
            flipped_ref[head * HEAD_DIM : (head + 1) * HEAD_DIM, :], prob_ref[...], 1, 0
        )
        mixed.append(out * (1.0 / total))
        lse_ref[head : head + 1, :] = best + jnp.log(total)
    attended = jnp.concatenate(mixed, 0).T.astype(bfloat)
    attended_ref[...] = attended
    branch = dot_of(attended, w_ref[...], 1, 0)
    if own:
        branch = branch + refs[0][...].astype(single)
    branch_ref[...] = branch.astype(bfloat)


def attend(projected, valid, w_out, block, received=None, after=()):
    seq, width = projected.shape[0], w_out.shape[0]
    rows = seq // 4
    heads = width // HEAD_DIM
    own = received is not None
    more = [received] if own else []
    out_shape = [
        of((rows, width), bfloat), of((heads, rows), single), of((rows, D), bfloat), token_of()
    ]
    return pl.pallas_call(
        functools.partial(attend_kernel, heads=heads, own=own),
        grid=(1,),
        in_specs=[
            pl.BlockSpec((rows, width), lambda i: (block, 0)),
            pl.BlockSpec((seq, width), lambda i: (0, 1)),
            pl.BlockSpec((seq, width), lambda i: (0, 2)),
            fixed(valid.shape),
            fixed(w_out.shape),
        ] + [fixed(value.shape) for value in more] + [anywhere()] * len(after),
        out_specs=[fixed(value.shape) for value in out_shape[:-1]] + [anywhere()],
        out_shape=out_shape,
        scratch_shapes=[
            pltpu.VMEM((width, seq), bfloat), pltpu.VMEM((seq, rows), single),
            pltpu.VMEM((seq, rows), bfloat),
        ],
        cost_estimate=cost(2 * 2 * rows * seq * width * heads, projected, *out_shape),
        compiler_params=pltpu.CompilerParams(vmem_limit_bytes=24 * 2**20),
        name="attend",
    )(projected, projected, projected, valid, w_out, *more, *after)


def attend_back_kernel(*refs, heads, first, extra):
    inputs = 11 if first else 13
    refs = refs[:inputs] + refs[inputs + extra :]
    if first:
        (own_ref, peer_ref, w_ref, q_ref, k_ref, v_ref, att_own, att_peer, lse_own, lse_peer,
         valid_ref, dq_ref, dk_ref, dv_ref, _, flipped_ref, grad_ref, score_ref, cross_ref, prob_ref, back_ref,
         att_ref, log_ref, dk_sum, dv_sum) = refs
    else:
        (own_ref, peer_ref, w_ref, q_ref, k_ref, v_ref, att_own, att_peer, lse_own, lse_peer,
         valid_ref, dk_in_ref, dv_in_ref, dq_ref, dk_ref, dv_ref, _, flipped_ref, grad_ref, score_ref,
         cross_ref, prob_ref, back_ref, att_ref, log_ref, dk_sum, dv_sum) = refs
    step = pl.program_id(0)
    keys, width = k_ref.shape
    rows = q_ref.shape[0]
    scale = HEAD_DIM ** (-0.5)
    tile = 128

    @pl.when(step == 0)
    def _():
        flipped_ref[...] = flip_rows(k_ref[...])
        grad_ref[...] = own_ref[...]
        att_ref[...] = att_own[...]
        log_ref[...] = lse_own[...]
        if first:
            dk_sum[...] = jnp.zeros_like(dk_sum)
            dv_sum[...] = jnp.zeros_like(dv_sum)
        else:
            dk_sum[...] = dk_in_ref[...]
            dv_sum[...] = dv_in_ref[...]

    @pl.when(step == 1)
    def _():
        grad_ref[...] = peer_ref[...]
        att_ref[...] = att_peer[...]
        log_ref[...] = lse_peer[...]

    grads = dot_of(grad_ref[...], w_ref[...], 1, 1).astype(bfloat)
    flat = grads.astype(single).T
    cross = flat * att_ref[...].astype(single).T
    grads_t = flat.astype(bfloat)
    queries = q_ref[...]
    queries_t = (flip_rows(queries) * scale).astype(bfloat)
    head_of = lax.broadcasted_iota(jnp.int32, (width, rows), 0) // HEAD_DIM
    none = jnp.zeros_like(grads_t)
    dq = []
    for head in range(heads):
        score_ref[...] = dot_of(k_ref[...], jnp.where(head_of == head, queries_t, none), 1, 0)
        cross_ref[...] = dot_of(v_ref[...], jnp.where(head_of == head, grads_t, none), 1, 0)
        lse = log_ref[head : head + 1, :]
        mean = jnp.sum(cross[head * HEAD_DIM : (head + 1) * HEAD_DIM], 0, keepdims=True)
        at = slice(head * rows, (head + 1) * rows)

        def weigh(index, nothing):
            here = pl.ds(pl.multiple_of(index * tile, tile), tile)
            valid = jnp.concatenate([valid_ref[here, :]] * (rows // 128), 1)
            value = jnp.where(valid > 0.0, score_ref[here, :], masked_score)
            prob = jnp.exp(value - lse)
            prob_ref[here, at] = prob.astype(bfloat)
            back_ref[here, at] = (prob * (cross_ref[here, :] - mean)).astype(bfloat)
            return nothing

        lax.fori_loop(0, keys // tile, weigh, 0, unroll=True)
        dq.append(
            dot_of(flipped_ref[head * HEAD_DIM : (head + 1) * HEAD_DIM, :], back_ref[:, at], 1, 0)
        )
    dq_ref[...] = (jnp.concatenate(dq, 0).T * scale).astype(bfloat)
    lane_head = lax.broadcasted_iota(jnp.int32, (rows, width), 1) // HEAD_DIM
    query_rows = jnp.concatenate(
        [jnp.where(lane_head == head, queries, jnp.zeros_like(queries)) for head in range(heads)], 0
    )
    grad_rows = jnp.concatenate(
        [jnp.where(lane_head == head, grads, jnp.zeros_like(grads)) for head in range(heads)], 0
    )

    def total(index, nothing):
        here = pl.ds(pl.multiple_of(index * 256, 256), 256)
        dk_sum[here, :] = dk_sum[here, :] + dot_of(back_ref[here, :], query_rows, 1, 0) * scale
        dv_sum[here, :] = dv_sum[here, :] + dot_of(prob_ref[here, :], grad_rows, 1, 0)
        return nothing

    lax.fori_loop(0, keys // 256, total, 0, unroll=True)

    @pl.when(step == 1)
    def _():
        dk_ref[...] = dk_sum[...].astype(dk_ref.dtype)
        dv_ref[...] = dv_sum[...].astype(dv_ref.dtype)


def attend_back(own, peer, w_out, projected, attended, lse, valid, part, earlier=None, after=()):
    seq, width = projected.shape[0], w_out.shape[0]
    rows = seq // 4
    heads = width // HEAD_DIM
    first = earlier is None
    kind = single if first else bfloat
    more = [] if first else list(earlier)
    out_shape = [
        of((2 * rows, width), bfloat), of((seq, width), kind), of((seq, width), kind), token_of()
    ]
    return pl.pallas_call(
        functools.partial(attend_back_kernel, heads=heads, first=first, extra=len(after)),
        grid=(2,),
        in_specs=[
            fixed(own.shape), fixed(peer.shape), fixed(w_out.shape),
            pl.BlockSpec((rows, width), lambda i: (2 * part + i, 0)),
            pl.BlockSpec((seq, width), lambda i: (0, 1)),
            pl.BlockSpec((seq, width), lambda i: (0, 2)),
            fixed((rows, width)), fixed((rows, width)), fixed((heads, rows)), fixed((heads, rows)),
            fixed(valid.shape),
        ] + [fixed((seq, width))] * len(more) + [anywhere()] * len(after),
        out_specs=[
            pl.BlockSpec((rows, width), lambda i: (i, 0)),
            fixed((seq, width)), fixed((seq, width)), anywhere(),
        ],
        out_shape=out_shape,
        scratch_shapes=[
            pltpu.VMEM((width, seq), bfloat), pltpu.VMEM((rows, D), bfloat),
            pltpu.VMEM((seq, rows), single), pltpu.VMEM((seq, rows), single),
            pltpu.VMEM((seq, heads * rows), bfloat), pltpu.VMEM((seq, heads * rows), bfloat),
            pltpu.VMEM((rows, width), bfloat), pltpu.VMEM((heads, rows), single),
            pltpu.VMEM((seq, width), single), pltpu.VMEM((seq, width), single),
        ],
        cost_estimate=cost(2 * 2 * rows * seq * width * 5 * heads, projected, *out_shape),
        compiler_params=pltpu.CompilerParams(vmem_limit_bytes=28 * 2**20),
        name="attend_back",
    )(own, peer, w_out, projected, projected, projected, *attended, *lse, valid, *more, *after)


def gelu_pair(value):
    size = jnp.abs(value)
    ratio = 1.0 / (1.0 + (0.3275911 * 0.5**0.5) * size)
    bell = jnp.exp(-0.5 * value * value)
    series = 0.5 * 1.061405429 * ratio + 0.5 * -1.453152027
    series = series * ratio + 0.5 * 1.421413741
    series = series * ratio + 0.5 * -0.284496736
    series = series * ratio + 0.5 * 0.254829592
    tail = series * ratio * bell
    below = jnp.where(value >= 0.0, 1.0 - tail, tail)
    return value * below, below + value * bell * (1.0 / math.sqrt(2.0 * math.pi))


def feed_kernel(rows_ref, up_ref, bias_ref, down_ref, *refs):
    act_ref, slope_ref, out_ref, _, pre_ref, sum_ref = refs[-6:]
    step = pl.program_id(0)
    rows = rows_ref.shape[0]
    tile = 32
    pre_ref[...] = dot_of(rows_ref[...], up_ref[...], 1, 0)

    def activate(index, nothing):
        here = pl.ds(pl.multiple_of(index * tile, tile), tile)
        value, slope = gelu_pair(pre_ref[here, :] + bias_ref[...])
        act_ref[here, :] = value.astype(bfloat)
        slope_ref[here, :] = slope.astype(bfloat)
        return nothing

    lax.fori_loop(0, rows // tile, activate, 0, unroll=4)
    add_up(step, dot_of(act_ref[...], down_ref[...], 1, 0), sum_ref, out_ref)


def add_up(step, more, sum_ref, out_ref):
    last = pl.num_programs(0) - 1

    @pl.when(step == 0)
    def _():
        sum_ref[...] = more

    @pl.when((step > 0) & (step < last))
    def _():
        sum_ref[...] = sum_ref[...] + more

    @pl.when(step == last)
    def _():
        out_ref[...] = (sum_ref[...] + more).astype(out_ref.dtype)


def feed(block, w_up, bias, w_down, kind, after=()):
    rows, hidden = block.shape[0], w_up.shape[1]
    step = 512
    out_shape = [
        of((rows, hidden), bfloat), of((rows, hidden), bfloat), of((rows, D), kind), token_of()
    ]
    return pl.pallas_call(
        feed_kernel,
        grid=(hidden // step,),
        in_specs=[
            fixed(block.shape),
            pl.BlockSpec((D, step), lambda j: (0, j)),
            pl.BlockSpec((1, step), lambda j: (0, j)),
            pl.BlockSpec((step, D), lambda j: (j, 0)),
        ] + [anywhere()] * len(after),
        out_specs=[
            pl.BlockSpec((rows, step), lambda j: (0, j)),
            pl.BlockSpec((rows, step), lambda j: (0, j)),
            fixed((rows, D)), anywhere(),
        ],
        out_shape=out_shape,
        scratch_shapes=[pltpu.VMEM((rows, step), single), pltpu.VMEM((rows, D), single)],
        cost_estimate=cost(4 * rows * D * hidden, w_up, w_down, *out_shape),
        compiler_params=pltpu.CompilerParams(vmem_limit_bytes=20 * 2**20),
        name="feed",
    )(block, w_up, bias, w_down, *after)


def feed_back_kernel(rows_ref, down_ref, up_ref, slope_ref, *refs):
    grad_ref, bias_ref, out_ref, _, sum_ref = refs[-5:]
    grads = dot_of(rows_ref[...], down_ref[...], 1, 1) * slope_ref[...].astype(single)
    grads = grads.astype(bfloat)
    grad_ref[...] = grads
    bias_ref[...] = jnp.sum(grads.astype(single), 0, keepdims=True)
    add_up(pl.program_id(0), dot_of(grads, up_ref[...], 1, 1), sum_ref, out_ref)


def feed_back(block, w_down, w_up, slope, kind, after=()):
    rows, hidden = block.shape[0], w_up.shape[1]
    step = 512
    out_shape = [
        of((rows, hidden), bfloat), of((1, hidden), single), of((rows, D), kind), token_of()
    ]
    return pl.pallas_call(
        feed_back_kernel,
        grid=(hidden // step,),
        in_specs=[
            fixed(block.shape),
            pl.BlockSpec((step, D), lambda j: (j, 0)),
            pl.BlockSpec((D, step), lambda j: (0, j)),
            pl.BlockSpec((rows, step), lambda j: (0, j)),
        ] + [anywhere()] * len(after),
        out_specs=[
            pl.BlockSpec((rows, step), lambda j: (0, j)),
            pl.BlockSpec((1, step), lambda j: (0, j)),
            fixed((rows, D)), anywhere(),
        ],
        out_shape=out_shape,
        scratch_shapes=[pltpu.VMEM((rows, D), single)],
        cost_estimate=cost(4 * rows * D * hidden, w_up, w_down, *out_shape),
        compiler_params=pltpu.CompilerParams(vmem_limit_bytes=20 * 2**20),
        name="feed_back",
    )(block, w_down, w_up, slope, *after)


def chip_kernel(keep_ref, got_ref, *refs):
    refs[-2][...] = (keep_ref[...] + got_ref[...].astype(single)).astype(bfloat)


def standardise(value):
    centred = value - jnp.mean(value, -1, keepdims=True)
    inv_std = lax.rsqrt(jnp.mean(centred * centred, -1, keepdims=True) + norm_eps)
    return centred * inv_std, inv_std


def through_norm(grads, normed, inv_std, gain):
    scaled = grads * gain
    mean_grad = jnp.mean(scaled, -1, keepdims=True)
    mean_cross = jnp.mean(scaled * normed, -1, keepdims=True)
    return inv_std * (scaled - mean_grad - normed * mean_cross)


def gain_sums(grads, normed, rounded):
    total = lambda value: jnp.sum(value, 0, keepdims=True)
    blank = jnp.zeros((5, grads.shape[1]), single)
    return jnp.concatenate(
        [total(grads * normed), total(grads), total(rounded.astype(single)), blank], 0
    )


norm_tile = 128


def norm_one_kernel(chip_ref, across_ref, rows_ref, vectors_ref, *refs):
    normed_ref, inv_ref, hidden_ref = refs[-4:-1]
    branch = chip_ref[...].astype(single) + across_ref[...].astype(single)
    normed, inv_std = standardise(rows_ref[...].astype(single) + (branch + vectors_ref[2:3, :]))
    normed_ref[...] = normed
    inv_ref[...] = jnp.broadcast_to(inv_std, inv_ref.shape)
    hidden_ref[...] = (normed * vectors_ref[0:1, :] + vectors_ref[1:2, :]).astype(bfloat)


def norm_two_kernel(
    chip_ref, across_ref, normed_ref, cot_ref, valid_ref, one_ref, two_ref, *refs
):
    out_ref, grad_ref, low_ref, sums_ref = refs[-5:-1]

    @pl.when(pl.program_id(0) == 0)
    def _():
        sums_ref[...] = jnp.zeros_like(sums_ref)

    hidden = normed_ref[...] * one_ref[0:1, :] + one_ref[1:2, :]
    down = chip_ref[...].astype(single) + across_ref[...].astype(single)
    normed, inv_std = standardise(hidden + (down + two_ref[2:3, :]))
    gain = two_ref[0:1, :]
    out_ref[...] = (normed * gain + two_ref[1:2, :]).astype(bfloat)
    grads = cot_ref[...].astype(single) * valid_ref[:, 0:1]
    back = through_norm(grads, normed, inv_std, gain)
    grad_ref[...] = back
    low = back.astype(bfloat)
    low_ref[...] = low
    sums_ref[...] += gain_sums(grads, normed, low)


def norm_back_kernel(
    chip_ref, across_ref, second_ref, normed_ref, inv_ref, one_ref, *refs
):
    grad_ref, low_ref, sums_ref = refs[-4:-1]

    @pl.when(pl.program_id(0) == 0)
    def _():
        sums_ref[...] = jnp.zeros_like(sums_ref)

    grads = chip_ref[...].astype(single) + across_ref[...].astype(single) + second_ref[...]
    normed = normed_ref[...]
    back = through_norm(grads, normed, inv_ref[:, 0:1], one_ref[0:1, :])
    grad_ref[...] = back
    low = back.astype(bfloat)
    low_ref[...] = low
    sums_ref[...] += gain_sums(grads, normed, low)


def norm_call(kernel, name, rowed, fixed_in, row_outs, sums, after=()):
    rows = rowed[0].shape[0]
    by_row = lambda width: pl.BlockSpec((norm_tile, width), lambda i: (i, 0))
    out_shape = [of((rows, width), kind) for width, kind in row_outs]
    out_specs = [by_row(width) for width, _ in row_outs]
    if sums:
        out_shape.append(of((8, D), single))
        out_specs.append(fixed((8, D)))
    out_shape.append(token_of())
    out_specs.append(anywhere())
    return pl.pallas_call(
        kernel,
        grid=(rows // norm_tile,),
        in_specs=[by_row(value.shape[1]) for value in rowed]
        + [fixed(value.shape) for value in fixed_in]
        + [anywhere()] * len(after),
        out_specs=out_specs,
        out_shape=out_shape,
        cost_estimate=cost(20 * rows * D, *rowed, *out_shape),
        compiler_params=pltpu.CompilerParams(vmem_limit_bytes=16 * 2**20),
        name=name,
    )(*rowed, *fixed_in, *after)


def token_back_kernel(*refs):
    dq_refs, (dk_ref, dv_ref, w_ref), outs = refs[:2], refs[2:5], refs[-5:-1]
    width = dk_ref.shape[1]
    rows = dk_ref.shape[0] // 4
    for block in range(4):
        here = slice(block * rows, (block + 1) * rows)
        parts = [
            dq_refs[block // 2][block % 2 * rows : (block % 2 + 1) * rows, :],
            dk_ref[here, :], dv_ref[here, :],
        ]
        value = dot_of(jnp.concatenate(parts, 1), w_ref[...], 1, 1)
        outs[block][...] = value.astype(outs[block].dtype)


def token_back(dq_a, dq_b, dk, dv, w_qkv, after=()):
    rows = dk.shape[0] // 4
    out_shape = [of((rows, D), kind) for kind in (single, bfloat, single, bfloat)] + [token_of()]
    return pl.pallas_call(
        token_back_kernel,
        in_specs=[whole_spec()] * 5 + [anywhere()] * len(after),
        out_specs=[whole_spec()] * 4 + [anywhere()],
        out_shape=out_shape,
        cost_estimate=cost(8 * rows * D * w_qkv.shape[1], w_qkv, dk, *out_shape),
        compiler_params=pltpu.CompilerParams(vmem_limit_bytes=12 * 2**20),
        name="token_back",
    )(dq_a, dq_b, dk, dv, w_qkv, *after)


def pack_kernel(target_ref, *refs, jobs, scale, regions, count, resumed):
    outs = refs[-4 - len(regions) : -4]
    held_ref, sem, in_sem = refs[-3:]
    if resumed:
        start = pltpu.make_async_copy(refs[count], held_ref, in_sem)
        start.start()
    waited = not resumed
    for lefts, rights, layout, rows, cols in jobs:
        right = jnp.concatenate([refs[index][...] for index in rights], 0)
        for row in range(0, rows, 2):
            span = min(2, rows - row)
            left = jnp.concatenate(
                [refs[index][:, row * BLK : (row + span) * BLK] for index in lefts], 0
            )
            weights = (dot_of(left, right, 0, 0) * scale).astype(bfloat)
            if not waited:
                start.wait()
                waited = True
            for i in range(span):
                for col in range(cols):
                    held_ref[target_ref[layout(row + i, col)]] = weights[
                        i * BLK : (i + 1) * BLK, col * BLK : (col + 1) * BLK
                    ]
    copies = [
        pltpu.make_async_copy(held_ref.at[first : first + size], out, sem.at[index])
        for index, ((first, size), out) in enumerate(zip(regions, outs))
    ]
    for copy in copies:
        copy.start()
    for copy in copies:
        copy.wait()


def pack(target, pairs, scale, regions, earlier=None, after=()):
    operands, jobs, blocks, flops = [], [], 0, 0
    total = target.shape[0]

    def places(arrays):
        found = []
        for value in arrays:
            if not any(value is other for other in operands):
                operands.append(value)
            found.append([value is other for other in operands].index(True))
        return found

    for lefts, rights, layout in pairs:
        rows, cols = lefts[0].shape[1] // BLK, rights[0].shape[1] // BLK
        jobs.append((places(lefts), places(rights), layout, rows, cols))
        blocks += rows * cols
        flops += 2 * rows * cols * BLK * BLK * sum(value.shape[0] for value in lefts)
    more = [] if earlier is None else [earlier]
    return pl.pallas_call(
        functools.partial(
            pack_kernel, jobs=jobs, scale=scale, regions=regions, count=len(operands),
            resumed=bool(more),
        ),
        grid_spec=pltpu.PrefetchScalarGridSpec(
            num_scalar_prefetch=1,
            grid=(),
            in_specs=[whole_spec()] * len(operands)
            + [in_hbm()] * len(more)
            + [anywhere()] * len(after),
            out_specs=[anywhere()] * (len(regions) + 1),
            scratch_shapes=[
                pltpu.VMEM((total, BLK, BLK), bfloat),
                pltpu.SemaphoreType.DMA((len(regions),)),
                pltpu.SemaphoreType.DMA,
            ],
        ),
        out_shape=[of((size, BLK, BLK), bfloat) for _, size in regions] + [token_of()],
        cost_estimate=cost(flops, *operands, of((blocks, BLK, BLK), bfloat)),
        compiler_params=pltpu.CompilerParams(vmem_limit_bytes=28 * 2**20),
        name="pack",
    )(target, *operands, *more, *after)


def join_kernel(*refs, groups):
    out_ref = refs[-2]
    at = 0
    for index, terms in enumerate(groups):
        total = 0.0
        for ref in refs[at : at + terms]:
            value = ref[...].reshape(-1, BLK, BLK)
            total = total + value.astype(single)
        at += terms
        size = total.shape[0]
        out_ref[index * size : (index + 1) * size] = total.astype(bfloat)


def join(hop, groups, after=()):
    operands, specs = [], []
    for keep, got, *carried in groups:
        slots = keep.shape[0] // (lax.axis_size("dp") // 2)
        block = pl.BlockSpec((slots, BLK, BLK), lambda i: (hop, 0, 0))
        operands += [keep, got, *carried]
        specs += [block] + [fixed((slots, BLK, BLK))] * (1 + len(carried))
    out = of((slots * len(groups), BLK, BLK), bfloat)
    return pl.pallas_call(
        functools.partial(join_kernel, groups=[len(group) for group in groups]),
        grid=(1,),
        in_specs=specs + [anywhere()] * len(after),
        out_specs=[fixed(out.shape), anywhere()],
        out_shape=[out, token_of()],
        cost_estimate=cost(1, out),
        compiler_params=pltpu.CompilerParams(vmem_limit_bytes=10 * 2**20),
        name="join",
    )(*operands, *after)


def block_counts(tensors):
    return (D * D // (tensors * BLK * BLK), D * FF // (tensors * BLK * BLK))


def rate_values(canon_index, tensors, seq_len):
    attn_count, ffn_count = block_counts(tensors)
    out_std = math.sqrt(seq_len / (3.0 * D))
    inner = jnp.where(canon_index < 4 * attn_count + ffn_count, D ** (-0.5), FF ** (-0.5))
    inner = jnp.where(canon_index < 4 * attn_count, out_std, inner)
    return jnp.where(canon_index < 3 * attn_count, D ** (-0.5), inner).astype(single)


def swap(value, axis, bit):
    count = lax.axis_size(axis)
    return lax.ppermute(value, axis, [(i, i ^ bit) for i in range(count)])


def ring(value):
    count = lax.axis_size("dp")
    return lax.ppermute(value, "dp", [(i, (i + 2) % count) for i in range(count)])


def gather_slots(local, parts):
    size = local.shape[0] // parts
    hops = lax.axis_size("dp") // 2
    pieces = [[[None] * parts for _ in range(2)] for _ in range(hops)]
    for part in range(parts):
        shard = local[part * size : (part + 1) * size] if parts > 1 else local
        for hop in range(hops):
            pieces[hop][0][part] = shard
            pieces[hop][1][part] = swap(shard, "dp", 1)
            if hop < hops - 1:
                shard = ring(shard)
    return [piece for pair in pieces for flip in pair for piece in flip]


def vector_kernel(rank_ref, one_ref, two_ref, up_a, up_b, up_c, up_d, dq_a, dq_b, dv_ref, *refs):
    out_ref = refs[-2]
    rank = rank_ref[0]
    out_ref[...] = jnp.zeros_like(out_ref)
    out_ref[0:2, :] = one_ref[0:2, :]
    out_ref[2:4, :] = two_ref[0:2, :]
    out_ref[6:7, :] = one_ref[2:3, :]
    out_ref[11:12, :] = two_ref[2:3, :]
    width = dv_ref.shape[1]
    query = jnp.sum(dq_a[...].astype(single), 0, keepdims=True) + jnp.sum(
        dq_b[...].astype(single), 0, keepdims=True
    )
    value = jnp.sum(dv_ref[...].astype(single), 0, keepdims=True)
    place = lax.broadcasted_iota(jnp.int32, (1, D), 1) // width == rank
    for row, total in ((4, query), (5, value)):
        wide = jnp.concatenate([total] * (D // width), 1)
        out_ref[row : row + 1, :] = jnp.where(place, wide, 0.0)
    bias = up_a[...] + up_b[...] + up_c[...] + up_d[...]
    size = bias.shape[1]
    for row in range(FF // D):
        for part in range(D // size if size < D else 1):
            here = (row * D + part * size) // size == rank
            out_ref[7 + row : 8 + row, part * size : (part + 1) * size] = jnp.where(here, bias, 0.0)


def vector_rows(rank, sums_one, sums_two, bias_parts, dq_a, dq_b, grad_value, after):
    operands = [sums_one, sums_two, *bias_parts, dq_a, dq_b, grad_value]
    return pl.pallas_call(
        vector_kernel,
        grid_spec=pltpu.PrefetchScalarGridSpec(
            num_scalar_prefetch=1,
            grid=(),
            in_specs=[whole_spec()] * len(operands) + [anywhere()] * len(after),
            out_specs=[whole_spec(), anywhere()],
        ),
        out_shape=[of((16, D), single), token_of()],
        cost_estimate=cost(1, *operands),
        compiler_params=pltpu.CompilerParams(vmem_limit_bytes=5 * 2**20),
        name="vector_rows",
    )(rank, *operands, *after)


def hop_sum(value, axis, bit):
    return value + swap(value, axis, bit)


def assemble_kernel(source_ref, *refs, sizes, layouts):
    count = len(sizes)
    pieces, outs, (held, sems) = refs[:count], refs[-2 - len(set(job[0] for job in layouts)) : -2], refs[-2:]
    copies, start = [], 0
    for index, size in enumerate(sizes):
        copies.append(pltpu.make_async_copy(pieces[index], held.at[start : start + size], sems.at[index]))
        start += size
    for copy in copies:
        copy.start()
    for copy in copies:
        copy.wait()
    canon = 0
    for target, rows, cols, row_at, col_at in layouts:
        for row in range(rows):
            for col in range(cols):
                outs[target][
                    (row_at + row) * BLK : (row_at + row + 1) * BLK,
                    (col_at + col) * BLK : (col_at + col + 1) * BLK,
                ] = held[source_ref[canon]]
                canon += 1


def assemble(source, pieces, shapes, layouts, after=()):
    sizes = [piece.shape[0] for piece in pieces]
    return pl.pallas_call(
        functools.partial(assemble_kernel, sizes=sizes, layouts=layouts),
        grid_spec=pltpu.PrefetchScalarGridSpec(
            num_scalar_prefetch=1,
            grid=(1,),
            in_specs=[in_hbm()] * len(pieces) + [anywhere()] * len(after),
            out_specs=[pl.BlockSpec(shape, lambda i, *_: (0, 0)) for shape in shapes],
            scratch_shapes=[
                pltpu.VMEM((sum(sizes), BLK, BLK), bfloat),
                pltpu.SemaphoreType.DMA((len(sizes),)),
            ],
        ),
        out_shape=[jax.ShapeDtypeStruct(shape, bfloat) for shape in shapes],
        compiler_params=pltpu.CompilerParams(vmem_limit_bytes=40 * 2**20),
        name="assemble",
    )(source, *pieces, *after)


def chip_sum(keep, send, after=()):
    return norm_call(
        chip_kernel, "chip_sum", [keep, peer_of(send)], [], [(D, bfloat)], False, after
    )


def across(value):
    return swap(value, "tensor", 2)


def peer_of(value):
    return swap(value, "tensor", 1)


def body(
    tokens,
    cotangent,
    seq_lengths,
    block_owner,
    master_blocks,
    first_moment,
    second_moment,
    left_stats,
    right_stats,
    left_basis,
    right_basis,
    vector_master,
    vector_first,
    vector_second,
):
    tensors = lax.axis_size("tensor")
    data_ranks = lax.axis_size("dp")
    tensor_rank = lax.axis_index("tensor")
    data_rank = lax.axis_index("dp")
    local_rows = tokens.shape[0]
    seq_len = local_rows * tensors
    slice_width = D // tensors
    hidden_width = FF // tensors
    block_total = block_owner.shape[0]
    slots_here = master_blocks.shape[1]
    length = seq_lengths[0]
    attn_count, ffn_count = block_counts(tensors)
    permuted = data_ranks <= 16
    hops = data_ranks // 2
    canon_ids = jnp.arange(block_total, dtype=jnp.int32)
    holder, slot = block_owner // slots_here, block_owner % slots_here
    source = target = block_owner
    if permuted:
        flip = (holder % 2) ^ (data_rank % 2)
        down = (data_rank // 2 - holder // 2) % hops
        up = (holder // 2 - data_rank // 2) % hops
        source = (down * 2 + flip) * slots_here + slot
        target = (flip * hops + up) * slots_here + slot
    mine = block_owner[None, :] == data_rank * slots_here + jnp.arange(slots_here)[:, None]
    own_canon = jnp.sum(jnp.where(mine, canon_ids[None, :], 0), 1)
    own_slots = jnp.arange(slots_here, dtype=jnp.int32)

    cols = slice_width // BLK
    wide = hidden_width // BLK
    full = D // BLK
    local_weights = master_blocks[0].astype(bfloat)
    if permuted:
        pieces = gather_slots(local_weights, 3)
    else:
        pieces = [lax.all_gather(local_weights, "dp", axis=0, tiled=True)]
    w_qkv, w_out, w_up, w_down = assemble(
        source,
        pieces,
        [(D, 3 * slice_width), (slice_width, D), (D, hidden_width), (hidden_width, D)],
        [
            (0, full, cols, 0, 0),
            (0, full, cols, 0, cols),
            (0, full, cols, 0, 2 * cols),
            (1, cols, full, 0, 0),
            (2, full, wide, 0, 0),
            (3, wide, full, 0, 0),
        ],
    )
    gain_one, shift_one = (vector_master[0:D], vector_master[D : 2 * D])
    gain_two, shift_two = (vector_master[2 * D : 3 * D], vector_master[3 * D : 4 * D])
    bias_query = lax.dynamic_slice_in_dim(
        vector_master, 4 * D + tensor_rank * slice_width, slice_width
    )
    bias_value = lax.dynamic_slice_in_dim(
        vector_master, 5 * D + tensor_rank * slice_width, slice_width
    )
    bias_out = vector_master[6 * D : 7 * D]
    bias_up = lax.dynamic_slice_in_dim(
        vector_master, 7 * D + tensor_rank * hidden_width, hidden_width
    )
    bias_down = vector_master[7 * D + FF : 8 * D + FF]

    tokens_b = swap(tokens, "tensor", 2)
    cotangent_b = swap(cotangent, "tensor", 2)
    full_tokens = jnp.concatenate(
        [tokens, peer_of(tokens), tokens_b, peer_of(tokens_b)], axis=0
    )
    quarters = tensor_rank ^ jnp.arange(4, dtype=jnp.int32)
    positions = (quarters[:, None] * local_rows + jnp.arange(local_rows)[None, :]).reshape(-1)
    key_valid = positions < length
    row_valid = key_valid.astype(single)[:, None]
    chunk = 2 * local_rows

    bias_qkv = jnp.concatenate([bias_query, jnp.zeros((slice_width,), single), bias_value])
    projected = (jnp.dot(full_tokens, w_qkv, preferred_element_type=single) + bias_qkv).astype(
        bfloat
    )
    one = jnp.stack([gain_one, shift_one, bias_out])
    two = jnp.stack([gain_two, shift_two, bias_down])
    valid = jnp.broadcast_to(row_valid, (seq_len, 128))
    grad_scale = 1.0 / math.sqrt(seq_len * data_ranks)
    up_start = 4 * attn_count

    attended, lse, shares = [None] * 4, [None] * 4, [None] * 4
    attended[3], lse[3], shares[3], token = attend(
        projected, valid, w_out, 3, after=[cotangent_b]
    )
    attended[1], lse[1], shares[1], token = attend(projected, valid, w_out, 1, after=[token])
    for block in (2, 0):
        attended[block], lse[block], shares[block], token = attend(
            projected, valid, w_out, block, peer_of(shares[block + 1]),
            after=[token],
        )
    chip = [shares[0], shares[2]]
    other = [across(chip[1]), across(chip[0])]

    normed_one, inv_one = [None] * 2, [None] * 2
    hidden, activation, slope, chip_two = [None] * 4, [None] * 4, [None] * 4, [None] * 2
    bias_row = bias_up[None, :]

    def norm_up(part, after):
        normed_one[part], inv_one[part], hidden[2 * part], token = norm_call(
            norm_one_kernel, "norm_one", [chip[part], other[part], (tokens, tokens_b)[part]],
            [one], [(D, single), (128, single), (D, bfloat)], False, after,
        )
        hidden[2 * part + 1] = peer_of(hidden[2 * part])
        return token

    def feed_part(part, token, arrived=()):
        block = 2 * part
        activation[block], slope[block], keep, token = feed(
            hidden[block], w_up, bias_row, w_down, single, [token]
        )
        block += 1
        activation[block], slope[block], send, token = feed(
            hidden[block], w_up, bias_row, w_down, bfloat, [token, *arrived]
        )
        return keep, send, token

    token = norm_up(0, [token])
    *sums, token = feed_part(0, token)
    token = norm_up(1, [token])
    chip_two[0], token = chip_sum(*sums, [token])
    other = [None, across(chip_two[0])]
    *sums, token = feed_part(1, token, [other[1]])
    chip_two[1], token = chip_sum(*sums, [token])
    other[0] = across(chip_two[1])

    grad_second, grad_down, grad_up = [None] * 2, [None] * 4, [None] * 4
    bias_parts, chip_three, outs, sums_two = [None] * 4, [None] * 2, [None] * 2, [None] * 2

    def norm_down(part, token):
        rows_valid = valid[part * chunk : part * chunk + local_rows]
        outs[part], grad_second[part], grad_down[2 * part], sums_two[part], token = norm_call(
            norm_two_kernel, "norm_two",
            [chip_two[part], other[part], normed_one[part], (cotangent, cotangent_b)[part],
             rows_valid],
            [one, two], [(D, bfloat), (D, single), (D, bfloat)], True, [token],
        )
        grad_down[2 * part + 1] = peer_of(grad_down[2 * part])
        return token

    def feed_back_part(part, token):
        block = 2 * part
        grad_up[block], bias_parts[block], keep, token = feed_back(
            grad_down[block], w_down, w_up, slope[block], single, [token]
        )
        block += 1
        grad_up[block], bias_parts[block], send, token = feed_back(
            grad_down[block], w_down, w_up, slope[block], bfloat, [token]
        )
        return keep, send, token

    token = norm_down(1, token)
    *sums, token = feed_back_part(1, token)
    token = norm_down(0, token)
    chip_three[1], token = chip_sum(*sums, [token])
    other = [across(chip_three[1]), None]
    *sums, token = feed_back_part(0, token)
    chip_three[0], token = chip_sum(*sums, [token])
    other[1] = across(chip_three[0])
    layer_output = outs[0]
    *sent, token = pack(
        target,
        [
            (hidden, grad_up, lambda row, col: up_start + row * wide + col),
            (activation, grad_down, lambda row, col: up_start + ffn_count + row * full + col),
        ],
        grad_scale,
        [(0, block_total)],
        after=[token],
    )

    grad_branch, grad_query, back, grad_rows, sums_one = [None] * 4, [None] * 2, None, [0, 0], [0, 0]
    for part in (0, 1):
        block = 2 * part
        grad_rows[part], grad_branch[block], sums_one[part], token = norm_call(
            norm_back_kernel, "norm_back",
            [chip_three[part], other[part], grad_second[part], normed_one[part], inv_one[part]],
            [one], [(D, single), (D, bfloat)], True, [token],
        )
        grad_branch[block + 1] = peer_of(grad_branch[block])
        grad_query[part], *back, token = attend_back(
            grad_branch[block], grad_branch[block + 1], w_out, projected,
            attended[block : block + 2], lse[block : block + 2], valid, part, back, [token],
        )
    grad_summed, sums_one = grad_rows[0], sums_one[0]
    grad_key, grad_value = back
    moved = hops * slots_here
    regions = [(0, block_total)]
    if permuted:
        regions = [(0, moved)] + [
            (moved + hop * slots_here, slots_here) for hop in range(hops)
        ]
    kept, *leaving, token = pack(
        target,
        [
            ([full_tokens], grad_query, lambda row, col: row * cols + col),
            ([full_tokens], [grad_key], lambda row, col: attn_count + row * cols + col),
            ([full_tokens], [grad_value], lambda row, col: 2 * attn_count + row * cols + col),
            (attended, grad_branch, lambda row, col: 3 * attn_count + row * full + col),
        ],
        grad_scale,
        regions,
        sent[0],
        [token],
    )
    vector_grad, token = vector_rows(
        tensor_rank.astype(jnp.int32)[None], sums_one, sums_two[0], bias_parts, *grad_query,
        grad_value, [token],
    )
    vector_grad = hop_sum(vector_grad, "tensor", 1)
    vector_grad = hop_sum(vector_grad, "tensor", 2)
    def finish_tokens(token):
        keep_a, send_a, keep_b, send_b, token = token_back(
            grad_query[0], grad_query[1], grad_key, grad_value, w_qkv, [token]
        )
        chip_b = chip_sum(keep_b, send_b, [token])[0]
        chip_a = chip_sum(keep_a, send_a, [token])[0]
        over = across(chip_b)
        token_grad = (chip_a.astype(single) + over.astype(single) + grad_summed).astype(bfloat)
        return token_grad, token

    bits = []
    bit = 1
    while bit < data_ranks:
        bits.append(bit)
        bit *= 2
    bits = bits[1:] + bits[:1]
    if permuted:
        carried, after = [], [token]
        for bit in bits[:-1]:
            vector_grad = hop_sum(vector_grad, "dp", bit)
            after.append(vector_grad)
        bits = bits[-1:]
        for hop in range(hops - 1, 0, -1):
            got = swap(leaving[hop], "dp", 1)
            total, token = join(hop, [[kept, got] + carried], after)
            if hop == hops - 1:
                token_grad, token = finish_tokens(token)
            carried, after = [ring(total)], [token]
        own_grad = [kept, swap(leaving[0], "dp", 1)] + carried
    else:
        token_grad, token = finish_tokens(token)
        own_grad = [lax.psum_scatter(kept, "dp", scatter_dimension=0, tiled=True)]
    for bit in bits:
        vector_grad = hop_sum(vector_grad, "dp", bit)
    vector_sum = vector_grad[: 8 + FF // D].reshape(-1) * grad_scale
    rates = rate_values(own_canon, tensors, seq_len)
    correction = 1.0 - moment_decay**STEP
    states = [
        first_moment[0], second_moment[0], master_blocks[0], left_stats[0], right_stats[0],
        left_basis[0], right_basis[0],
    ]
    *fresh, _ = optimise(own_slots, rates, own_grad, states)
    fresh_first, fresh_second, fresh_master, fresh_left, fresh_right, basis_left, basis_right = fresh
    vec_first = moment_decay * vector_first + (1.0 - moment_decay) * vector_sum
    vec_second = moment_decay * vector_second + (1.0 - moment_decay) * vector_sum * vector_sum
    vec_master = vector_master - vector_rate * (vec_first / correction) / (
        jnp.sqrt(vec_second / correction) + adam_eps
    )
    return (
        layer_output,
        token_grad,
        fresh_first[None],
        fresh_second[None],
        fresh_master[None],
        fresh_left[None],
        fresh_right[None],
        basis_left[None],
        basis_right[None],
        vec_first,
        vec_second,
        vec_master,
    )


def solution(mesh):
    return jax.shard_map(
        body,
        mesh=mesh,
        in_specs=(
            P(("dp", "tensor"), None),
            P(("dp", "tensor"), None),
            P("dp"),
            P(),
            P("tensor", "dp", None, None),
            P("tensor", "dp", None, None),
            P("tensor", "dp", None, None),
            P("tensor", "dp", None, None),
            P("tensor", "dp", None, None),
            P("tensor", "dp", None, None),
            P("tensor", "dp", None, None),
            P(),
            P(),
            P(),
        ),
        out_specs=(
            P(("dp", "tensor"), None),
            P(("dp", "tensor"), None),
            P("tensor", "dp", None, None),
            P("tensor", "dp", None, None),
            P("tensor", "dp", None, None),
            P("tensor", "dp", None, None),
            P("tensor", "dp", None, None),
            P("tensor", "dp", None, None),
            P("tensor", "dp", None, None),
            P(),
            P(),
            P(),
        ),
        check_vma=False,
    )
```
